32 devices in a mesh: elem: 16 (over z, y, x), band: 2 (over core).
Axes of the slice: x: 2, y: 2, z: 4, core: 2. Of those that a mesh axis runs over, the one named last changes fastest.
Arguments:
- orbitals: bfloat16 [2048, 2, 1536], P('elem', None, 'band'), may hold values from -6 to 6
- elem_count: int32 [16], P('elem'), may hold values from 1 to 4, as said below
- connectivity: int32 [16, 4, 343], P('elem'), may hold values from 0 to 383
- elem_coef: float32 [16, 4], P('elem'), may hold values from 0.5 to 2
- elem_matrix: bfloat16 [343, 343], replicated, may hold values from -1 to 1, as said below
- potential: float32 [2048], P('elem'), may hold values from -1 to 1
- absorber: float32 [2048], P('elem'), may hold values from 0.05 to 1
- rotation: bfloat16 [1536, 2, 512], replicated, may hold values from -0.109375 to 0.109375
Outputs:
- filtered: bfloat16 [2048, 2, 1536], P('elem', None, 'band')
- rotated: bfloat16 [2048, 2, 512], P('elem', None, 'band')
- intersection: float32 [1536, 2, 512], P('band')
The draws below stay inside these ranges and needn't reach their ends.
Inputs may be any that keep to these rules, and one draw needn't show every extreme that they name: Each block has between 1 and 4 live elements; the first elem_count[b] slots are live. `connectivity`: indices 0 to 127 name the previous block's last owned nodes, 128 to 255 the block's own nodes, the rest the next block's first nodes. `elem_matrix`: symmetric.
All inputs are finite; a program needn't handle non-finite values.
Results may differ from the reference program's by a relative error of at most 0.0055.
Values may be sent and summed in bfloat16 or wider, within the bound.
No kernel may reach another device: no remote copies, remote signals or barrier semaphores. Data moves between devices by JAX's collectives and lax.ppermute only.
A program may use at most 64 MiB of HBM per device.

```python
import math
import jax
import jax.numpy as jnp
from jax import lax

ELEM_NODES = 343
BANDS = 1536
PANEL = 512
NODE_DEV = 128
FACE = 128
E_CAP = 4
BLOCKS = 16
NODES = 2048


def draw_elem_count(key, part):
    first_key = jax.random.fold_in(key, 11)
    second_key = jax.random.fold_in(key, 12)
    third_key = jax.random.fold_in(key, 13)
    draw_one = jax.random.randint(first_key, (BLOCKS,), 1, E_CAP + 1)
    draw_two = jax.random.randint(second_key, (BLOCKS,), 1, E_CAP + 1)
    counts = jnp.minimum(draw_one, draw_two)
    busiest = jax.random.randint(third_key, (), 0, BLOCKS)
    return jnp.where(jnp.arange(BLOCKS) == busiest, E_CAP, counts).astype(jnp.int32)


def draw_elem_matrix(key, part):
    normals = jnp.clip(jax.random.normal(jax.random.fold_in(key, 21), (ELEM_NODES, ELEM_NODES), jnp.float32), -4.0, 4.0)
    matrix = (normals + normals.T) / jnp.sqrt(2.0 * ELEM_NODES)
    return matrix.astype(jnp.bfloat16)


def touch_ends(result, rng, least, top_value):
    longest = result.shape.index(max(result.shape))
    spots = []
    for shift in (0, 1):
        where = [jax.random.randint(jax.random.fold_in(rng, axis), (), 0, length) for axis, length in enumerate(result.shape)]
        where[longest] = (where[longest] + shift) % result.shape[longest]
        spots.append(tuple(where))
    return result.at[spots[0]].set(least).at[spots[1]].set(top_value)


def levels(stream_key, extent, cuts, smallest, high):
    def one(dim, parts):
        heights = jax.random.uniform(jax.random.fold_in(jax.random.fold_in(stream_key, 6), dim), (parts,), jnp.float32, smallest / len(cuts), high / len(cuts))
        return jnp.repeat(jnp.exp(heights), extent[dim] // parts).reshape((-1,) + (1,) * (len(extent) - dim - 1))

    loudness = one(*cuts[0])
    for cut in cuts[1:]:
        loudness = loudness * one(*cut)
    return loudness


def centred(rng, extent, width, most, pieces=(), kind=jnp.bfloat16):
    drawn = jax.random.normal(rng, extent, jnp.float32) * width
    if len(pieces) > 0:
        drawn = levels(rng, extent, pieces, -0.22, 0.18) * drawn
    return jnp.clip(drawn, min=-most, max=most).astype(kind)


def setup_inputs(seed: int = 0) -> dict:
    seeds = jax.random.split(jax.random.key(seed), 9)
    orbitals = centred(seeds[0], (NODES, 2, BANDS), 1.0, 6.0, ((0, 16), (2, 2)))
    elem_count = draw_elem_count(jax.random.fold_in(seeds[8], 71), 0)
    connectivity = touch_ends(jax.random.randint(seeds[2], (BLOCKS, E_CAP, ELEM_NODES), 0, NODE_DEV + 2 * FACE), jax.random.fold_in(seeds[2], 1), 0, (NODE_DEV + 2 * FACE) - 1).astype(jnp.int32)
    elem_coef = jnp.clip(jnp.exp(math.log(2.0) - 1.3862944 * jax.random.uniform(seeds[3], (BLOCKS, E_CAP), jnp.float32) ** levels(seeds[3], (BLOCKS, E_CAP), ((0, 16),), -0.2, 0.2)), 0.5, 2.0)
    elem_matrix = draw_elem_matrix(jax.random.fold_in(seeds[8], 71), 0)
    potential = jnp.clip(jax.random.uniform(seeds[5], (NODES,), jnp.float32, -1.0, 1.0) * levels(seeds[5], (NODES,), ((0, 16),), -0.4, 0.0), -1.0, 1.0)
    absorber = jnp.clip(jnp.exp(math.log(1.0) - 2.9957323 * jax.random.uniform(seeds[6], (NODES,), jnp.float32) ** levels(seeds[6], (NODES,), ((0, 16),), -0.2, 0.2)), 0.05, 1.0)
    rotation = centred(seeds[7], (BANDS, 2, PANEL), (2 * BANDS) ** -0.5, 0.109375)
    return dict(orbitals=orbitals, elem_count=elem_count, connectivity=connectivity, elem_coef=elem_coef, elem_matrix=elem_matrix, potential=potential, absorber=absorber, rotation=rotation)


FILTER_CENTER = 1.0
FILTER_HALF = 4.0

def assemble(field, elem_count, connectivity, elem_coef, elem_matrix):
    width_all = field.shape[1] * field.shape[2]
    flat_field = field.reshape(NODES, width_all)
    padded = jnp.pad(flat_field, ((FACE, FACE), (0, 0)))

    def one_block(inputs):
        block_id, live_count, node_lists, coefs = inputs
        extended = lax.dynamic_slice_in_dim(padded, (block_id * NODE_DEV).astype(jnp.int32), NODE_DEV + 2 * FACE, 0)
        totals = jnp.zeros((NODE_DEV + 2 * FACE, width_all), jnp.float32)
        for element in range(E_CAP):
            node_ids = node_lists[element]
            factor = coefs[element] * (element < live_count).astype(jnp.float32)
            product = jnp.dot(elem_matrix, extended[node_ids], preferred_element_type=jnp.float32)
            totals = totals.at[node_ids].add(product * factor)
        return totals
    blocks = lax.map(one_block, (jnp.arange(BLOCKS, dtype=jnp.int32), elem_count, connectivity, elem_coef))
    owned = blocks[:, FACE:FACE + NODE_DEV]
    owned = owned.at[1:, :FACE].add(blocks[:-1, FACE + NODE_DEV:])
    owned = owned.at[:-1, NODE_DEV - FACE:].add(blocks[1:, :FACE])
    return owned.reshape(field.shape)

def hamiltonian(field, elem_count, connectivity, elem_coef, elem_matrix, potential, absorber):
    summed = assemble(field, elem_count, connectivity, elem_coef, elem_matrix)
    vector = field.astype(jnp.float32)
    pot_col = potential[:, None]
    cap_col = absorber[:, None]
    ham_re = summed[:, 0] + pot_col * vector[:, 0] + cap_col * vector[:, 1]
    ham_im = summed[:, 1] + pot_col * vector[:, 1] - cap_col * vector[:, 0]
    return (ham_re, ham_im, vector)

def reference(orbitals, elem_count, connectivity, elem_coef, elem_matrix, potential, absorber, rotation):
    ham_re, ham_im, vector = hamiltonian(orbitals, elem_count, connectivity, elem_coef, elem_matrix, potential, absorber)
    first = jnp.stack([(ham_re - FILTER_CENTER * vector[:, 0]) / FILTER_HALF, (ham_im - FILTER_CENTER * vector[:, 1]) / FILTER_HALF], axis=1).astype(jnp.bfloat16)
    ham_re, ham_im, inner = hamiltonian(first, elem_count, connectivity, elem_coef, elem_matrix, potential, absorber)
    anchor = orbitals.astype(jnp.float32)
    filtered = jnp.stack([2.0 * (ham_re - FILTER_CENTER * inner[:, 0]) / FILTER_HALF - anchor[:, 0], 2.0 * (ham_im - FILTER_CENTER * inner[:, 1]) / FILTER_HALF - anchor[:, 1]], axis=1).astype(jnp.bfloat16)
    flat_bands = filtered.reshape(NODES, 2 * BANDS)
    rot_re = rotation[:, 0]
    rot_im = rotation[:, 1]
    block_matrix = jnp.concatenate([jnp.concatenate([rot_re, rot_im], axis=1), jnp.concatenate([-rot_im, rot_re], axis=1)], axis=0)
    rotated = jnp.dot(flat_bands, block_matrix, preferred_element_type=jnp.float32).astype(jnp.bfloat16).reshape(NODES, 2, PANEL)
    flat_panel = rotated.reshape(NODES, 2 * PANEL)
    products = lax.dot_general(flat_bands, flat_panel, (((0,), (0,)), ((), ())), preferred_element_type=jnp.float32)
    products = products.reshape(2, BANDS, 2, PANEL)
    over_re = products[0, :, 0] - products[1, :, 1]
    over_im = products[0, :, 1] + products[1, :, 0]
    intersection = jnp.stack([over_re, over_im], axis=1) * (1.0 / math.sqrt(NODES))
    return (filtered, rotated, intersection)
```

```python
import functools

import jax
import jax.numpy as jnp
from jax import lax
from jax.experimental import pallas as pl
from jax.experimental.pallas import tpu as pltpu
from jax.sharding import PartitionSpec as P

FILTER_CENTER = 1.0
FILTER_HALF = 4.0
GROUP = 4
BF16 = jnp.bfloat16
F32 = jnp.float32
SMALL_ROWS = 16
VMEM_LIMIT = 48 * 1024 * 1024


def up(value, step):
    return -(-value // step) * step


def kernel_call(body, out_shape, n_scalars, scratch=(), flops=0, moved=0):
    many = isinstance(out_shape, (list, tuple))
    vmem = pl.BlockSpec(memory_space=pltpu.VMEM)

    def call(scalars, *arrays):
        return pl.pallas_call(
            body,
            out_shape=out_shape,
            in_specs=[pl.BlockSpec(memory_space=pltpu.SMEM)] + [vmem] * len(arrays),
            out_specs=[vmem] * len(out_shape) if many else vmem,
            scratch_shapes=list(scratch),
            compiler_params=pltpu.CompilerParams(vmem_limit_bytes=VMEM_LIMIT),
            cost_estimate=pl.CostEstimate(flops=flops, bytes_accessed=moved, transcendentals=0),
        )(scalars, *arrays)

    return call


def pieces(value):
    top = value.astype(BF16).astype(F32)
    rest = value - top
    middle = rest.astype(BF16).astype(F32)
    return (top, middle, rest - middle)


def small_body(e_cap, elem_nodes, nodes, width, scal, conn, coef, pot, cap, out):
    out[...] = jnp.zeros(out.shape, BF16)
    ids = conn[...]
    high = ids >> 7
    out[0:e_cap, 0:elem_nodes] = (ids - (high << 7)).astype(F32).astype(BF16)
    pad = jnp.full((e_cap, width), 64.0, F32)
    out[4 : 4 + e_cap, :] = pad.astype(BF16)
    out[4 : 4 + e_cap, 0:elem_nodes] = high.astype(F32).astype(BF16)
    lane = lax.broadcasted_iota(jnp.int32, (1, e_cap), 1)
    live = jnp.where(lane < scal[3], coef[...], 0.0)
    for at, part in enumerate(pieces(live)):
        out[8 + at : 9 + at, 0:e_cap] = part.astype(BF16)
    for row, vector in ((11, pot), (12, cap)):
        for at, part in enumerate(pieces(vector[...])):
            out[row : row + 1, at * nodes : (at + 1) * nodes] = part.astype(BF16)


def pack_body(nodes, w, wp, scal, vec, small, small_low, small_high, *outs):
    mine = scal[0]
    for chunk in range(GROUP):
        re = vec[0, :, chunk * w : (chunk + 1) * w]
        im = vec[1, :, chunk * w : (chunk + 1) * w]
        if wp > w:
            fill = jnp.zeros((nodes, wp - w), BF16)
            both = jnp.concatenate([re, fill, im, fill], axis=1)
        else:
            both = jnp.concatenate([re, im], axis=1)
        for k in range(GROUP):

            @pl.when((mine ^ k) == chunk)
            def _():
                outs[k][0:nodes, :] = both

    for k in range(GROUP):
        for at, part in enumerate((small_low, small, small_high)):
            outs[k][nodes + at * SMALL_ROWS : nodes + (at + 1) * SMALL_ROWS, 0 : small.shape[1]] = part[...]


def build_body(nodes, e_cap, rows_out, scal, m0, m1, m2, m3, matrix, k_hi, k_lo, ids, coefs, coefs_s, acc, sem):
    mine = scal[0]
    width = matrix.shape[0]
    blocks = 3 * GROUP
    messages = (m0, m1, m2, m3)
    for k in range(GROUP):
        for dz in range(3):
            at = nodes + dz * SMALL_ROWS
            rows = messages[k][at : at + SMALL_ROWS, 0:width].astype(F32)
            t = dz * GROUP + (mine ^ k)
            ids[t, 0:4, :] = rows[0:4] + 128.0 * rows[4:8]
            coefs[pl.ds(t, 1), :] = (rows[8:9] + rows[9:10] + rows[10:11])[:, 0:128]
    copy = pltpu.make_async_copy(coefs, coefs_s, sem)
    copy.start()
    acc[...] = jnp.zeros(acc.shape, F32)
    copy.wait()
    span = 3 * nodes

    def one(step, carry):
        t = 1 + step // e_cap
        e = step % e_cap
        factor = coefs_s[t, e]

        @pl.when(factor != 0.0)
        def _():
            row = ids[t, pl.ds(e, 1), :]
            place = lax.broadcasted_iota(jnp.int32, (span, width), 0).astype(F32)
            hot = jnp.where(place == row, 1.0, 0.0).astype(BF16)
            half = jnp.dot(hot, matrix[...], preferred_element_type=F32)
            half_hi = half.astype(BF16)
            half_lo = (half - half_hi.astype(F32)).astype(BF16)
            dims = (((1,), (1,)), ((), ()))
            full = lax.dot_general(half_hi, hot, dims, preferred_element_type=F32)
            full = full + lax.dot_general(half_lo, hot, dims, preferred_element_type=F32)
            full = full * factor
            for j in range(3):
                i = t + j - 3

                @pl.when((i >= 0) & (i < rows_out))
                def _():
                    acc[i, :, (2 - j) * nodes : (5 - j) * nodes] += full[j * nodes : (j + 1) * nodes, :]

        return carry

    lax.fori_loop(0, (blocks - 2) * e_cap, one, 0)
    for i in range(rows_out):
        value = acc[i]
        top = value.astype(BF16)
        k_hi[i] = top
        k_lo[i] = (value - top.astype(F32)).astype(BF16)


def filter_body(
    nodes, wp, scal, m0, m1, m2, m3, low, high, k_hi, k_lo, f0, f1, f2, f3, vec, first, cols
):
    mine = scal[0]
    messages = (m0, m1, m2, m3)
    outs = (f0, f1, f2, f3)
    rows_out = 2 * GROUP
    for k in range(GROUP):
        other = mine ^ k
        vec[pl.ds(pl.multiple_of(other * nodes, nodes), nodes), :] = low[k]
        vec[pl.ds(pl.multiple_of((GROUP + other) * nodes, nodes), nodes), :] = messages[k][0:nodes, :]
        vec[pl.ds(pl.multiple_of((2 * GROUP + other) * nodes, nodes), nodes), :] = high[k]
    diag = lax.broadcasted_iota(jnp.int32, (nodes, nodes), 0) == lax.broadcasted_iota(
        jnp.int32, (nodes, nodes), 1
    )
    for k in range(GROUP):
        for dz in range(3):
            at = nodes + dz * SMALL_ROWS
            rows = messages[k][at : at + SMALL_ROWS, :].astype(F32)
            t = dz * GROUP + (mine ^ k)
            for slot, row in ((0, 11), (1, 12)):
                line = rows[row : row + 1, 0:nodes] + rows[row : row + 1, nodes : 2 * nodes]
                line = line + rows[row : row + 1, 2 * nodes : 3 * nodes]
                column = jnp.sum(jnp.where(diag, line, 0.0), axis=1, keepdims=True)
                cols[slot, t] = jnp.broadcast_to(column, (nodes, 128))
    sign = jnp.where(lax.broadcasted_iota(jnp.int32, (1, 2 * wp), 1) < wp, 1.0, -1.0)

    def applied(source, start, i):
        block = source[start * nodes : (start + 5) * nodes, :]
        total = jnp.dot(k_hi[i], block, preferred_element_type=F32)
        total = total + jnp.dot(k_lo[i], block, preferred_element_type=F32)
        own = source[(start + 2) * nodes : (start + 3) * nodes, :].astype(F32)
        turned = pltpu.roll(own, wp, 1)
        pot = cols[0, i + 2][:, 0:1]
        cap = cols[1, i + 2][:, 0:1]
        return (total + pot * own + (cap * sign) * turned, own)

    inside_low = scal[1] > 0
    inside_high = scal[1] < scal[2] - 1
    for i in range(rows_out):
        ham, own = applied(vec, i, i)
        value = (ham - FILTER_CENTER * own) / FILTER_HALF
        if i < 2:
            value = jnp.where(inside_low, value, 0.0)
        if i >= rows_out - 2:
            value = jnp.where(inside_high, value, 0.0)
        first[i * nodes : (i + 1) * nodes, :] = value.astype(BF16)
    for i in range(GROUP):
        ham, own = applied(first, i, i + 2)
        anchor = vec[(GROUP + i) * nodes : (GROUP + i + 1) * nodes, :].astype(F32)
        value = 2.0 * (ham - FILTER_CENTER * own) / FILTER_HALF - anchor
        value = value.astype(BF16)
        for k in range(GROUP):

            @pl.when((mine ^ k) == i)
            def _():
                outs[k][...] = value


def rotate_body(nodes, w, wp, parts, scal, g0, g1, g2, g3, rot, filtered, *out):
    mine = scal[0]
    received = (g0, g1, g2, g3)
    panel = rot.shape[3]
    with_re = jnp.zeros((2 * nodes, panel), F32)
    with_im = jnp.zeros((2 * nodes, panel), F32)
    for k in range(GROUP):
        chunk = mine ^ k
        re = received[k][:, 0:wp]
        im = received[k][:, wp : 2 * wp]
        both = jnp.concatenate([re, im], axis=0)
        with_re = with_re + jnp.dot(both, rot[0, chunk], preferred_element_type=F32)
        with_im = with_im + jnp.dot(both, rot[1, chunk], preferred_element_type=F32)
        for q in range(GROUP):

            @pl.when(chunk == q)
            def _():
                filtered[0, :, q * w : (q + 1) * w] = re[:, 0:w]
                filtered[1, :, q * w : (q + 1) * w] = im[:, 0:w]

    out_re = with_re[0:nodes] - with_im[nodes:]
    out_im = with_im[0:nodes] + with_re[nodes:]
    cols = panel // parts
    for h in range(parts):
        value_re = out_re[:, h * cols : (h + 1) * cols]
        value_im = out_im[:, h * cols : (h + 1) * cols]
        if parts == 2:

            @pl.when(scal[4] == h)
            def _():
                out[0][:, 0:cols] = value_re
                out[0][:, cols : 2 * cols] = value_im

            @pl.when(scal[4] != h)
            def _():
                out[1][:, 0:cols] = value_re
                out[1][:, cols : 2 * cols] = value_im

        else:
            out[0][h, :, 0:cols] = value_re
            out[0][h, :, cols : 2 * cols] = value_im


def overlap_body(nodes, w, wp, parts, cols, scale, split, scal, *refs):
    fields = refs[0:GROUP]
    panels = refs[GROUP : GROUP + GROUP * parts]
    outs = refs[GROUP + GROUP * parts : -3]
    left, right, result = refs[-3:]
    panel = parts * cols
    for k in range(GROUP):
        left[:, k * nodes : (k + 1) * nodes] = jnp.transpose(fields[k][...].astype(F32)).astype(BF16)
        for h in range(parts):
            if parts == 2:

                @pl.when(scal[4] == h)
                def _():
                    right[k * nodes : (k + 1) * nodes, h * 2 * cols : (h + 1) * 2 * cols] = panels[k][...]

                @pl.when(scal[4] != h)
                def _():
                    right[k * nodes : (k + 1) * nodes, h * 2 * cols : (h + 1) * 2 * cols] = panels[
                        GROUP + k
                    ][...]

            else:
                right[k * nodes : (k + 1) * nodes, h * 2 * cols : (h + 1) * 2 * cols] = panels[
                    h * GROUP + k
                ][...]
    product = jnp.dot(left[...], right[...], preferred_element_type=F32)
    top, bottom = product[0:w], product[wp : wp + w]
    for h in range(parts):
        a, b, c = 2 * h * cols, (2 * h + 1) * cols, (2 * h + 2) * cols
        result[:, h * cols : (h + 1) * cols] = (top[:, a:b] - bottom[:, b:c]) * scale
        result[:, panel + h * cols : panel + (h + 1) * cols] = (top[:, b:c] + bottom[:, a:b]) * scale
    if split == 1:
        outs[0][...] = result[...]
    else:
        rows = w // split
        for j in range(split):
            at = pl.multiple_of((scal[1] ^ j) * rows, rows)
            outs[j][...] = result[pl.ds(at, rows), :].astype(BF16)


def sum_body(scal, s0, s1, s2, s3, out):
    total = s0[...].astype(F32) + s1[...].astype(F32)
    total = total + (s2[...].astype(F32) + s3[...].astype(F32))
    out[...] = total.astype(BF16)


def spread_body(w, rows, split, panel, scal, a0, a1, a2, a3, out):
    mine, group = scal[0], scal[1]
    for k, part in enumerate((a0, a1, a2, a3)):
        for j in range(split):
            at = (mine ^ k) * w + ((group ^ j) if split > 1 else 0) * rows
            value = part[j].astype(F32)
            out[pl.ds(at, rows), 0, :] = value[:, 0:panel]
            out[pl.ds(at, rows), 1, :] = value[:, panel : 2 * panel]


def on_device(
    orbitals, elem_count, connectivity, elem_coef, elem_matrix, potential, absorber, rotation
):
    nodes, _, bands = orbitals.shape
    blocks = lax.axis_size("elem")
    parts = lax.axis_size("band")
    e_cap, elem_nodes = connectivity.shape[1:]
    panel = rotation.shape[2]
    groups = blocks // GROUP
    w = bands // GROUP
    wp = up(w, 64)
    lanes = 2 * wp
    span = 3 * nodes
    width = up(max(elem_nodes, span), 128)
    cols = panel // parts
    elem = lax.axis_index("elem")
    band = lax.axis_index("band")
    mine = elem % GROUP
    group = elem // GROUP
    scal = jnp.stack(
        [mine, group, jnp.int32(groups), elem_count[0], band, jnp.int32(0), jnp.int32(0), jnp.int32(0)]
    ).astype(jnp.int32)

    def in_group(k):
        return [(i, i ^ k) for i in range(blocks)]

    def swap(values):
        return [values[0]] + [lax.ppermute(values[k], "elem", in_group(k)) for k in range(1, GROUP)]

    up_perm = [(i, i + GROUP) for i in range(blocks - GROUP)]
    down_perm = [(b, a) for a, b in up_perm]

    def both_ways(value):
        return lax.ppermute(value, "elem", up_perm), lax.ppermute(value, "elem", down_perm)

    small = kernel_call(
        functools.partial(small_body, e_cap, elem_nodes, nodes, width),
        jax.ShapeDtypeStruct((SMALL_ROWS, width), BF16),
        1,
    )(scal, connectivity[0], elem_coef, potential[None], absorber[None])
    small_low, small_high = both_ways(small)
    message = jax.ShapeDtypeStruct((nodes + 3 * SMALL_ROWS, max(lanes, width)), BF16)
    message = jax.ShapeDtypeStruct((nodes + 3 * SMALL_ROWS, lanes if lanes >= width else width), BF16)
    lanes = message.shape[1]
    wp = lanes // 2
    messages = kernel_call(functools.partial(pack_body, nodes, w, wp), [message] * GROUP, 1)(
        scal, jnp.moveaxis(orbitals, 1, 0), small, small_low, small_high
    )
    messages = swap(messages)
    stacked = jnp.stack([m[:nodes] for m in messages])
    low, high = both_ways(stacked)

    matrix = jnp.pad(elem_matrix, ((0, width - elem_nodes), (0, width - elem_nodes)))
    rows_out = 2 * GROUP
    operator = jax.ShapeDtypeStruct((rows_out, nodes, 5 * nodes), BF16)
    k_hi, k_lo = kernel_call(
        functools.partial(build_body, nodes, e_cap, rows_out),
        [operator, operator],
        1,
        scratch=[
            pltpu.VMEM((3 * GROUP, 8, width), F32),
            pltpu.VMEM((up(3 * GROUP, 8), 128), F32),
            pltpu.SMEM((up(3 * GROUP, 8), 128), F32),
            pltpu.VMEM((rows_out, nodes, 5 * nodes), F32),
            pltpu.SemaphoreType.DMA,
        ],
        flops=2 * 20 * 3 * width * width * span,
        moved=4 * rows_out * nodes * 5 * nodes,
    )(scal, *messages, matrix)

    piece = jax.ShapeDtypeStruct((nodes, lanes), BF16)
    fields = kernel_call(
        functools.partial(filter_body, nodes, wp),
        [piece] * GROUP,
        1,
        scratch=[
            pltpu.VMEM((3 * GROUP * nodes, lanes), BF16),
            pltpu.VMEM((rows_out * nodes, lanes), BF16),
            pltpu.VMEM((2, 3 * GROUP, nodes, 128), F32),
        ],
        flops=2 * 2 * 12 * nodes * 5 * nodes * lanes,
        moved=4 * rows_out * nodes * 5 * nodes,
    )(scal, *messages, low, high, k_hi, k_lo)

    received = swap(fields)
    rot = lax.dynamic_slice_in_dim(rotation, band * bands, bands, 0)
    rot = jnp.moveaxis(rot, 1, 0).reshape(2, GROUP, w, panel)
    rot = jnp.pad(rot, ((0, 0), (0, 0), (0, wp - w), (0, 0)))
    half = jax.ShapeDtypeStruct((nodes, 2 * cols), F32)
    partial = jax.ShapeDtypeStruct((parts, nodes, 2 * cols), F32)
    filtered, *sums = kernel_call(
        functools.partial(rotate_body, nodes, w, wp, parts),
        [jax.ShapeDtypeStruct((2, nodes, bands), BF16)] + ([half, half] if parts == 2 else [partial]),
        1,
        flops=2 * nodes * 2 * bands * 2 * panel,
        moved=2 * bands * 2 * panel,
    )(scal, *received, rot)
    filtered = jnp.moveaxis(filtered, 0, 1)
    if parts == 2:
        turn = [(0, 1), (1, 0)]
        rotated = (sums[0] + lax.ppermute(sums[1], "band", turn)).astype(BF16)
        gathered = swap([rotated] * GROUP)
        panels = gathered + [lax.ppermute(x, "band", turn) for x in gathered]
    else:
        rotated = lax.psum_scatter(sums[0], "band", scatter_dimension=0, tiled=True)[0].astype(BF16)
        gathered = lax.all_gather(jnp.stack(swap([rotated] * GROUP)), "band", axis=0)
        panels = [gathered[h, k] for h in range(parts) for k in range(GROUP)]
    scale = 1.0 / (nodes * blocks) ** 0.5
    direct = groups == 4 and w % (groups * 16) == 0
    split = groups if direct else 1
    rows = w // split
    term = jax.ShapeDtypeStruct((rows, 2 * panel), BF16 if direct else F32)
    terms = kernel_call(
        functools.partial(overlap_body, nodes, w, wp, parts, cols, scale, split),
        [term] * split,
        1,
        scratch=[
            pltpu.VMEM((lanes, GROUP * nodes), BF16),
            pltpu.VMEM((GROUP * nodes, 2 * panel), BF16),
            pltpu.VMEM((w, 2 * panel), F32),
        ],
        flops=2 * GROUP * nodes * lanes * 2 * panel,
        moved=4 * GROUP * nodes * panel,
    )(scal, *fields, *panels)
    if direct:

        def across(values):
            return [values[0]] + [
                lax.ppermute(values[j], "elem", [(i, i ^ (GROUP * j)) for i in range(blocks)])
                for j in range(1, split)
            ]

        own = kernel_call(sum_body, term, 1)(scal, *across(terms))
        stack = jnp.stack(across([own] * split))
    else:
        lines = [[GROUP * z + i for z in range(groups)] for i in range(GROUP)]
        stack = lax.psum(terms[0], "elem", axis_index_groups=lines).astype(BF16)[None]
    spread = swap([stack] * GROUP)
    intersection = kernel_call(
        functools.partial(spread_body, w, rows, split, panel),
        jax.ShapeDtypeStruct((bands, 2, panel), F32),
        1,
    )(scal, *spread)
    return (filtered, rotated.reshape(nodes, 2, cols), intersection)


def solution(mesh):
    placed = (
        P("elem", None, "band"),
        P("elem"),
        P("elem", None, None),
        P("elem", None),
        P(),
        P("elem"),
        P("elem"),
        P(),
    )
    return jax.shard_map(
        on_device,
        mesh=mesh,
        in_specs=placed,
        out_specs=(P("elem", None, "band"), P("elem", None, "band"), P("band", None, None)),
        check_vma=False,
    )
```

```python
import functools

import jax
import jax.numpy as jnp
from jax import lax
from jax.experimental import pallas as pl
from jax.experimental.pallas import tpu as pltpu
from jax.sharding import PartitionSpec as P

FILTER_CENTER = 1.0
FILTER_HALF = 4.0
GROUP = 4
BF16 = jnp.bfloat16
F32 = jnp.float32
SMALL = 16
VMEM_LIMIT = 48 * 1024 * 1024
VMEM = pl.BlockSpec(memory_space=pltpu.VMEM)
SMEM = pl.BlockSpec(memory_space=pltpu.SMEM)
ANY = pl.BlockSpec(memory_space=pl.ANY)


def up(value, step):
    return -(-value // step) * step


def call(body, out_shape, specs, arrays, scratch=(), flops=0, moved=0, out_specs=None, aliases=None):
    if out_specs is None:
        out_specs = [VMEM] * len(out_shape) if isinstance(out_shape, list) else VMEM
    return pl.pallas_call(
        body,
        out_shape=out_shape,
        in_specs=specs,
        out_specs=out_specs,
        scratch_shapes=list(scratch),
        input_output_aliases=aliases or {},
        compiler_params=pltpu.CompilerParams(vmem_limit_bytes=VMEM_LIMIT),
        cost_estimate=pl.CostEstimate(flops=flops, bytes_accessed=moved, transcendentals=0),
    )(*arrays)


def pieces(value):
    top = value.astype(BF16).astype(F32)
    rest = value - top
    middle = rest.astype(BF16).astype(F32)
    return (top, middle, rest - middle)


def paired(re, im, size):
    if size == re.shape[1]:
        return jnp.concatenate([re, im], axis=1)
    fill = jnp.zeros((re.shape[0], size - re.shape[1]), re.dtype)
    return jnp.concatenate([re, fill, im, fill], axis=1)


def pack_body(w, wp, pc, pcp, count, vec, own, other, conn_h, coef_h, pot_h, cap_h, *refs):
    out, conn, coef, pot, cap, small, sems = refs
    copies = [
        pltpu.make_async_copy(src, dst, sems.at[at])
        for at, (src, dst) in enumerate(((conn_h, conn), (coef_h, coef), (pot_h, pot), (cap_h, cap)))
    ]
    for copy in copies:
        copy.start()
    nodes = vec.shape[1]
    cols = pc * GROUP
    total = own[...] + other[...]
    for q in range(GROUP):
        out[q, 0:nodes, 0 : 2 * wp] = paired(
            vec[0, :, q * w : (q + 1) * w], vec[1, :, q * w : (q + 1) * w], wp
        )
        out[q, 0:nodes, 2 * wp :] = paired(
            total[:, q * pc : (q + 1) * pc], total[:, cols + q * pc : cols + (q + 1) * pc], pcp
        ).astype(BF16)
    for copy in copies:
        copy.wait()
    e_cap, elem_nodes = conn.shape
    ids = conn[...]
    high = ids >> 7
    small[...] = jnp.zeros(small.shape, F32)
    small[0:e_cap, 0:elem_nodes] = (ids - (high << 7)).astype(F32)
    small[4 : 4 + e_cap, :] = jnp.full((e_cap, small.shape[1]), 64.0, F32)
    small[4 : 4 + e_cap, 0:elem_nodes] = high.astype(F32)
    lane = lax.broadcasted_iota(jnp.int32, (1, e_cap), 1)
    live = jnp.where(lane < count[0], coef[...], 0.0)
    for at, part in enumerate(pieces(live)):
        small[8 + at : 9 + at, 0:e_cap] = part
    for row, vector in ((11, pot), (12, cap)):
        for at, part in enumerate(pieces(vector[...])):
            small[row : row + 1, at * nodes : (at + 1) * nodes] = part
    for q in range(GROUP):
        out[q, nodes : nodes + SMALL, :] = small[...].astype(BF16)


def rotate_body(parts, scal, vec, rot, *out):
    nodes, bands = vec.shape[1:]
    panel = rot.shape[2]
    mine = pl.ds(pl.multiple_of(scal[3] * bands, bands), bands)
    both = jnp.concatenate([vec[0], vec[1]], axis=0)
    with_re = jnp.dot(both, rot[0, mine, :], preferred_element_type=F32)
    with_im = jnp.dot(both, rot[1, mine, :], preferred_element_type=F32)
    out_re = with_re[0:nodes] - with_im[nodes:]
    out_im = with_im[0:nodes] + with_re[nodes:]
    cols = panel // parts
    for h in range(parts):
        value_re = out_re[:, h * cols : (h + 1) * cols]
        value_im = out_im[:, h * cols : (h + 1) * cols]
        if parts == 2:

            @pl.when(scal[3] == h)
            def _():
                out[0][:, 0:cols] = value_re
                out[0][:, cols : 2 * cols] = value_im

            @pl.when(scal[3] != h)
            def _():
                out[1][:, 0:cols] = value_re
                out[1][:, cols : 2 * cols] = value_im

        else:
            out[0][h, :, 0:cols] = value_re
            out[0][h, :, cols : 2 * cols] = value_im


def column_of(rows, row, nodes):
    line = rows[row : row + 1, 0:nodes] + rows[row : row + 1, nodes : 2 * nodes]
    line = line + rows[row : row + 1, 2 * nodes : 3 * nodes]
    shape = (nodes, nodes)
    diag = lax.broadcasted_iota(jnp.int32, shape, 0) == lax.broadcasted_iota(jnp.int32, shape, 1)
    return jnp.where(diag, line, 0.0), diag


def build_body(nodes, e_cap, scal, own, twin, next_, matrix, k_hi, k_lo, ids, coefs, coefs_s, acc, sem):
    rows_out = k_hi.shape[0]
    width = matrix.shape[0]
    blocks = 3 * GROUP
    odd = scal[1] & 1
    acc[...] = jnp.zeros(acc.shape, F32)
    for source, dz in ((own, 1), (twin, 2 - 2 * odd), (next_, 2 * odd)):
        for p in range(GROUP):
            rows = source[p][:, 0:width].astype(F32)
            t = dz * GROUP + p
            ids[t, 0:4, :] = rows[0:4] + 128.0 * rows[4:8]
            coefs[pl.ds(t, 1), :] = (rows[8:9] + rows[9:10] + rows[10:11])[:, 0:128]
            i = t - 2

            @pl.when((i >= 0) & (i < rows_out))
            def _():
                line, diag = column_of(rows, 11, nodes)
                acc[i, :, 2 * nodes : 3 * nodes] = line - jnp.where(diag, FILTER_CENTER, 0.0)

    copy = pltpu.make_async_copy(coefs, coefs_s, sem)
    copy.start()
    copy.wait()
    span = 3 * nodes

    def one(step, carry):
        t = 1 + step

        def add(count):
            place = lax.broadcasted_iota(jnp.int32, (span, width), 0).astype(F32)
            hots = [jnp.where(place == ids[t, e : e + 1, :], 1.0, 0.0).astype(BF16) for e in range(count)]
            half = jnp.dot(jnp.concatenate(hots, axis=0), matrix[...], preferred_element_type=F32)
            half = [half[e * span : (e + 1) * span] * coefs_s[t, e] for e in range(count)]
            tops = [value.astype(BF16) for value in half]
            lows = [(value - top.astype(F32)).astype(BF16) for value, top in zip(half, tops)]
            full = lax.dot_general(
                jnp.concatenate(tops + lows, axis=1),
                jnp.concatenate(hots + hots, axis=1),
                (((1,), (1,)), ((), ())),
                preferred_element_type=F32,
            )
            for j in range(3):
                i = t + j - 3

                @pl.when((i >= 0) & (i < rows_out))
                def _():
                    acc[i, :, (2 - j) * nodes : (5 - j) * nodes] += full[j * nodes : (j + 1) * nodes, :]

        live = jnp.int32(0)
        for e in range(e_cap):
            live = live + (coefs_s[t, e] != 0.0).astype(jnp.int32)
        steps = [n for n in (1, 2) if n < e_cap] + [e_cap]
        for at, count in enumerate(steps):
            least = steps[at - 1] if at else 0

            @pl.when((live > least) & (live <= count))
            def _():
                add(count)

        return carry

    lax.fori_loop(0, blocks - 2, one, 0)
    for i in range(rows_out):
        value = acc[i] * (1.0 / FILTER_HALF)
        top = value.astype(BF16)
        k_hi[i] = top
        k_lo[i] = (value - top.astype(F32)).astype(BF16)


def filter_body(nodes, wp, pcp, scal, own, twin, next_, k_hi, k_lo, *refs):
    outs = refs[0:GROUP]
    out_left, out_panel, vec, first, cols = refs[GROUP:]
    mine = scal[0]
    lanes = 2 * wp
    rows_out = 2 * GROUP
    odd = scal[1] & 1
    for source, dz in ((own, 1), (twin, 2 - 2 * odd), (next_, 2 * odd)):
        for p in range(GROUP):
            t = dz * GROUP + p
            vec[pl.ds(pl.multiple_of(t * nodes, nodes), nodes), :] = source[p][0:nodes]
            line, _ = column_of(source[p][nodes : nodes + SMALL].astype(F32), 12, nodes)
            column = jnp.sum(line, axis=1, keepdims=True) * (1.0 / FILTER_HALF)
            cols[t] = jnp.broadcast_to(column, (nodes, 128))

    def signs(width):
        return jnp.where(lax.broadcasted_iota(jnp.int32, (1, 2 * width), 1) < width, 1.0, -1.0)

    sign = jnp.concatenate([signs(wp), signs(pcp)], axis=1)

    def applied(source, start, i):
        block = source[start * nodes : (start + 5) * nodes, :]
        total = jnp.dot(k_hi[i], block, preferred_element_type=F32)
        total = total + jnp.dot(k_lo[i], block, preferred_element_type=F32)
        own = source[(start + 2) * nodes : (start + 3) * nodes, :].astype(F32)
        turned = jnp.concatenate(
            [pltpu.roll(own[:, 0:lanes], wp, 1), pltpu.roll(own[:, lanes:], pcp, 1)], axis=1
        )
        return total + (cols[i + 2][:, 0:1] * sign) * turned

    inside_low = scal[1] > 0
    inside_high = scal[1] < scal[2] - 1
    for i in range(rows_out):
        value = applied(vec, i, i)
        if i < 2:
            value = jnp.where(inside_low, value, 0.0)
        if i >= rows_out - 2:
            value = jnp.where(inside_high, value, 0.0)
        first[i * nodes : (i + 1) * nodes, :] = value.astype(BF16)
    for i in range(GROUP):
        anchor = vec[(GROUP + i) * nodes : (GROUP + i + 1) * nodes, :].astype(F32)
        value = (2.0 * applied(first, i, i + 2) - anchor).astype(BF16)
        out_panel[i] = value[:, lanes:]
        out_left[i] = value[:, 0:lanes]
        for k in range(1, GROUP):

            @pl.when((mine ^ k) == i)
            def _():
                outs[k][...] = value[:, 0:lanes]

        @pl.when(mine == i)
        def _():
            outs[0][...] = value[:, 0:lanes]


def collect_body(w, wp, scal, g0, g1, g2, g3, out):
    mine = scal[0]
    for k, part in enumerate((g0, g1, g2, g3)):
        re = part[:, 0:w]
        im = part[:, wp : wp + w]
        for q in range(GROUP):

            @pl.when((mine ^ k) == q)
            def _():
                out[0, :, q * w : (q + 1) * w] = re
                out[1, :, q * w : (q + 1) * w] = im


def overlap_body(w, wp, pc, pcp, parts, scale, split, scal, fields, *refs):
    panels = refs[0 : GROUP * parts]
    outs = refs[GROUP * parts : -4]
    rotated, left, right, result = refs[-4:]
    mine, band = scal[0], scal[3]
    nodes = fields.shape[1]
    tile = 2 * pcp
    chunks = parts * GROUP
    panel = pc * chunks
    for p in range(GROUP):
        left[:, p * nodes : (p + 1) * nodes] = jnp.transpose(fields[p].astype(F32)).astype(BF16)
    for g in range(parts):
        for j in range(GROUP):
            half = (band + g) % parts
            at = pl.multiple_of((half * GROUP + (mine ^ j)) * tile, tile)
            for p in range(GROUP):
                right[p * nodes : (p + 1) * nodes, pl.ds(at, tile)] = panels[g * GROUP + j][p]
    for j in range(GROUP):
        value = panels[j][mine]
        for q in range(GROUP):

            @pl.when((mine ^ j) == q)
            def _():
                rotated[0, :, q * pc : (q + 1) * pc] = value[:, 0:pc]
                rotated[1, :, q * pc : (q + 1) * pc] = value[:, pcp : pcp + pc]

    product = jnp.dot(left[...], right[...], preferred_element_type=F32) * scale
    top, bottom = product[0:w], product[wp : wp + w]
    for s in range(chunks):
        a, b = s * tile, s * tile + pcp
        result[:, s * pc : (s + 1) * pc] = top[:, a : a + pc] - bottom[:, b : b + pc]
        result[:, panel + s * pc : panel + (s + 1) * pc] = top[:, b : b + pc] + bottom[:, a : a + pc]
    if split == 1:
        outs[0][...] = result[...]
    else:
        rows = w // split
        for j in range(split):
            at = pl.multiple_of((scal[1] ^ j) * rows, rows)
            outs[j][...] = result[pl.ds(at, rows), :].astype(BF16)


def sum_body(s0, s1, s2, s3, out):
    total = s0[...].astype(F32) + s1[...].astype(F32)
    total = total + (s2[...].astype(F32) + s3[...].astype(F32))
    out[...] = total.astype(BF16)


def spread_body(w, rows, batch, panel, has_base, scal, *refs):
    parts = refs[0:GROUP]
    out, buffer, sems = refs[GROUP + has_base :]
    mine, group = scal[0], scal[1]
    copies = []
    for k in range(GROUP):
        for at, j in enumerate(batch):
            slot = k * len(batch) + at
            value = parts[k][at].astype(F32)
            buffer[slot, :, 0, :] = value[:, 0:panel]
            buffer[slot, :, 1, :] = value[:, panel : 2 * panel]
            start = (mine ^ k) * w + ((group ^ j) * rows if rows < w else 0)
            copy = pltpu.make_async_copy(buffer.at[slot], out.at[pl.ds(start, rows)], sems.at[slot])
            copy.start()
            copies.append(copy)
    for copy in copies:
        copy.wait()


def on_device(
    orbitals, elem_count, connectivity, elem_coef, elem_matrix, potential, absorber, rotation
):
    nodes, _, bands = orbitals.shape
    blocks = lax.axis_size("elem")
    parts = lax.axis_size("band")
    e_cap, elem_nodes = connectivity.shape[1:]
    panel = rotation.shape[2]
    groups = blocks // GROUP
    w = bands // GROUP
    span = 3 * nodes
    width = up(max(elem_nodes, span), 128)
    wp = max(up(w, 64), width // 2)
    lanes = 2 * wp
    cols = panel // parts
    pc = cols // GROUP
    pcp = up(pc, 64)
    elem = lax.axis_index("elem")
    band = lax.axis_index("band")
    scal = jnp.stack([elem % GROUP, elem // GROUP, jnp.int32(groups), band]).astype(jnp.int32)

    def struct(*shape, dtype=BF16):
        return jax.ShapeDtypeStruct(shape, dtype)

    def in_group(k):
        return [(i, i ^ k) for i in range(blocks)]

    def swap(values):
        return [values[0]] + [lax.ppermute(values[k], "elem", in_group(k)) for k in range(1, GROUP)]

    twins = [(i, i ^ GROUP) for i in range(blocks) if i ^ GROUP < blocks]
    nexts = [(i, i + GROUP) for i in range(blocks - GROUP) if i // GROUP % 2]
    nexts = nexts + [(b, a) for a, b in nexts]

    def neighbours(value):
        return lax.ppermute(value, "elem", twins), lax.ppermute(value, "elem", nexts)

    turn = [(0, 1), (1, 0)]

    vec = jnp.moveaxis(orbitals, 1, 0)
    rot = jnp.moveaxis(rotation, 1, 0)
    half = struct(nodes, 2 * cols, dtype=F32)
    sums = call(
        functools.partial(rotate_body, parts),
        [half, half] if parts == 2 else [struct(parts, nodes, 2 * cols, dtype=F32)],
        [SMEM, VMEM, VMEM],
        (scal, vec, rot),
        flops=2 * nodes * 2 * bands * 2 * panel,
        moved=2 * bands * 2 * panel,
    )
    if parts == 2:
        terms = (sums[0], lax.ppermute(sums[1], "band", turn))
    else:
        whole = lax.psum_scatter(sums[0], "band", scatter_dimension=0, tiled=True)[0]
        terms = (whole, jnp.zeros_like(whole))

    all_lanes = lanes + 2 * pcp
    messages = call(
        functools.partial(pack_body, w, wp, pc, pcp),
        struct(GROUP, nodes + SMALL, all_lanes),
        [SMEM, VMEM, VMEM, VMEM, ANY, ANY, ANY, ANY],
        (elem_count, vec, *terms, connectivity[0], elem_coef, potential[None], absorber[None]),
        scratch=[
            pltpu.VMEM((e_cap, elem_nodes), jnp.int32),
            pltpu.VMEM((1, e_cap), F32),
            pltpu.VMEM((1, nodes), F32),
            pltpu.VMEM((1, nodes), F32),
            pltpu.VMEM((SMALL, all_lanes), F32),
            pltpu.SemaphoreType.DMA((4,)),
        ],
        moved=4 * nodes * bands * 2,
    )
    lines = [[GROUP * z + i for i in range(GROUP)] for z in range(groups)]
    messages = lax.all_to_all(messages, "elem", 0, 0, axis_index_groups=lines, tiled=True)

    small = messages[:, nodes:]
    small_near = neighbours(small)
    near = neighbours(messages)
    matrix = jnp.pad(elem_matrix, ((0, width - elem_nodes), (0, width - elem_nodes)))
    rows_out = 2 * GROUP
    k_hi, k_lo = call(
        functools.partial(build_body, nodes, e_cap),
        [struct(rows_out, nodes, 5 * nodes)] * 2,
        [SMEM] + [VMEM] * 4,
        (scal, small, *small_near, matrix),
        scratch=[
            pltpu.VMEM((3 * GROUP, 8, width), F32),
            pltpu.VMEM((up(3 * GROUP, 8), 128), F32),
            pltpu.SMEM((up(3 * GROUP, 8), 128), F32),
            pltpu.VMEM((rows_out, nodes, 5 * nodes), F32),
            pltpu.SemaphoreType.DMA,
        ],
        flops=2 * 40 * 3 * width * width * span,
        moved=4 * rows_out * nodes * 5 * nodes,
    )
    *fields, left, out_panel = call(
        functools.partial(filter_body, nodes, wp, pcp),
        [struct(nodes, lanes)] * GROUP + [struct(GROUP, nodes, lanes), struct(GROUP, nodes, 2 * pcp)],
        [SMEM] + [VMEM] * 5,
        (scal, messages, *near, k_hi, k_lo),
        scratch=[
            pltpu.VMEM((3 * GROUP * nodes, all_lanes), BF16),
            pltpu.VMEM((rows_out * nodes, all_lanes), BF16),
            pltpu.VMEM((3 * GROUP, nodes, 128), F32),
        ],
        flops=2 * 2 * 12 * nodes * 5 * nodes * all_lanes,
        moved=4 * rows_out * nodes * 5 * nodes,
    )

    gathered = swap([out_panel] * GROUP)
    if parts == 2:
        all_panels = gathered + [lax.ppermute(x, "band", turn) for x in gathered]
    else:
        every = lax.all_gather(jnp.stack(gathered), "band", axis=0)
        every = jnp.roll(every, -band, axis=0)
        all_panels = [every[h, j] for h in range(parts) for j in range(GROUP)]

    direct = groups == 4 and w % (groups * 16) == 0
    split = groups if direct else 1
    rows = w // split
    *terms, rotated = call(
        functools.partial(
            overlap_body, w, wp, pc, pcp, parts, 1.0 / (nodes * blocks) ** 0.5, split
        ),
        [struct(rows, 2 * panel, dtype=BF16 if direct else F32)] * split + [struct(2, nodes, cols)],
        [SMEM] + [VMEM] * (1 + GROUP * parts),
        (scal, left, *all_panels),
        scratch=[
            pltpu.VMEM((lanes, GROUP * nodes), BF16),
            pltpu.VMEM((GROUP * nodes, 2 * pcp * GROUP * parts), BF16),
            pltpu.VMEM((w, 2 * panel), F32),
        ],
        flops=2 * GROUP * nodes * lanes * 2 * panel,
        moved=4 * GROUP * nodes * panel,
    )
    fields, _ = lax.optimization_barrier((list(fields), gathered[GROUP - 1]))
    received = swap(fields)
    filtered = call(
        functools.partial(collect_body, w, wp),
        struct(2, nodes, bands),
        [SMEM] + [VMEM] * GROUP,
        (scal, *received),
    )
    if direct:

        def across(values):
            return [values[0]] + [
                lax.ppermute(values[j], "elem", [(i, i ^ (GROUP * j)) for i in range(blocks)])
                for j in range(1, split)
            ]

        moved = across(terms)
        moved, filtered = lax.optimization_barrier((moved, filtered))
        own = call(sum_body, struct(rows, 2 * panel), [VMEM] * split, moved)
        stack = across([own] * split)
        batches = [[0], list(range(1, split))]
    else:
        lines = [[GROUP * z + i for z in range(groups)] for i in range(GROUP)]
        stack = [lax.psum(terms[0], "elem", axis_index_groups=lines).astype(BF16)]
        batches = [[0]]
    intersection = None
    spread = None
    for batch in batches:
        ready = jnp.stack([stack[j] for j in batch])
        if spread is not None:
            ready, spread = lax.optimization_barrier((ready, spread))
        base = [] if intersection is None else [intersection]
        spread = swap([ready] * GROUP)
        intersection = call(
            functools.partial(spread_body, w, rows, batch, panel, len(base)),
            struct(bands, 2, panel, dtype=F32),
            [SMEM] + [VMEM] * GROUP + [ANY] * len(base),
            (scal, *spread, *base),
            scratch=[
                pltpu.VMEM((GROUP * len(batch), rows, 2, panel), F32),
                pltpu.SemaphoreType.DMA((GROUP * len(batch),)),
            ],
            out_specs=ANY,
            aliases={GROUP + 1: 0} if base else None,
        )
    return (jnp.moveaxis(filtered, 0, 1), jnp.moveaxis(rotated, 0, 1), intersection)


def solution(mesh):
    placed = (
        P("elem", None, "band"),
        P("elem"),
        P("elem", None, None),
        P("elem", None),
        P(),
        P("elem"),
        P("elem"),
        P(),
    )
    return jax.shard_map(
        on_device,
        mesh=mesh,
        in_specs=placed,
        out_specs=(P("elem", None, "band"), P("elem", None, "band"), P("band", None, None)),
        check_vma=False,
    )
```

```python
import functools

import jax
import jax.numpy as jnp
from jax import lax
from jax.experimental import pallas as pl
from jax.experimental.pallas import tpu as pltpu
from jax.sharding import PartitionSpec as P

FILTER_CENTER = 1.0
FILTER_HALF = 4.0
GROUP = 4
BF16 = jnp.bfloat16
F32 = jnp.float32
SMALL = 16
VMEM_LIMIT = 48 * 1024 * 1024
VMEM = pl.BlockSpec(memory_space=pltpu.VMEM)
SMEM = pl.BlockSpec(memory_space=pltpu.SMEM)
ANY = pl.BlockSpec(memory_space=pl.ANY)


def up(value, step):
    return -(-value // step) * step


def call(body, out_shape, specs, arrays, scratch=(), flops=0, moved=0, out_specs=None, aliases=None):
    if out_specs is None:
        out_specs = [VMEM] * len(out_shape) if isinstance(out_shape, list) else VMEM
    return pl.pallas_call(
        body,
        out_shape=out_shape,
        in_specs=specs,
        out_specs=out_specs,
        scratch_shapes=list(scratch),
        input_output_aliases=aliases or {},
        compiler_params=pltpu.CompilerParams(vmem_limit_bytes=VMEM_LIMIT),
        cost_estimate=pl.CostEstimate(flops=flops, bytes_accessed=moved, transcendentals=0),
    )(*arrays)


def pieces(value):
    top = value.astype(BF16).astype(F32)
    rest = value - top
    middle = rest.astype(BF16).astype(F32)
    return (top, middle, rest - middle)


def describe_body(count, conn, values, out, small):
    e_cap, elem_nodes = conn.shape
    nodes = (values.shape[1] - 128) // 2
    small[...] = jnp.zeros(small.shape, F32)
    ids = conn[...]
    high = ids >> 7
    small[0:e_cap, 0:elem_nodes] = (ids - (high << 7)).astype(F32)
    small[4 : 4 + e_cap, :] = jnp.full((e_cap, small.shape[1]), 64.0, F32)
    small[4 : 4 + e_cap, 0:elem_nodes] = high.astype(F32)
    lane = lax.broadcasted_iota(jnp.int32, (1, 128), 1)
    coef = jnp.where(lane < jnp.minimum(count[0], e_cap), values[:, 0:128], 0.0)
    for at, part in enumerate(pieces(coef)):
        small[8 + at : 9 + at, 0:128] = part
    for row in (0, 1):
        for at, part in enumerate(pieces(values[:, 128 + row * nodes : 128 + (row + 1) * nodes])):
            small[11 + row : 12 + row, at * nodes : (at + 1) * nodes] = part
    out[...] = small[...].astype(BF16)


def order_body(scal, a0, a1, a2, a3, out, small):
    nodes = out.shape[1]
    for k, part in enumerate((a0, a1, a2, a3)):
        out[scal[0] ^ k] = part[0:nodes]
        small[scal[0] ^ k] = part[nodes:, 0 : small.shape[2]]


def paired(re, im, size):
    if size == re.shape[1]:
        return jnp.concatenate([re, im], axis=1)
    fill = jnp.zeros((re.shape[0], size - re.shape[1]), re.dtype)
    return jnp.concatenate([re, fill, im, fill], axis=1)


def pack_body(w, wp, pc, pcp, scal, vec, own, other, small, twin, next_, *outs):
    cols = pc * GROUP
    nodes = vec.shape[1]
    total = own[...] + other[...]
    for q in range(GROUP):
        bands = paired(vec[0, :, q * w : (q + 1) * w], vec[1, :, q * w : (q + 1) * w], wp)
        panel = paired(
            total[:, q * pc : (q + 1) * pc], total[:, cols + q * pc : cols + (q + 1) * pc], pcp
        ).astype(BF16)
        for k in range(GROUP):

            @pl.when((scal[0] ^ k) == q)
            def _():
                outs[k][0:nodes, 0 : 2 * wp] = bands
                outs[k][0:nodes, 2 * wp :] = panel

    for k in range(GROUP):
        for at, part in enumerate((small, twin, next_)):
            row = nodes + at * SMALL
            outs[k][row : row + SMALL, 0 : small.shape[1]] = part[...]


def rotate_body(parts, scal, vec, rot, *out):
    nodes, bands = vec.shape[1:]
    panel = rot.shape[2]
    mine = pl.ds(pl.multiple_of(scal[3] * bands, bands), bands)
    both = jnp.concatenate([vec[0], vec[1]], axis=0)
    with_re = jnp.dot(both, rot[0, mine, :], preferred_element_type=F32)
    with_im = jnp.dot(both, rot[1, mine, :], preferred_element_type=F32)
    out_re = with_re[0:nodes] - with_im[nodes:]
    out_im = with_im[0:nodes] + with_re[nodes:]
    cols = panel // parts
    for h in range(parts):
        value_re = out_re[:, h * cols : (h + 1) * cols]
        value_im = out_im[:, h * cols : (h + 1) * cols]
        if parts == 2:

            @pl.when(scal[3] == h)
            def _():
                out[0][:, 0:cols] = value_re
                out[0][:, cols : 2 * cols] = value_im

            @pl.when(scal[3] != h)
            def _():
                out[1][:, 0:cols] = value_re
                out[1][:, cols : 2 * cols] = value_im

        else:
            out[0][h, :, 0:cols] = value_re
            out[0][h, :, cols : 2 * cols] = value_im


def spread_line(rows, row, nodes):
    line = rows[row : row + 1, 0:nodes] + rows[row : row + 1, nodes : 2 * nodes]
    line = line + rows[row : row + 1, 2 * nodes : 3 * nodes]
    shape = (nodes, nodes)
    diag = lax.broadcasted_iota(jnp.int32, shape, 0) == lax.broadcasted_iota(jnp.int32, shape, 1)
    return jnp.where(diag, line, 0.0), diag


def add_block(t, first, thirds, nodes, e_cap, ids, coefs_s, matrix, acc, base):
    width = matrix.shape[0]
    span = 3 * nodes
    rows = thirds * nodes

    def add(count):
        place = lax.broadcasted_iota(jnp.int32, (span, width), 0).astype(F32)
        marks = [ids[t, e : e + 1, :] for e in range(count)]
        hots = [jnp.where(place == mark, 1.0, 0.0).astype(BF16) for mark in marks]
        if thirds == 3:
            used = hots
        else:
            shift = (first * nodes).astype(F32)
            used = [jnp.where(place[:rows] == mark - shift, 1.0, 0.0).astype(BF16) for mark in marks]
        half = jnp.dot(jnp.concatenate(used, axis=0), matrix[...], preferred_element_type=F32)
        half = [half[e * rows : (e + 1) * rows] * coefs_s[t, e] for e in range(count)]
        tops = [value.astype(BF16) for value in half]
        lows = [(value - part.astype(F32)).astype(BF16) for value, part in zip(half, tops)]
        full = lax.dot_general(
            jnp.concatenate(tops + lows, axis=1),
            jnp.concatenate(hots + hots, axis=1),
            (((1,), (1,)), ((), ())),
            preferred_element_type=F32,
        )
        for j in range(thirds):
            third = first + j
            i = t + third - 3 - base
            at = pl.multiple_of((2 - third) * nodes, nodes)
            acc[i, :, pl.ds(at, span)] += full[j * nodes : (j + 1) * nodes]

    live = jnp.int32(0)
    for e in range(e_cap):
        live = live + (coefs_s[t, e] != 0.0).astype(jnp.int32)
    steps = [n for n in (1, 2) if n < e_cap] + [e_cap]
    for at, count in enumerate(steps):
        least = steps[at - 1] if at else 0

        @pl.when((live > least) & (live <= count))
        def _():
            add(count)


def build_body(nodes, e_cap, scal, side_s, small, matrix, *refs):
    outs = refs[0:GROUP]
    ids, coefs, coefs_s, acc, sem = refs[GROUP:]
    side = side_s[0]
    odd = scal[1] & 1
    base = side * GROUP
    coefs[...] = jnp.zeros(coefs.shape, F32)
    acc[...] = jnp.zeros(acc.shape, F32)
    sources = ((0, 1), (1, 2 - 2 * odd), (2, 2 * odd))
    for source, dz in sources:
        for p in range(GROUP):
            rows = small[p, source * SMALL : (source + 1) * SMALL].astype(F32)
            t = dz * GROUP + p
            ids[t, 0:4, :] = rows[0:4] + 128.0 * rows[4:8]
            coefs[pl.ds(t, 1), :] = (rows[8:9] + rows[9:10] + rows[10:11])[:, 0:128]
    copy = pltpu.make_async_copy(coefs, coefs_s, sem)
    copy.start()
    for source, dz in sources:
        for p in range(GROUP):
            i = dz * GROUP + p - 2 - base

            @pl.when((i >= 0) & (i < GROUP))
            def _():
                rows = small[p, source * SMALL : (source + 1) * SMALL].astype(F32)
                line, diag = spread_line(rows, 11, nodes)
                acc[i, :, 2 * nodes : 3 * nodes] = line - jnp.where(diag, FILTER_CENTER, 0.0)

    copy.wait()
    args = (nodes, e_cap, ids, coefs_s, matrix, acc, base)
    low = side == 0

    def whole(step, carry):
        add_block(GROUP - 1 + side * GROUP + step, 0, 3, *args)
        return carry

    def two(step, carry):
        outer = step == 0
        t = jnp.where(low, jnp.where(outer, 2, 5), jnp.where(outer, 9, 6))
        add_block(t, jnp.where(low == outer, 1, 0), 2, *args)
        return carry

    def one(step, carry):
        outer = step == 0
        t = jnp.where(low, jnp.where(outer, 1, 6), jnp.where(outer, 10, 5))
        add_block(t, jnp.where(low == outer, 2, 0), 1, *args)
        return carry

    lax.fori_loop(0, 2, whole, 0)
    lax.fori_loop(0, 2, two, 0)
    lax.fori_loop(0, 2, one, 0)
    for i in range(GROUP):
        value = acc[i] * (1.0 / FILTER_HALF)
        top = value.astype(BF16)
        outs[i][0] = top
        outs[i][1] = (value - top.astype(F32)).astype(BF16)


def join_body(scal, own, twin, next_, small, vec, cols):
    nodes = own.shape[1]
    rows_out = cols.shape[0]
    odd = scal[1] & 1
    for source, (array, dz) in enumerate(((own, 1), (twin, 2 - 2 * odd), (next_, 2 * odd))):
        for p in range(GROUP):
            t = dz * GROUP + p
            vec[pl.ds(pl.multiple_of(t * nodes, nodes), nodes), :] = array[p]
            i = t - 2

            @pl.when((i >= 0) & (i < rows_out))
            def _():
                rows = small[p, source * SMALL : (source + 1) * SMALL].astype(F32)
                line, _ = spread_line(rows, 12, nodes)
                column = jnp.sum(line, axis=1, keepdims=True) * (1.0 / FILTER_HALF)
                cols[i] = jnp.broadcast_to(column, cols.shape[1:])


def filter_body(at, half, scal, side_s, vec, cols, *refs):
    k_one, k_two, refs = refs[:GROUP], refs[GROUP : 2 * GROUP], refs[2 * GROUP :]
    first, keep = refs[-2:]
    outs = refs[:-2]
    rows_out = 2 * GROUP
    nodes = cols.shape[1]
    sign = jnp.where(lax.broadcasted_iota(jnp.int32, (1, 2 * half), 1) < half, 1.0, -1.0)

    def rows_at(block, count):
        return pl.ds(pl.multiple_of(block * nodes, nodes), count * nodes)

    def applied(source, lanes, start, i, rows):
        block = source[rows_at(start, 5), lanes]
        total = jnp.dot(rows[0], block, preferred_element_type=F32)
        total = total + jnp.dot(rows[1], block, preferred_element_type=F32)
        mid = source[rows_at(start + 2, 1), lanes].astype(F32)
        return total + (cols[i][:, 0:1] * sign) * pltpu.roll(mid, half, 1)

    inside_low = scal[1] > 0
    inside_high = scal[1] < scal[2] - 1
    sides = ((k_one, side_s[0]), (k_two, 1 - side_s[0]))
    for parts, side in sides:
        for local in range(GROUP):
            i = side * GROUP + local
            value = applied(vec, slice(at, at + 2 * half), i, i, parts[local])
            kept = ((i >= 2) | inside_low) & ((i < rows_out - 2) | inside_high)
            first[rows_at(i, 1), :] = jnp.where(kept, value, 0.0).astype(BF16)
    for low in (True, False):
        for step in range(GROUP // 2):
            local = GROUP // 2 + step if low else step
            i = step if low else GROUP // 2 + step
            anchor = vec[rows_at(GROUP + i, 1), at : at + 2 * half].astype(F32)
            for parts, side in sides:

                @pl.when((side == 0) == low)
                def _():
                    keep[...] = applied(first, slice(None), i, i + 2, parts[local])

            value = 2.0 * keep[...] - anchor
            if len(outs) == 1:
                outs[0][i] = value.astype(BF16)
                continue
            outs[GROUP][:, rows_at(i, 1)] = jnp.transpose(value).astype(BF16)
            value = value.astype(BF16)
            for k in range(GROUP):

                @pl.when((scal[0] ^ k) == i)
                def _():
                    outs[k][...] = value


def collect_body(w, wp, scal, g0, g1, g2, g3, out):
    mine = scal[0]
    for k, part in enumerate((g0, g1, g2, g3)):
        re = part[:, 0:w]
        im = part[:, wp : wp + w]
        for q in range(GROUP):

            @pl.when((mine ^ k) == q)
            def _():
                out[0, :, q * w : (q + 1) * w] = re
                out[1, :, q * w : (q + 1) * w] = im


def overlap_body(w, wp, pc, pcp, parts, scale, split, scal, left, *refs):
    panels = refs[0 : GROUP * parts]
    outs = refs[GROUP * parts : -3]
    rotated, right, result = refs[-3:]
    mine, band = scal[0], scal[3]
    nodes = panels[0].shape[1]
    tile = 2 * pcp
    chunks = parts * GROUP
    panel = pc * chunks
    for g in range(parts):
        for j in range(GROUP):
            half = (band + g) % parts
            at = pl.multiple_of((half * GROUP + (mine ^ j)) * tile, tile)
            for p in range(GROUP):
                right[p * nodes : (p + 1) * nodes, pl.ds(at, tile)] = panels[g * GROUP + j][p]
    for j in range(GROUP):
        value = panels[j][mine]
        for q in range(GROUP):

            @pl.when((mine ^ j) == q)
            def _():
                rotated[0, :, q * pc : (q + 1) * pc] = value[:, 0:pc]
                rotated[1, :, q * pc : (q + 1) * pc] = value[:, pcp : pcp + pc]

    product = jnp.dot(left[...], right[...], preferred_element_type=F32) * scale
    top, bottom = product[0:w], product[wp : wp + w]
    for s in range(chunks):
        a, b = s * tile, s * tile + pcp
        result[:, s * pc : (s + 1) * pc] = top[:, a : a + pc] - bottom[:, b : b + pc]
        result[:, panel + s * pc : panel + (s + 1) * pc] = top[:, b : b + pc] + bottom[:, a : a + pc]
    if split == 1:
        outs[0][...] = result[...]
    else:
        rows = w // split
        for j in range(split):
            at = pl.multiple_of((scal[1] ^ j) * rows, rows)
            outs[j][...] = result[pl.ds(at, rows), :].astype(BF16)


def sum_body(s0, s1, s2, s3, out):
    total = s0[...].astype(F32) + s1[...].astype(F32)
    total = total + (s2[...].astype(F32) + s3[...].astype(F32))
    out[...] = total.astype(BF16)


def spread_body(w, rows, batch, panel, has_base, scal, *refs):
    parts = refs[0:GROUP]
    out, buffer, sems = refs[GROUP + has_base :]
    mine, group = scal[0], scal[1]
    copies = []
    for k in range(GROUP):
        for at, j in enumerate(batch):
            slot = k * len(batch) + at
            value = parts[k][at].astype(F32)
            buffer[slot, :, 0, :] = value[:, 0:panel]
            buffer[slot, :, 1, :] = value[:, panel : 2 * panel]
            start = (mine ^ k) * w + ((group ^ j) * rows if rows < w else 0)
            copy = pltpu.make_async_copy(buffer.at[slot], out.at[pl.ds(start, rows)], sems.at[slot])
            copy.start()
            copies.append(copy)
    for copy in copies:
        copy.wait()


def on_device(
    orbitals, elem_count, connectivity, elem_coef, elem_matrix, potential, absorber, rotation
):
    nodes, _, bands = orbitals.shape
    blocks = lax.axis_size("elem")
    parts = lax.axis_size("band")
    e_cap, elem_nodes = connectivity.shape[1:]
    panel = rotation.shape[2]
    groups = blocks // GROUP
    w = bands // GROUP
    span = 3 * nodes
    width = up(max(elem_nodes, span), 128)
    wp = max(up(w, 64), width // 2)
    lanes = 2 * wp
    cols = panel // parts
    pc = cols // GROUP
    pcp = up(pc, 64)
    elem = lax.axis_index("elem")
    band = lax.axis_index("band")
    scal = jnp.stack([elem % GROUP, elem // GROUP, jnp.int32(groups), band]).astype(jnp.int32)

    def struct(*shape, dtype=BF16):
        return jax.ShapeDtypeStruct(shape, dtype)

    def in_group(k):
        return [(i, i ^ k) for i in range(blocks)]

    def swap(values):
        return [values[0]] + [lax.ppermute(values[k], "elem", in_group(k)) for k in range(1, GROUP)]

    twins = [(i, i ^ GROUP) for i in range(blocks) if i ^ GROUP < blocks]
    nexts = [(i, i + GROUP) for i in range(blocks - GROUP) if i // GROUP % 2]
    nexts = nexts + [(b, a) for a, b in nexts]

    def neighbours(value):
        return lax.ppermute(value, "elem", twins), lax.ppermute(value, "elem", nexts)

    turn = [(0, 1), (1, 0)]

    values = jnp.concatenate([jnp.pad(elem_coef[0], (0, 128 - e_cap)), potential, absorber])[None]
    small = call(
        describe_body,
        struct(SMALL, width),
        [SMEM, VMEM, VMEM],
        (elem_count, connectivity[0], values),
        scratch=[pltpu.VMEM((SMALL, width), F32)],
    )
    small_near = neighbours(small)
    orbitals, rotation, small = lax.optimization_barrier((orbitals, rotation, small))

    vec = jnp.moveaxis(orbitals, 1, 0)
    rot = jnp.moveaxis(rotation, 1, 0)
    half = struct(nodes, 2 * cols, dtype=F32)
    sums = call(
        functools.partial(rotate_body, parts),
        [half, half] if parts == 2 else [struct(parts, nodes, 2 * cols, dtype=F32)],
        [SMEM, VMEM, VMEM],
        (scal, vec, rot),
        flops=2 * nodes * 2 * bands * 2 * panel,
        moved=2 * bands * 2 * panel,
    )
    if parts == 2:
        terms = (sums[0], lax.ppermute(sums[1], "band", turn))
    else:
        whole = lax.psum_scatter(sums[0], "band", scatter_dimension=0, tiled=True)[0]
        terms = (whole, jnp.zeros_like(whole))

    all_lanes = lanes + 2 * pcp
    messages = call(
        functools.partial(pack_body, w, wp, pc, pcp),
        [struct(nodes + 3 * SMALL, all_lanes)] * GROUP,
        [SMEM] + [VMEM] * 6,
        (scal, vec, *terms, small, *small_near),
        moved=4 * nodes * bands * 2,
    )
    messages, small = call(
        order_body,
        [struct(GROUP, nodes, all_lanes), struct(GROUP, 3 * SMALL, width)],
        [SMEM] + [VMEM] * GROUP,
        (scal, *swap(messages)),
    )
    near = neighbours(messages)

    matrix = jnp.pad(elem_matrix, ((0, width - elem_nodes), (0, width - elem_nodes)))
    table = (up(3 * GROUP, 8), 128)

    def operator(side):
        return call(
            functools.partial(build_body, nodes, e_cap),
            [struct(2, nodes, 5 * nodes)] * GROUP,
            [SMEM, SMEM, VMEM, VMEM],
            (scal, side, small, matrix),
            scratch=[
                pltpu.VMEM((3 * GROUP, 8, width), F32),
                pltpu.VMEM(table, F32),
                pltpu.SMEM(table, F32),
                pltpu.VMEM((GROUP, nodes, 5 * nodes), F32),
                pltpu.SemaphoreType.DMA,
            ],
            flops=4 * 2 * 6 * width * width * span,
            moved=8 * GROUP * nodes * 5 * nodes,
        )

    if parts == 2:
        side = band[None].astype(jnp.int32)
        halves = [operator(side)]
        halves.append([lax.ppermute(part, "band", turn) for part in halves[0]])
    else:
        side = jnp.zeros((1,), jnp.int32)
        halves = [operator(side), operator(side + 1)]

    vec, absorb = call(
        join_body,
        [struct(3 * GROUP * nodes, all_lanes), struct(2 * GROUP, nodes, 128, dtype=F32)],
        [SMEM] + [VMEM] * 4,
        (scal, messages, *near, small),
    )

    def filtered_lanes(at, size, out_shape):
        return call(
            functools.partial(filter_body, at, size // 2),
            out_shape,
            [SMEM, SMEM] + [VMEM] * (2 + 2 * GROUP),
            (scal, side, vec, absorb, *halves[0], *halves[1]),
            scratch=[pltpu.VMEM((2 * GROUP * nodes, size), BF16), pltpu.VMEM((nodes, size), F32)],
            flops=2 * 2 * 12 * nodes * 5 * nodes * size,
            moved=8 * GROUP * nodes * 5 * nodes,
        )

    out_panel = filtered_lanes(lanes, 2 * pcp, struct(GROUP, nodes, 2 * pcp))
    *fields, left = filtered_lanes(
        0, lanes, [struct(nodes, lanes)] * GROUP + [struct(lanes, GROUP * nodes)]
    )

    gathered = swap([out_panel] * GROUP)
    gathered, left, fields = lax.optimization_barrier((gathered, left, list(fields)))
    if parts == 2:
        all_panels = gathered + [lax.ppermute(x, "band", turn) for x in gathered]
    else:
        every = lax.all_gather(jnp.stack(gathered), "band", axis=0)
        every = jnp.roll(every, -band, axis=0)
        all_panels = [every[h, j] for h in range(parts) for j in range(GROUP)]

    direct = groups == 4 and w % (groups * 16) == 0
    split = groups if direct else 1
    rows = w // split
    *terms, rotated = call(
        functools.partial(
            overlap_body, w, wp, pc, pcp, parts, 1.0 / (nodes * blocks) ** 0.5, split
        ),
        [struct(rows, 2 * panel, dtype=BF16 if direct else F32)] * split + [struct(2, nodes, cols)],
        [SMEM] + [VMEM] * (1 + GROUP * parts),
        (scal, left, *all_panels),
        scratch=[
            pltpu.VMEM((GROUP * nodes, 2 * pcp * GROUP * parts), BF16),
            pltpu.VMEM((w, 2 * panel), F32),
        ],
        flops=2 * GROUP * nodes * lanes * 2 * panel,
        moved=4 * GROUP * nodes * panel,
    )
    if direct:

        def across(values):
            return [values[0]] + [
                lax.ppermute(values[j], "elem", [(i, i ^ (GROUP * j)) for i in range(blocks)])
                for j in range(1, split)
            ]

        moved = across(terms)
        moved[1], fields = lax.optimization_barrier((moved[1], fields))
        own = call(sum_body, struct(rows, 2 * panel), [VMEM] * split, moved)
        stack = across([own] * split)
        batches = [[0], list(range(1, split))]
    else:
        lines = [[GROUP * z + i for z in range(groups)] for i in range(GROUP)]
        stack = [lax.psum(terms[0], "elem", axis_index_groups=lines).astype(BF16)]
        batches = [[0]]
    received = swap(fields)
    filtered = call(
        functools.partial(collect_body, w, wp),
        struct(2, nodes, bands),
        [SMEM] + [VMEM] * GROUP,
        (scal, *received),
    )
    intersection = None
    earliest = None
    for batch in batches:
        ready = jnp.stack([stack[j] for j in batch])
        if earliest is not None:
            ready, filtered, _ = lax.optimization_barrier((ready, filtered, earliest))
        base = [] if intersection is None else [intersection]
        spread = swap([ready] * GROUP)
        if earliest is None:
            earliest = spread
        intersection = call(
            functools.partial(spread_body, w, rows, batch, panel, len(base)),
            struct(bands, 2, panel, dtype=F32),
            [SMEM] + [VMEM] * GROUP + [ANY] * len(base),
            (scal, *spread, *base),
            scratch=[
                pltpu.VMEM((GROUP * len(batch), rows, 2, panel), F32),
                pltpu.SemaphoreType.DMA((GROUP * len(batch),)),
            ],
            out_specs=ANY,
            aliases={GROUP + 1: 0} if base else None,
        )
    return (jnp.moveaxis(filtered, 0, 1), jnp.moveaxis(rotated, 0, 1), intersection)


def solution(mesh):
    placed = (
        P("elem", None, "band"),
        P("elem"),
        P("elem", None, None),
        P("elem", None),
        P(),
        P("elem"),
        P("elem"),
        P(),
    )
    return jax.shard_map(
        on_device,
        mesh=mesh,
        in_specs=placed,
        out_specs=(P("elem", None, "band"), P("elem", None, "band"), P("band", None, None)),
        check_vma=False,
    )
```

```python
import functools

import jax
import jax.numpy as jnp
from jax import lax
from jax.experimental import pallas as pl
from jax.experimental.pallas import tpu as pltpu
from jax.sharding import PartitionSpec as P

FILTER_CENTER = 1.0
FILTER_HALF = 4.0
GROUP = 4
BF16 = jnp.bfloat16
F32 = jnp.float32
SMALL = 16
VMEM_LIMIT = 48 * 1024 * 1024
WEIGHT = 4 * 10**9
VMEM = pl.BlockSpec(memory_space=pltpu.VMEM)
SMEM = pl.BlockSpec(memory_space=pltpu.SMEM)
ANY = pl.BlockSpec(memory_space=pl.ANY)


def up(value, step):
    return -(-value // step) * step


def call(body, out_shape, specs, arrays, scratch=(), flops=0, moved=0, out_specs=None, aliases=None):
    if out_specs is None:
        out_specs = [VMEM] * len(out_shape) if isinstance(out_shape, list) else VMEM
    return pl.pallas_call(
        body,
        out_shape=out_shape,
        in_specs=specs,
        out_specs=out_specs,
        scratch_shapes=list(scratch),
        input_output_aliases=aliases or {},
        compiler_params=pltpu.CompilerParams(vmem_limit_bytes=VMEM_LIMIT),
        cost_estimate=pl.CostEstimate(flops=flops, bytes_accessed=moved, transcendentals=0),
    )(*arrays)


def pieces(value):
    top = value.astype(BF16).astype(F32)
    rest = value - top
    middle = rest.astype(BF16).astype(F32)
    return (top, middle, rest - middle)


def describe_body(count, conn, values, out, small):
    e_cap, elem_nodes = conn.shape
    nodes = (values.shape[1] - 128) // 2
    small[...] = jnp.zeros(small.shape, F32)
    ids = conn[...]
    high = ids >> 7
    small[0:e_cap, 0:elem_nodes] = (ids - (high << 7)).astype(F32)
    small[4 : 4 + e_cap, :] = jnp.full((e_cap, small.shape[1]), 64.0, F32)
    small[4 : 4 + e_cap, 0:elem_nodes] = high.astype(F32)
    lane = lax.broadcasted_iota(jnp.int32, (1, 128), 1)
    coef = jnp.where(lane < jnp.minimum(count[0], e_cap), values[:, 0:128], 0.0)
    for at, part in enumerate(pieces(coef)):
        small[8 + at : 9 + at, 0:128] = part
    for row in (0, 1):
        for at, part in enumerate(pieces(values[:, 128 + row * nodes : 128 + (row + 1) * nodes])):
            small[11 + row : 12 + row, at * nodes : (at + 1) * nodes] = part
    out[...] = small[...].astype(BF16)


def order_body(scal, a0, a1, a2, a3, out, small):
    nodes = out.shape[1]
    for k, part in enumerate((a0, a1, a2, a3)):
        out[scal[0] ^ k] = part[0:nodes]
        small[scal[0] ^ k] = part[nodes:, 0 : small.shape[2]]


def paired(re, im, size):
    if size == re.shape[1]:
        return jnp.concatenate([re, im], axis=1)
    fill = jnp.zeros((re.shape[0], size - re.shape[1]), re.dtype)
    return jnp.concatenate([re, fill, im, fill], axis=1)


def pack_body(w, wp, pc, pcp, scal, vec, own, other, small, twin, next_, *outs):
    cols = pc * GROUP
    nodes = vec.shape[1]
    total = own[...] + other[...]
    for q in range(GROUP):
        bands = paired(vec[0, :, q * w : (q + 1) * w], vec[1, :, q * w : (q + 1) * w], wp)
        panel = paired(
            total[:, q * pc : (q + 1) * pc], total[:, cols + q * pc : cols + (q + 1) * pc], pcp
        ).astype(BF16)
        for k in range(GROUP):

            @pl.when((scal[0] ^ k) == q)
            def _():
                outs[k][0:nodes, 0 : 2 * wp] = bands
                outs[k][0:nodes, 2 * wp :] = panel

    for k in range(GROUP):
        for at, part in enumerate((small, twin, next_)):
            row = nodes + at * SMALL
            outs[k][row : row + SMALL, 0 : small.shape[1]] = part[...]


def rotate_body(parts, scal, vec, rot, *out):
    nodes, bands = vec.shape[1:]
    panel = rot.shape[2]
    mine = pl.ds(pl.multiple_of(scal[3] * bands, bands), bands)
    both = jnp.concatenate([vec[0], vec[1]], axis=0)
    with_re = jnp.dot(both, rot[0, mine, :], preferred_element_type=F32)
    with_im = jnp.dot(both, rot[1, mine, :], preferred_element_type=F32)
    out_re = with_re[0:nodes] - with_im[nodes:]
    out_im = with_im[0:nodes] + with_re[nodes:]
    cols = panel // parts
    for h in range(parts):
        value_re = out_re[:, h * cols : (h + 1) * cols]
        value_im = out_im[:, h * cols : (h + 1) * cols]
        if parts == 2:

            @pl.when(scal[3] == h)
            def _():
                out[0][:, 0:cols] = value_re
                out[0][:, cols : 2 * cols] = value_im

            @pl.when(scal[3] != h)
            def _():
                out[1][:, 0:cols] = value_re
                out[1][:, cols : 2 * cols] = value_im

        else:
            out[0][h, :, 0:cols] = value_re
            out[0][h, :, cols : 2 * cols] = value_im


def spread_line(rows, row, nodes):
    line = rows[row : row + 1, 0:nodes] + rows[row : row + 1, nodes : 2 * nodes]
    line = line + rows[row : row + 1, 2 * nodes : 3 * nodes]
    shape = (nodes, nodes)
    diag = lax.broadcasted_iota(jnp.int32, shape, 0) == lax.broadcasted_iota(jnp.int32, shape, 1)
    return jnp.where(diag, line, 0.0), diag


def add_block(t, first, thirds, nodes, e_cap, ids, coefs_s, matrix, acc, base):
    width = matrix.shape[0]
    span = 3 * nodes
    rows = thirds * nodes

    def add(count):
        place = lax.broadcasted_iota(jnp.int32, (span, width), 0).astype(F32)
        marks = [ids[t, e : e + 1, :] for e in range(count)]
        hots = [jnp.where(place == mark, 1.0, 0.0).astype(BF16) for mark in marks]
        if thirds == 3:
            used = hots
        else:
            shift = (first * nodes).astype(F32)
            used = [jnp.where(place[:rows] == mark - shift, 1.0, 0.0).astype(BF16) for mark in marks]
        half = jnp.dot(jnp.concatenate(used, axis=0), matrix[...], preferred_element_type=F32)
        half = [half[e * rows : (e + 1) * rows] * coefs_s[t, e] for e in range(count)]
        tops = [value.astype(BF16) for value in half]
        lows = [(value - part.astype(F32)).astype(BF16) for value, part in zip(half, tops)]
        full = lax.dot_general(
            jnp.concatenate(tops + lows, axis=1),
            jnp.concatenate(hots + hots, axis=1),
            (((1,), (1,)), ((), ())),
            preferred_element_type=F32,
        )
        for j in range(thirds):
            third = first + j
            i = t + third - 3 - base
            at = pl.multiple_of((2 - third) * nodes, nodes)
            acc[i, :, pl.ds(at, span)] += full[j * nodes : (j + 1) * nodes]

    live = jnp.int32(0)
    for e in range(e_cap):
        live = live + (coefs_s[t, e] != 0.0).astype(jnp.int32)
    steps = [n for n in (1, 2) if n < e_cap] + [e_cap]
    for at, count in enumerate(steps):
        least = steps[at - 1] if at else 0

        @pl.when((live > least) & (live <= count))
        def _():
            add(count)


def build_body(nodes, e_cap, scal, side_s, small, matrix, *refs):
    outs = refs[0:GROUP]
    ids, coefs, coefs_s, acc, sem = refs[GROUP:]
    side = side_s[0]
    odd = scal[1] & 1
    base = side * GROUP
    coefs[...] = jnp.zeros(coefs.shape, F32)
    acc[...] = jnp.zeros(acc.shape, F32)
    sources = ((0, 1), (1, 2 - 2 * odd), (2, 2 * odd))
    for source, dz in sources:
        for p in range(GROUP):
            rows = small[p, source * SMALL : (source + 1) * SMALL].astype(F32)
            t = dz * GROUP + p
            ids[t, 0:4, :] = rows[0:4] + 128.0 * rows[4:8]
            coefs[pl.ds(t, 1), :] = (rows[8:9] + rows[9:10] + rows[10:11])[:, 0:128]
    copy = pltpu.make_async_copy(coefs, coefs_s, sem)
    copy.start()
    for source, dz in sources:
        for p in range(GROUP):
            i = dz * GROUP + p - 2 - base

            @pl.when((i >= 0) & (i < GROUP))
            def _():
                rows = small[p, source * SMALL : (source + 1) * SMALL].astype(F32)
                line, diag = spread_line(rows, 11, nodes)
                acc[i, :, 2 * nodes : 3 * nodes] = line - jnp.where(diag, FILTER_CENTER, 0.0)

    copy.wait()
    args = (nodes, e_cap, ids, coefs_s, matrix, acc, base)
    low = side == 0

    def whole(step, carry):
        add_block(GROUP - 1 + side * GROUP + step, 0, 3, *args)
        return carry

    def two(step, carry):
        outer = step == 0
        t = jnp.where(low, jnp.where(outer, 2, 5), jnp.where(outer, 9, 6))
        add_block(t, jnp.where(low == outer, 1, 0), 2, *args)
        return carry

    def one(step, carry):
        outer = step == 0
        t = jnp.where(low, jnp.where(outer, 1, 6), jnp.where(outer, 10, 5))
        add_block(t, jnp.where(low == outer, 2, 0), 1, *args)
        return carry

    lax.fori_loop(0, 2, whole, 0)
    lax.fori_loop(0, 2, two, 0)
    lax.fori_loop(0, 2, one, 0)
    for i in range(GROUP):
        value = acc[i] * (1.0 / FILTER_HALF)
        top = value.astype(BF16)
        outs[i][0] = top
        outs[i][1] = (value - top.astype(F32)).astype(BF16)


def columns_body(scal, small, cols):
    rows_out, nodes = cols.shape[0:2]
    odd = scal[1] & 1
    for source, dz in ((0, 1), (1, 2 - 2 * odd), (2, 2 * odd)):
        for p in range(GROUP):
            i = dz * GROUP + p - 2

            @pl.when((i >= 0) & (i < rows_out))
            def _():
                rows = small[p, source * SMALL : (source + 1) * SMALL].astype(F32)
                line, _ = spread_line(rows, 12, nodes)
                column = jnp.sum(line, axis=1, keepdims=True) * (1.0 / FILTER_HALF)
                cols[i] = jnp.broadcast_to(column, cols.shape[1:])


def join_body(scal, own, twin, next_, vec):
    nodes = own.shape[1]
    odd = scal[1] & 1
    for array, dz in ((own, 1), (twin, 2 - 2 * odd), (next_, 2 * odd)):
        for p in range(GROUP):
            t = dz * GROUP + p
            vec[pl.ds(pl.multiple_of(t * nodes, nodes), nodes), :] = array[p]


def filter_body(at, half, scal, side_s, vec, cols, *refs):
    k_one, k_two, refs = refs[:GROUP], refs[GROUP : 2 * GROUP], refs[2 * GROUP :]
    first, keep = refs[-2:]
    outs = refs[:-2]
    rows_out = 2 * GROUP
    nodes = cols.shape[1]
    sign = jnp.where(lax.broadcasted_iota(jnp.int32, (1, 2 * half), 1) < half, 1.0, -1.0)

    def rows_at(block, count):
        return pl.ds(pl.multiple_of(block * nodes, nodes), count * nodes)

    def applied(source, lanes, start, i, rows):
        block = source[rows_at(start, 5), lanes]
        total = jnp.dot(rows[0], block, preferred_element_type=F32)
        total = total + jnp.dot(rows[1], block, preferred_element_type=F32)
        mid = source[rows_at(start + 2, 1), lanes].astype(F32)
        return total + (cols[i][:, 0:1] * sign) * pltpu.roll(mid, half, 1)

    inside_low = scal[1] > 0
    inside_high = scal[1] < scal[2] - 1
    sides = ((k_one, side_s[0]), (k_two, 1 - side_s[0]))
    for parts, side in sides:
        for local in range(GROUP):
            i = side * GROUP + local
            value = applied(vec, slice(at, at + 2 * half), i, i, parts[local])
            kept = ((i >= 2) | inside_low) & ((i < rows_out - 2) | inside_high)
            first[rows_at(i, 1), :] = jnp.where(kept, value, 0.0).astype(BF16)
    for low in (True, False):
        for step in range(GROUP // 2):
            local = GROUP // 2 + step if low else step
            i = step if low else GROUP // 2 + step
            anchor = vec[rows_at(GROUP + i, 1), at : at + 2 * half].astype(F32)
            for parts, side in sides:

                @pl.when((side == 0) == low)
                def _():
                    keep[...] = applied(first, slice(None), i, i + 2, parts[local])

            value = 2.0 * keep[...] - anchor
            if len(outs) == 1:
                outs[0][i] = value.astype(BF16)
                continue
            outs[GROUP][:, rows_at(i, 1)] = jnp.transpose(value).astype(BF16)
            value = value.astype(BF16)
            for k in range(GROUP):

                @pl.when((scal[0] ^ k) == i)
                def _():
                    outs[k][...] = value


def collect_body(w, wp, scal, g0, g1, g2, g3, out):
    mine = scal[0]
    for k, part in enumerate((g0, g1, g2, g3)):
        re = part[:, 0:w]
        im = part[:, wp : wp + w]
        for q in range(GROUP):

            @pl.when((mine ^ k) == q)
            def _():
                out[0, :, q * w : (q + 1) * w] = re
                out[1, :, q * w : (q + 1) * w] = im


def overlap_body(w, wp, pc, pcp, parts, scale, split, scal, left, *refs):
    panels = refs[0 : GROUP * parts]
    outs = refs[GROUP * parts : -3]
    rotated, right, result = refs[-3:]
    mine, band = scal[0], scal[3]
    nodes = panels[0].shape[1]
    tile = 2 * pcp
    chunks = parts * GROUP
    panel = pc * chunks
    for g in range(parts):
        for j in range(GROUP):
            half = (band + g) % parts
            at = pl.multiple_of((half * GROUP + (mine ^ j)) * tile, tile)
            for p in range(GROUP):
                right[p * nodes : (p + 1) * nodes, pl.ds(at, tile)] = panels[g * GROUP + j][p]
    for j in range(GROUP):
        value = panels[j][mine]
        for q in range(GROUP):

            @pl.when((mine ^ j) == q)
            def _():
                rotated[0, :, q * pc : (q + 1) * pc] = value[:, 0:pc]
                rotated[1, :, q * pc : (q + 1) * pc] = value[:, pcp : pcp + pc]

    product = jnp.dot(left[...], right[...], preferred_element_type=F32) * scale
    top, bottom = product[0:w], product[wp : wp + w]
    for s in range(chunks):
        a, b = s * tile, s * tile + pcp
        result[:, s * pc : (s + 1) * pc] = top[:, a : a + pc] - bottom[:, b : b + pc]
        result[:, panel + s * pc : panel + (s + 1) * pc] = top[:, b : b + pc] + bottom[:, a : a + pc]
    if split == 1:
        outs[0][...] = result[...]
    else:
        rows = w // split
        for j in range(split):
            at = pl.multiple_of((scal[1] ^ j) * rows, rows)
            outs[j][...] = result[pl.ds(at, rows), :].astype(BF16)


def sum_body(s0, s1, s2, s3, out):
    total = s0[...].astype(F32) + s1[...].astype(F32)
    total = total + (s2[...].astype(F32) + s3[...].astype(F32))
    out[...] = total.astype(BF16)


def copy_body(given, out):
    out[...] = given[...]


def spread_body(w, rows, plan, count, panel, scal, *refs):
    out, buffer, sems = refs[-3:]
    mine, group = scal[0], scal[1]
    copies = []
    for slot, (array, at, k, j) in enumerate(plan):
        value = refs[array][at].astype(F32)
        buffer[slot, :, 0, :] = value[:, 0:panel]
        buffer[slot, :, 1, :] = value[:, panel : 2 * panel]
        start = (mine ^ k) * w + ((group ^ j) * rows if rows < w else 0)
        copy = pltpu.make_async_copy(buffer.at[slot], out.at[pl.ds(start, rows)], sems.at[slot])
        copy.start()
        copies.append(copy)
    for copy in copies:
        copy.wait()


def on_device(
    orbitals, elem_count, connectivity, elem_coef, elem_matrix, potential, absorber, rotation
):
    nodes, _, bands = orbitals.shape
    blocks = lax.axis_size("elem")
    parts = lax.axis_size("band")
    e_cap, elem_nodes = connectivity.shape[1:]
    panel = rotation.shape[2]
    groups = blocks // GROUP
    w = bands // GROUP
    span = 3 * nodes
    width = up(max(elem_nodes, span), 128)
    wp = max(up(w, 64), width // 2)
    lanes = 2 * wp
    cols = panel // parts
    pc = cols // GROUP
    pcp = up(pc, 64)
    elem = lax.axis_index("elem")
    band = lax.axis_index("band")
    scal = jnp.stack([elem % GROUP, elem // GROUP, jnp.int32(groups), band]).astype(jnp.int32)

    def struct(*shape, dtype=BF16):
        return jax.ShapeDtypeStruct(shape, dtype)

    def in_group(k):
        return [(i, i ^ k) for i in range(blocks)]

    def swap(values):
        return [values[0]] + [lax.ppermute(values[k], "elem", in_group(k)) for k in range(1, GROUP)]

    twins = [(i, i ^ GROUP) for i in range(blocks) if i ^ GROUP < blocks]
    nexts = [(i, i + GROUP) for i in range(blocks - GROUP) if i // GROUP % 2]
    nexts = nexts + [(b, a) for a, b in nexts]

    def neighbours(value):
        return lax.ppermute(value, "elem", twins), lax.ppermute(value, "elem", nexts)

    turn = [(0, 1), (1, 0)]

    values = jnp.concatenate([jnp.pad(elem_coef[0], (0, 128 - e_cap)), potential, absorber])[None]
    small = call(
        describe_body,
        struct(SMALL, width),
        [SMEM, VMEM, VMEM],
        (elem_count, connectivity[0], values),
        scratch=[pltpu.VMEM((SMALL, width), F32)],
    )
    small_near = neighbours(small)
    orbitals, small = lax.optimization_barrier((orbitals, small))
    rotation, small_near = lax.optimization_barrier((rotation, small_near))

    vec = jnp.moveaxis(orbitals, 1, 0)
    rot = jnp.moveaxis(rotation, 1, 0)
    half = struct(nodes, 2 * cols, dtype=F32)
    sums = call(
        functools.partial(rotate_body, parts),
        [half, half] if parts == 2 else [struct(parts, nodes, 2 * cols, dtype=F32)],
        [SMEM, VMEM, VMEM],
        (scal, vec, rot),
        flops=2 * nodes * 2 * bands * 2 * panel,
        moved=2 * bands * 2 * panel,
    )
    if parts == 2:
        terms = (sums[0], lax.ppermute(sums[1], "band", turn))
    else:
        whole = lax.psum_scatter(sums[0], "band", scatter_dimension=0, tiled=True)[0]
        terms = (whole, jnp.zeros_like(whole))

    all_lanes = lanes + 2 * pcp
    messages = call(
        functools.partial(pack_body, w, wp, pc, pcp),
        [struct(nodes + 3 * SMALL, all_lanes)] * GROUP,
        [SMEM] + [VMEM] * 6,
        (scal, vec, *terms, small, *small_near),
        moved=4 * nodes * bands * 2,
    )
    messages, small = call(
        order_body,
        [struct(GROUP, nodes, all_lanes), struct(GROUP, 3 * SMALL, width)],
        [SMEM] + [VMEM] * GROUP,
        (scal, *swap(messages)),
    )
    near = neighbours(messages)

    matrix = jnp.pad(elem_matrix, ((0, width - elem_nodes), (0, width - elem_nodes)))
    table = (up(3 * GROUP, 8), 128)

    def operator(side):
        return call(
            functools.partial(build_body, nodes, e_cap),
            [struct(2, nodes, 5 * nodes)] * GROUP,
            [SMEM, SMEM, VMEM, VMEM],
            (scal, side, small, matrix),
            scratch=[
                pltpu.VMEM((3 * GROUP, 8, width), F32),
                pltpu.VMEM(table, F32),
                pltpu.SMEM(table, F32),
                pltpu.VMEM((GROUP, nodes, 5 * nodes), F32),
                pltpu.SemaphoreType.DMA,
            ],
            flops=4 * 2 * 6 * width * width * span,
            moved=8 * GROUP * nodes * 5 * nodes,
        )

    if parts == 2:
        side = band[None].astype(jnp.int32)
        halves = [operator(side)]
        halves.append([lax.ppermute(part, "band", turn) for part in halves[0]])
    else:
        side = jnp.zeros((1,), jnp.int32)
        halves = [operator(side), operator(side + 1)]

    absorb = call(
        columns_body, struct(2 * GROUP, nodes, 128, dtype=F32), [SMEM, VMEM], (scal, small)
    )
    vec = call(
        join_body,
        struct(3 * GROUP * nodes, all_lanes),
        [SMEM] + [VMEM] * 3,
        (scal, messages, *near),
    )

    def filtered_lanes(at, size, out_shape):
        return call(
            functools.partial(filter_body, at, size // 2),
            out_shape,
            [SMEM, SMEM] + [VMEM] * (2 + 2 * GROUP),
            (scal, side, vec, absorb, *halves[0], *halves[1]),
            scratch=[pltpu.VMEM((2 * GROUP * nodes, size), BF16), pltpu.VMEM((nodes, size), F32)],
            flops=2 * 2 * 12 * nodes * 5 * nodes * size,
            moved=8 * GROUP * nodes * 5 * nodes,
        )

    out_panel = filtered_lanes(lanes, 2 * pcp, struct(GROUP, nodes, 2 * pcp))
    *fields, left = filtered_lanes(
        0, lanes, [struct(nodes, lanes)] * GROUP + [struct(lanes, GROUP * nodes)]
    )

    gathered = swap([out_panel] * GROUP)
    gathered, left, fields = lax.optimization_barrier((gathered, left, list(fields)))
    if parts == 2:
        all_panels = gathered + [lax.ppermute(x, "band", turn) for x in gathered]
    else:
        every = lax.all_gather(jnp.stack(gathered), "band", axis=0)
        every = jnp.roll(every, -band, axis=0)
        all_panels = [every[h, j] for h in range(parts) for j in range(GROUP)]

    direct = groups == 4 and w % (groups * 16) == 0
    split = groups if direct else 1
    rows = w // split
    *terms, rotated = call(
        functools.partial(
            overlap_body, w, wp, pc, pcp, parts, 1.0 / (nodes * blocks) ** 0.5, split
        ),
        [struct(rows, 2 * panel, dtype=BF16 if direct else F32)] * split + [struct(2, nodes, cols)],
        [SMEM] + [VMEM] * (1 + GROUP * parts),
        (scal, left, *all_panels),
        scratch=[
            pltpu.VMEM((GROUP * nodes, 2 * pcp * GROUP * parts), BF16),
            pltpu.VMEM((w, 2 * panel), F32),
        ],
        flops=2 * GROUP * nodes * lanes * 2 * panel,
        moved=4 * GROUP * nodes * panel,
    )
    if direct:

        def across(values, least=1):
            return values[:least] + [
                lax.ppermute(values[j], "elem", [(i, i ^ (GROUP * j)) for i in range(blocks)])
                for j in range(least, split)
            ]

        moved = across(terms)
        moved[1], fields = lax.optimization_barrier((moved[1], fields))
        received = swap(fields)
        moved[2:], received = lax.optimization_barrier((moved[2:], received))
        own = call(sum_body, struct(rows, 2 * panel), [VMEM] * split, moved)
        stack = [own, None] + across([own] * split, 2)[2:]
    else:
        received = swap(fields)
        lines = [[GROUP * z + i for z in range(groups)] for i in range(GROUP)]
        stack = [lax.psum(terms[0], "elem", axis_index_groups=lines).astype(BF16)]
    def write(arrays, plan, base=None):
        more = [] if base is None else [base]
        return call(
            functools.partial(spread_body, w, rows, plan, len(arrays), panel),
            struct(bands, 2, panel, dtype=F32),
            [SMEM] + [VMEM] * len(arrays) + [ANY] * len(more),
            (scal, *arrays, *more),
            scratch=[pltpu.VMEM((len(plan), rows, 2, panel), F32), pltpu.SemaphoreType.DMA((len(plan),))],
            out_specs=ANY,
            aliases=None if base is None else {1 + len(arrays): 0},
        )

    everywhere = range(GROUP)
    mine = stack[0][None]
    if direct:
        mine = call(copy_body, struct(1, rows, 2 * panel), [VMEM], (mine,), flops=WEIGHT, moved=WEIGHT // 256)
    near_pieces = swap([mine] * GROUP)
    intersection = write(near_pieces, [(k, 0, k, 0) for k in everywhere])
    if direct:
        far = jnp.stack(stack[2:])
        twin_pieces, far = lax.optimization_barrier((jnp.concatenate(near_pieces), far))
        far_pieces = swap([far] * GROUP)
        twin_pieces = lax.ppermute(twin_pieces, "elem", twins)
        intersection = write([twin_pieces], [(0, k, k, 1) for k in everywhere], intersection)
        plan = [(k, j - 2, k, j) for k in everywhere for j in range(2, split)]
        intersection = write(far_pieces, plan, intersection)
    filtered = call(
        functools.partial(collect_body, w, wp),
        struct(2, nodes, bands),
        [SMEM] + [VMEM] * GROUP,
        (scal, *received),
    )
    return (jnp.moveaxis(filtered, 0, 1), jnp.moveaxis(rotated, 0, 1), intersection)


def solution(mesh):
    placed = (
        P("elem", None, "band"),
        P("elem"),
        P("elem", None, None),
        P("elem", None),
        P(),
        P("elem"),
        P("elem"),
        P(),
    )
    return jax.shard_map(
        on_device,
        mesh=mesh,
        in_specs=placed,
        out_specs=(P("elem", None, "band"), P("elem", None, "band"), P("band", None, None)),
        check_vma=False,
    )
```

```python
import functools

import jax
import jax.numpy as jnp
from jax import lax
from jax.experimental import pallas as pl
from jax.experimental.pallas import tpu as pltpu
from jax.sharding import PartitionSpec as P

FILTER_CENTER = 1.0
FILTER_HALF = 4.0
GROUP = 4
BF16 = jnp.bfloat16
F32 = jnp.float32
SMALL = 16
VMEM_LIMIT = 48 * 1024 * 1024
WEIGHT = 4 * 10**9
VMEM = pl.BlockSpec(memory_space=pltpu.VMEM)
SMEM = pl.BlockSpec(memory_space=pltpu.SMEM)
ANY = pl.BlockSpec(memory_space=pl.ANY)


def up(value, step):
    return -(-value // step) * step


def call(body, out_shape, specs, arrays, scratch=(), flops=0, moved=0, out_specs=None, aliases=None):
    if out_specs is None:
        out_specs = [VMEM] * len(out_shape) if isinstance(out_shape, list) else VMEM
    return pl.pallas_call(
        body,
        out_shape=out_shape,
        in_specs=specs,
        out_specs=out_specs,
        scratch_shapes=list(scratch),
        input_output_aliases=aliases or {},
        compiler_params=pltpu.CompilerParams(vmem_limit_bytes=VMEM_LIMIT),
        cost_estimate=pl.CostEstimate(flops=flops, bytes_accessed=moved, transcendentals=0),
    )(*arrays)


def pieces(value):
    top = value.astype(BF16).astype(F32)
    rest = value - top
    middle = rest.astype(BF16).astype(F32)
    return (top, middle, rest - middle)


def describe_body(count, conn, values, out, small):
    e_cap, elem_nodes = conn.shape
    nodes = (values.shape[1] - 128) // 2
    small[...] = jnp.zeros(small.shape, F32)
    ids = conn[...]
    high = ids >> 7
    small[0:e_cap, 0:elem_nodes] = (ids - (high << 7)).astype(F32)
    small[4 : 4 + e_cap, :] = jnp.full((e_cap, small.shape[1]), 64.0, F32)
    small[4 : 4 + e_cap, 0:elem_nodes] = high.astype(F32)
    lane = lax.broadcasted_iota(jnp.int32, (1, 128), 1)
    coef = jnp.where(lane < jnp.minimum(count[0], e_cap), values[:, 0:128], 0.0)
    for at, part in enumerate(pieces(coef)):
        small[8 + at : 9 + at, 0:128] = part
    for row in (0, 1):
        for at, part in enumerate(pieces(values[:, 128 + row * nodes : 128 + (row + 1) * nodes])):
            small[11 + row : 12 + row, at * nodes : (at + 1) * nodes] = part
    out[...] = small[...].astype(BF16)


def order_body(scal, a0, a1, a2, a3, out):
    for k, part in enumerate((a0, a1, a2, a3)):
        out[scal[0] ^ k] = part[...]


def combine_body(scal, bands, a0, a1, a2, a3, out, small):
    nodes, lanes = bands.shape[1:]
    tile = out.shape[2] - lanes
    out[:, :, 0:lanes] = bands[...]
    for k, part in enumerate((a0, a1, a2, a3)):
        out[scal[0] ^ k, :, lanes:] = part[0:nodes, 0:tile]
        small[scal[0] ^ k] = part[nodes:]


def paired(re, im, size):
    if size == re.shape[1]:
        return jnp.concatenate([re, im], axis=1)
    fill = jnp.zeros((re.shape[0], size - re.shape[1]), re.dtype)
    return jnp.concatenate([re, fill, im, fill], axis=1)


def pack_bands_body(w, wp, scal, vec, *outs):
    for q in range(GROUP):
        bands = paired(vec[0, :, q * w : (q + 1) * w], vec[1, :, q * w : (q + 1) * w], wp)
        for k in range(GROUP):

            @pl.when((scal[0] ^ k) == q)
            def _():
                outs[k][...] = bands


def pack_panel_body(pc, pcp, scal, own, other, small, twin, next_, *outs):
    cols = pc * GROUP
    total = own[...] + other[...]
    nodes = total.shape[0]
    for q in range(GROUP):
        panel = paired(
            total[:, q * pc : (q + 1) * pc], total[:, cols + q * pc : cols + (q + 1) * pc], pcp
        ).astype(BF16)
        for k in range(GROUP):

            @pl.when((scal[0] ^ k) == q)
            def _():
                outs[k][0:nodes, :] = panel

    tile = 2 * pcp
    for k in range(GROUP):
        row = nodes
        for part in (small, twin, next_):
            for at in range(0, part.shape[1], tile):
                outs[k][row : row + SMALL, :] = part[:, at : at + tile]
                row += SMALL


def rotate_body(parts, scal, vec, rot, *out):
    nodes, bands = vec.shape[1:]
    panel = rot.shape[2]
    mine = pl.ds(pl.multiple_of(scal[3] * bands, bands), bands)
    both = jnp.concatenate([vec[0], vec[1]], axis=0)
    with_re = jnp.dot(both, rot[0, mine, :], preferred_element_type=F32)
    with_im = jnp.dot(both, rot[1, mine, :], preferred_element_type=F32)
    out_re = with_re[0:nodes] - with_im[nodes:]
    out_im = with_im[0:nodes] + with_re[nodes:]
    cols = panel // parts
    for h in range(parts):
        value_re = out_re[:, h * cols : (h + 1) * cols]
        value_im = out_im[:, h * cols : (h + 1) * cols]
        if parts == 2:

            @pl.when(scal[3] == h)
            def _():
                out[0][:, 0:cols] = value_re
                out[0][:, cols : 2 * cols] = value_im

            @pl.when(scal[3] != h)
            def _():
                out[1][:, 0:cols] = value_re
                out[1][:, cols : 2 * cols] = value_im

        else:
            out[0][h, :, 0:cols] = value_re
            out[0][h, :, cols : 2 * cols] = value_im


def described(small, p, source, width):
    tile = small.shape[2]
    count = small.shape[1] // (3 * SMALL)
    start = source * count
    parts = [small[p, (start + at) * SMALL : (start + at + 1) * SMALL] for at in range(count)]
    return jnp.concatenate(parts, axis=1)[:, 0:width].astype(F32)


def spread_line(rows, row, nodes):
    line = rows[row : row + 1, 0:nodes] + rows[row : row + 1, nodes : 2 * nodes]
    line = line + rows[row : row + 1, 2 * nodes : 3 * nodes]
    shape = (nodes, nodes)
    diag = lax.broadcasted_iota(jnp.int32, shape, 0) == lax.broadcasted_iota(jnp.int32, shape, 1)
    return jnp.where(diag, line, 0.0), diag


def add_block(t, first, thirds, nodes, e_cap, ids, coefs_s, matrix, acc, base):
    width = matrix.shape[0]
    span = 3 * nodes
    rows = thirds * nodes

    def add(count):
        place = lax.broadcasted_iota(jnp.int32, (span, width), 0).astype(F32)
        marks = [ids[t, e : e + 1, :] for e in range(count)]
        hots = [jnp.where(place == mark, 1.0, 0.0).astype(BF16) for mark in marks]
        if thirds == 3:
            used = hots
        else:
            shift = (first * nodes).astype(F32)
            used = [jnp.where(place[:rows] == mark - shift, 1.0, 0.0).astype(BF16) for mark in marks]
        half = jnp.dot(jnp.concatenate(used, axis=0), matrix[...], preferred_element_type=F32)
        half = [half[e * rows : (e + 1) * rows] * coefs_s[t, e] for e in range(count)]
        tops = [value.astype(BF16) for value in half]
        lows = [(value - part.astype(F32)).astype(BF16) for value, part in zip(half, tops)]
        full = lax.dot_general(
            jnp.concatenate(tops + lows, axis=1),
            jnp.concatenate(hots + hots, axis=1),
            (((1,), (1,)), ((), ())),
            preferred_element_type=F32,
        )
        for j in range(thirds):
            third = first + j
            i = t + third - 3 - base
            at = pl.multiple_of((2 - third) * nodes, nodes)
            acc[i, :, pl.ds(at, span)] += full[j * nodes : (j + 1) * nodes]

    live = jnp.int32(0)
    for e in range(e_cap):
        live = live + (coefs_s[t, e] != 0.0).astype(jnp.int32)
    steps = [n for n in (1, 2, 3) if n < e_cap] + [e_cap]
    for at, count in enumerate(steps):
        least = steps[at - 1] if at else 0

        @pl.when((live > least) & (live <= count))
        def _():
            add(count)


def build_body(nodes, e_cap, scal, side_s, small, matrix, *refs):
    outs = refs[0:GROUP]
    ids, coefs, coefs_s, acc, sem = refs[GROUP:]
    side = side_s[0]
    odd = scal[1] & 1
    base = side * GROUP
    coefs[...] = jnp.zeros(coefs.shape, F32)
    acc[...] = jnp.zeros(acc.shape, F32)
    sources = ((0, 1), (1, 2 - 2 * odd), (2, 2 * odd))
    for source, dz in sources:
        for p in range(GROUP):
            rows = described(small, p, source, matrix.shape[0])
            t = dz * GROUP + p
            ids[t, 0:4, :] = rows[0:4] + 128.0 * rows[4:8]
            coefs[pl.ds(t, 1), :] = (rows[8:9] + rows[9:10] + rows[10:11])[:, 0:128]
    copy = pltpu.make_async_copy(coefs, coefs_s, sem)
    copy.start()
    for source, dz in sources:
        for p in range(GROUP):
            i = dz * GROUP + p - 2 - base

            @pl.when((i >= 0) & (i < GROUP))
            def _():
                rows = described(small, p, source, matrix.shape[0])
                line, diag = spread_line(rows, 11, nodes)
                acc[i, :, 2 * nodes : 3 * nodes] = line - jnp.where(diag, FILTER_CENTER, 0.0)

    copy.wait()
    args = (nodes, e_cap, ids, coefs_s, matrix, acc, base)
    low = side == 0

    def whole(step, carry):
        add_block(GROUP - 1 + side * GROUP + step, 0, 3, *args)
        return carry

    def two(step, carry):
        outer = step == 0
        t = jnp.where(low, jnp.where(outer, 2, 5), jnp.where(outer, 9, 6))
        add_block(t, jnp.where(low == outer, 1, 0), 2, *args)
        return carry

    def one(step, carry):
        outer = step == 0
        t = jnp.where(low, jnp.where(outer, 1, 6), jnp.where(outer, 10, 5))
        add_block(t, jnp.where(low == outer, 2, 0), 1, *args)
        return carry

    lax.fori_loop(0, 2, whole, 0)
    lax.fori_loop(0, 2, two, 0)
    lax.fori_loop(0, 2, one, 0)
    for i in range(GROUP):
        value = acc[i] * (1.0 / FILTER_HALF)
        top = value.astype(BF16)
        outs[i][0] = top
        outs[i][1] = (value - top.astype(F32)).astype(BF16)


def columns_body(scal, small, cols):
    rows_out, nodes = cols.shape[0:2]
    odd = scal[1] & 1
    for source, dz in ((0, 1), (1, 2 - 2 * odd), (2, 2 * odd)):
        for p in range(GROUP):
            i = dz * GROUP + p - 2

            @pl.when((i >= 0) & (i < rows_out))
            def _():
                rows = described(small, p, source, 3 * nodes)
                line, _ = spread_line(rows, 12, nodes)
                column = jnp.sum(line, axis=1, keepdims=True) * (1.0 / FILTER_HALF)
                cols[i] = jnp.broadcast_to(column, cols.shape[1:])


def join_body(scal, own, twin, next_, vec):
    nodes = own.shape[1]
    odd = scal[1] & 1
    for array, dz in ((own, 1), (twin, 2 - 2 * odd), (next_, 2 * odd)):
        for p in range(GROUP):
            t = dz * GROUP + p
            vec[pl.ds(pl.multiple_of(t * nodes, nodes), nodes), :] = array[p]


def filter_body(at, half, scal, side_s, vec, cols, *refs):
    k_one, k_two, refs = refs[:GROUP], refs[GROUP : 2 * GROUP], refs[2 * GROUP :]
    first, keep = refs[-2:]
    outs = refs[:-2]
    rows_out = 2 * GROUP
    nodes = cols.shape[1]
    sign = jnp.where(lax.broadcasted_iota(jnp.int32, (1, 2 * half), 1) < half, 1.0, -1.0)

    def rows_at(block, count):
        return pl.ds(pl.multiple_of(block * nodes, nodes), count * nodes)

    def applied(source, lanes, start, i, rows):
        block = source[rows_at(start, 5), lanes]
        total = jnp.dot(rows[0], block, preferred_element_type=F32)
        total = total + jnp.dot(rows[1], block, preferred_element_type=F32)
        mid = source[rows_at(start + 2, 1), lanes].astype(F32)
        return total + (cols[i][:, 0:1] * sign) * pltpu.roll(mid, half, 1)

    inside_low = scal[1] > 0
    inside_high = scal[1] < scal[2] - 1
    sides = ((k_one, side_s[0]), (k_two, 1 - side_s[0]))
    for parts, side in sides:
        for local in range(GROUP):
            i = side * GROUP + local
            value = applied(vec, slice(at, at + 2 * half), i, i, parts[local])
            kept = ((i >= 2) | inside_low) & ((i < rows_out - 2) | inside_high)
            first[rows_at(i, 1), :] = jnp.where(kept, value, 0.0).astype(BF16)
    for low in (True, False):
        for step in range(GROUP // 2):
            local = GROUP // 2 + step if low else step
            i = step if low else GROUP // 2 + step
            anchor = vec[rows_at(GROUP + i, 1), at : at + 2 * half].astype(F32)
            for parts, side in sides:

                @pl.when((side == 0) == low)
                def _():
                    keep[...] = applied(first, slice(None), i, i + 2, parts[local])

            value = 2.0 * keep[...] - anchor
            if len(outs) == 1:
                outs[0][i] = value.astype(BF16)
                continue
            outs[GROUP][:, rows_at(i, 1)] = jnp.transpose(value).astype(BF16)
            value = value.astype(BF16)
            for k in range(GROUP):

                @pl.when((scal[0] ^ k) == i)
                def _():
                    outs[k][...] = value


def collect_body(w, wp, scal, g0, g1, g2, g3, out):
    mine = scal[0]
    for k, part in enumerate((g0, g1, g2, g3)):
        re = part[:, 0:w]
        im = part[:, wp : wp + w]
        for q in range(GROUP):

            @pl.when((mine ^ k) == q)
            def _():
                out[0, :, q * w : (q + 1) * w] = re
                out[1, :, q * w : (q + 1) * w] = im


def overlap_body(w, wp, pc, pcp, parts, scale, split, scal, left, *refs):
    panels = refs[0 : GROUP * parts]
    outs = refs[GROUP * parts : -3]
    rotated, right, result = refs[-3:]
    mine, band = scal[0], scal[3]
    nodes = panels[0].shape[1]
    tile = 2 * pcp
    chunks = parts * GROUP
    panel = pc * chunks
    for g in range(parts):
        for j in range(GROUP):
            half = (band + g) % parts
            at = pl.multiple_of((half * GROUP + (mine ^ j)) * tile, tile)
            for p in range(GROUP):
                right[p * nodes : (p + 1) * nodes, pl.ds(at, tile)] = panels[g * GROUP + j][p]
    for j in range(GROUP):
        value = panels[j][mine]
        for q in range(GROUP):

            @pl.when((mine ^ j) == q)
            def _():
                rotated[0, :, q * pc : (q + 1) * pc] = value[:, 0:pc]
                rotated[1, :, q * pc : (q + 1) * pc] = value[:, pcp : pcp + pc]

    product = jnp.dot(left[...], right[...], preferred_element_type=F32) * scale
    top, bottom = product[0:w], product[wp : wp + w]
    for s in range(chunks):
        a, b = s * tile, s * tile + pcp
        result[:, s * pc : (s + 1) * pc] = top[:, a : a + pc] - bottom[:, b : b + pc]
        result[:, panel + s * pc : panel + (s + 1) * pc] = top[:, b : b + pc] + bottom[:, a : a + pc]
    if split == 1:
        outs[0][...] = result[...]
    else:
        rows = w // split
        for j in range(split):
            at = pl.multiple_of((scal[1] ^ j) * rows, rows)
            outs[j][...] = result[pl.ds(at, rows), :].astype(BF16)


def sum_body(s0, s1, s2, s3, out):
    total = s0[...].astype(F32) + s1[...].astype(F32)
    total = total + (s2[...].astype(F32) + s3[...].astype(F32))
    out[...] = total.astype(BF16)


def copy_body(given, out):
    out[...] = given[...]


def spread_body(w, rows, plan, count, panel, scal, *refs):
    out, buffer, sems = refs[-3:]
    mine, group = scal[0], scal[1]
    copies = []
    for slot, (array, at, k, j) in enumerate(plan):
        value = refs[array][at].astype(F32)
        buffer[slot, :, 0, :] = value[:, 0:panel]
        buffer[slot, :, 1, :] = value[:, panel : 2 * panel]
        start = (mine ^ k) * w + ((group ^ j) * rows if rows < w else 0)
        copy = pltpu.make_async_copy(buffer.at[slot], out.at[pl.ds(start, rows)], sems.at[slot])
        copy.start()
        copies.append(copy)
    for copy in copies:
        copy.wait()


def on_device(
    orbitals, elem_count, connectivity, elem_coef, elem_matrix, potential, absorber, rotation
):
    nodes, _, bands = orbitals.shape
    blocks = lax.axis_size("elem")
    parts = lax.axis_size("band")
    e_cap, elem_nodes = connectivity.shape[1:]
    panel = rotation.shape[2]
    groups = blocks // GROUP
    w = bands // GROUP
    span = 3 * nodes
    width = up(max(elem_nodes, span), 128)
    wp = max(up(w, 64), width // 2)
    lanes = 2 * wp
    cols = panel // parts
    pc = cols // GROUP
    pcp = up(pc, 64)
    elem = lax.axis_index("elem")
    band = lax.axis_index("band")
    scal = jnp.stack([elem % GROUP, elem // GROUP, jnp.int32(groups), band]).astype(jnp.int32)

    def struct(*shape, dtype=BF16):
        return jax.ShapeDtypeStruct(shape, dtype)

    def in_group(k):
        return [(i, i ^ k) for i in range(blocks)]

    def swap(values):
        return [values[0]] + [lax.ppermute(values[k], "elem", in_group(k)) for k in range(1, GROUP)]

    twins = [(i, i ^ GROUP) for i in range(blocks) if i ^ GROUP < blocks]
    nexts = [(i, i + GROUP) for i in range(blocks - GROUP) if i // GROUP % 2]
    nexts = nexts + [(b, a) for a, b in nexts]

    def neighbours(value):
        return lax.ppermute(value, "elem", twins), lax.ppermute(value, "elem", nexts)

    turn = [(0, 1), (1, 0)]

    values = jnp.concatenate([jnp.pad(elem_coef[0], (0, 128 - e_cap)), potential, absorber])[None]
    small = call(
        describe_body,
        struct(SMALL, width),
        [SMEM, VMEM, VMEM],
        (elem_count, connectivity[0], values),
        scratch=[pltpu.VMEM((SMALL, width), F32)],
    )
    small_near = neighbours(small)
    orbitals, small = lax.optimization_barrier((orbitals, small))
    vec = jnp.moveaxis(orbitals, 1, 0)
    messages = call(
        functools.partial(pack_bands_body, w, wp),
        [struct(nodes, lanes)] * GROUP,
        [SMEM, VMEM],
        (scal, vec),
        moved=4 * nodes * bands * 2,
    )
    messages, rotation, small_near = lax.optimization_barrier((messages, rotation, small_near))
    messages = call(
        order_body, struct(GROUP, nodes, lanes), [SMEM] + [VMEM] * GROUP, (scal, *swap(messages))
    )

    rot = jnp.moveaxis(rotation, 1, 0)
    half = struct(nodes, 2 * cols, dtype=F32)
    sums = call(
        functools.partial(rotate_body, parts),
        [half, half] if parts == 2 else [struct(parts, nodes, 2 * cols, dtype=F32)],
        [SMEM, VMEM, VMEM],
        (scal, vec, rot),
        flops=WEIGHT,
        moved=WEIGHT // 256,
    )
    if parts == 2:
        terms = (sums[0], lax.ppermute(sums[1], "band", turn))
    else:
        whole = lax.psum_scatter(sums[0], "band", scatter_dimension=0, tiled=True)[0]
        terms = (whole, jnp.zeros_like(whole))

    all_lanes = lanes + 2 * pcp
    tall = 3 * SMALL * (up(width, 2 * pcp) // (2 * pcp))
    panels = call(
        functools.partial(pack_panel_body, pc, pcp),
        [struct(nodes + tall, 2 * pcp)] * GROUP,
        [SMEM] + [VMEM] * 5,
        (scal, *terms, small, *small_near),
        moved=8 * nodes * cols,
    )
    messages, small = call(
        combine_body,
        [struct(GROUP, nodes, all_lanes), struct(GROUP, tall, 2 * pcp)],
        [SMEM] + [VMEM] * (1 + GROUP),
        (scal, messages, *swap(panels)),
    )
    near = neighbours(messages)

    matrix = jnp.pad(elem_matrix, ((0, width - elem_nodes), (0, width - elem_nodes)))
    table = (up(3 * GROUP, 8), 128)

    def operator(side):
        return call(
            functools.partial(build_body, nodes, e_cap),
            [struct(2, nodes, 5 * nodes)] * GROUP,
            [SMEM, SMEM, VMEM, VMEM],
            (scal, side, small, matrix),
            scratch=[
                pltpu.VMEM((3 * GROUP, 8, width), F32),
                pltpu.VMEM(table, F32),
                pltpu.SMEM(table, F32),
                pltpu.VMEM((GROUP, nodes, 5 * nodes), F32),
                pltpu.SemaphoreType.DMA,
            ],
            flops=4 * 2 * 6 * width * width * span,
            moved=8 * GROUP * nodes * 5 * nodes,
        )

    if parts == 2:
        side = band[None].astype(jnp.int32)
        halves = [operator(side)]
        halves.append([lax.ppermute(part, "band", turn) for part in halves[0]])
    else:
        side = jnp.zeros((1,), jnp.int32)
        halves = [operator(side), operator(side + 1)]

    absorb = call(
        columns_body, struct(2 * GROUP, nodes, 128, dtype=F32), [SMEM, VMEM], (scal, small)
    )
    vec = call(
        join_body,
        struct(3 * GROUP * nodes, all_lanes),
        [SMEM] + [VMEM] * 3,
        (scal, messages, *near),
    )

    def filtered_lanes(at, size, out_shape):
        return call(
            functools.partial(filter_body, at, size // 2),
            out_shape,
            [SMEM, SMEM] + [VMEM] * (2 + 2 * GROUP),
            (scal, side, vec, absorb, *halves[0], *halves[1]),
            scratch=[pltpu.VMEM((2 * GROUP * nodes, size), BF16), pltpu.VMEM((nodes, size), F32)],
            flops=2 * 2 * 12 * nodes * 5 * nodes * size,
            moved=8 * GROUP * nodes * 5 * nodes,
        )

    out_panel = filtered_lanes(lanes, 2 * pcp, struct(GROUP, nodes, 2 * pcp))
    *fields, left = filtered_lanes(
        0, lanes, [struct(nodes, lanes)] * GROUP + [struct(lanes, GROUP * nodes)]
    )

    gathered = swap([out_panel] * GROUP)
    gathered, left, fields = lax.optimization_barrier((gathered, left, list(fields)))
    if parts == 2:
        all_panels = gathered + [lax.ppermute(x, "band", turn) for x in gathered]
    else:
        every = lax.all_gather(jnp.stack(gathered), "band", axis=0)
        every = jnp.roll(every, -band, axis=0)
        all_panels = [every[h, j] for h in range(parts) for j in range(GROUP)]

    direct = groups == 4 and w % (groups * 16) == 0
    split = groups if direct else 1
    rows = w // split
    *terms, rotated = call(
        functools.partial(
            overlap_body, w, wp, pc, pcp, parts, 1.0 / (nodes * blocks) ** 0.5, split
        ),
        [struct(rows, 2 * panel, dtype=BF16 if direct else F32)] * split + [struct(2, nodes, cols)],
        [SMEM] + [VMEM] * (1 + GROUP * parts),
        (scal, left, *all_panels),
        scratch=[
            pltpu.VMEM((GROUP * nodes, 2 * pcp * GROUP * parts), BF16),
            pltpu.VMEM((w, 2 * panel), F32),
        ],
        flops=2 * GROUP * nodes * lanes * 2 * panel,
        moved=4 * GROUP * nodes * panel,
    )
    if direct:

        def across(values):
            return [values[0]] + [
                lax.ppermute(values[j], "elem", [(i, i ^ (GROUP * j)) for i in range(blocks)])
                for j in range(1, split)
            ]

        moved = across(terms)
        moved[1], fields = lax.optimization_barrier((moved[1], fields))
        received = swap(fields)
        moved[2:], received = lax.optimization_barrier((moved[2:], received))
        own = call(sum_body, struct(rows, 2 * panel), [VMEM] * split, moved)
        stack = [own, None, lax.ppermute(own, "elem", [(i, i ^ (2 * GROUP)) for i in range(blocks)])]
        stack.append(lax.ppermute(stack[2], "elem", twins))
    else:
        received = swap(fields)
        lines = [[GROUP * z + i for z in range(groups)] for i in range(GROUP)]
        stack = [lax.psum(terms[0], "elem", axis_index_groups=lines).astype(BF16)]
    def write(arrays, plan, base=None):
        more = [] if base is None else [base]
        return call(
            functools.partial(spread_body, w, rows, plan, len(arrays), panel),
            struct(bands, 2, panel, dtype=F32),
            [SMEM] + [VMEM] * len(arrays) + [ANY] * len(more),
            (scal, *arrays, *more),
            scratch=[pltpu.VMEM((len(plan), rows, 2, panel), F32), pltpu.SemaphoreType.DMA((len(plan),))],
            out_specs=ANY,
            aliases=None if base is None else {1 + len(arrays): 0},
        )

    everywhere = range(GROUP)
    mine = stack[0][None]
    if direct:
        mine = call(copy_body, struct(1, rows, 2 * panel), [VMEM], (mine,), flops=WEIGHT, moved=WEIGHT // 256)
    near_pieces = swap([mine] * GROUP)
    intersection = write(near_pieces, [(k, 0, k, 0) for k in everywhere])
    if direct:
        far = jnp.stack(stack[2:])
        twin_pieces, far = lax.optimization_barrier((jnp.concatenate(near_pieces), far))
        far_pieces = swap([far] * GROUP)
        twin_pieces = lax.ppermute(twin_pieces, "elem", twins)
        plan = [(0, k, k, 1) for k in everywhere] + [(1, j - 2, 0, j) for j in range(2, split)]
        intersection = write([twin_pieces, far], plan, intersection)
        plan = [(k - 1, j - 2, k, j) for k in range(1, GROUP) for j in range(2, split)]
        intersection = write(far_pieces[1:], plan, intersection)
    filtered = call(
        functools.partial(collect_body, w, wp),
        struct(2, nodes, bands),
        [SMEM] + [VMEM] * GROUP,
        (scal, *received),
    )
    return (jnp.moveaxis(filtered, 0, 1), jnp.moveaxis(rotated, 0, 1), intersection)


def solution(mesh):
    placed = (
        P("elem", None, "band"),
        P("elem"),
        P("elem", None, None),
        P("elem", None),
        P(),
        P("elem"),
        P("elem"),
        P(),
    )
    return jax.shard_map(
        on_device,
        mesh=mesh,
        in_specs=placed,
        out_specs=(P("elem", None, "band"), P("elem", None, "band"), P("band", None, None)),
        check_vma=False,
    )
```

```python
import functools

import jax
import jax.numpy as jnp
from jax import lax
from jax.experimental import pallas as pl
from jax.experimental.pallas import tpu as pltpu
from jax.sharding import PartitionSpec as P

FILTER_CENTER = 1.0
FILTER_HALF = 4.0
GROUP = 4
BF16 = jnp.bfloat16
F32 = jnp.float32
SMALL = 16
VMEM_LIMIT = 48 * 1024 * 1024
WEIGHT = 4 * 10**9
VMEM = pl.BlockSpec(memory_space=pltpu.VMEM)
SMEM = pl.BlockSpec(memory_space=pltpu.SMEM)
ANY = pl.BlockSpec(memory_space=pl.ANY)


def up(value, step):
    return -(-value // step) * step


def call(body, out_shape, specs, arrays, scratch=(), flops=0, moved=0, out_specs=None, aliases=None):
    if out_specs is None:
        out_specs = [VMEM] * len(out_shape) if isinstance(out_shape, list) else VMEM
    return pl.pallas_call(
        body,
        out_shape=out_shape,
        in_specs=specs,
        out_specs=out_specs,
        scratch_shapes=list(scratch),
        input_output_aliases=aliases or {},
        compiler_params=pltpu.CompilerParams(vmem_limit_bytes=VMEM_LIMIT),
        cost_estimate=pl.CostEstimate(flops=flops, bytes_accessed=moved, transcendentals=0),
    )(*arrays)


def pieces(value):
    top = value.astype(BF16).astype(F32)
    rest = value - top
    middle = rest.astype(BF16).astype(F32)
    return (top, middle, rest - middle)


def describe_body(count, conn, values, out, small):
    e_cap, elem_nodes = conn.shape
    nodes = (values.shape[1] - 128) // 2
    small[...] = jnp.zeros(small.shape, F32)
    ids = conn[...]
    high = ids >> 7
    small[0:e_cap, 0:elem_nodes] = (ids - (high << 7)).astype(F32)
    small[4 : 4 + e_cap, :] = jnp.full((e_cap, small.shape[1]), 64.0, F32)
    small[4 : 4 + e_cap, 0:elem_nodes] = high.astype(F32)
    lane = lax.broadcasted_iota(jnp.int32, (1, 128), 1)
    coef = jnp.where(lane < jnp.minimum(count[0], e_cap), values[:, 0:128], 0.0)
    for at, part in enumerate(pieces(coef)):
        small[8 + at : 9 + at, 0:128] = part
    for row in (0, 1):
        for at, part in enumerate(pieces(values[:, 128 + row * nodes : 128 + (row + 1) * nodes])):
            small[11 + row : 12 + row, at * nodes : (at + 1) * nodes] = part
    out[...] = small[...].astype(BF16)


def order_body(scal, a0, a1, a2, a3, out):
    for k, part in enumerate((a0, a1, a2, a3)):
        out[scal[0] ^ k] = part[...]


def combine_body(scal, bands, a0, a1, a2, a3, out, small):
    nodes, lanes = bands.shape[1:]
    tile = out.shape[2] - lanes
    out[:, :, 0:lanes] = bands[...]
    for k, part in enumerate((a0, a1, a2, a3)):
        out[scal[0] ^ k, :, lanes:] = part[0:nodes, 0:tile]
        small[scal[0] ^ k] = part[nodes:]


def paired(re, im, size):
    if size == re.shape[1]:
        return jnp.concatenate([re, im], axis=1)
    fill = jnp.zeros((re.shape[0], size - re.shape[1]), re.dtype)
    return jnp.concatenate([re, fill, im, fill], axis=1)


def pack_bands_body(w, wp, scal, vec, *outs):
    for q in range(GROUP):
        bands = paired(vec[0, :, q * w : (q + 1) * w], vec[1, :, q * w : (q + 1) * w], wp)
        for k in range(GROUP):

            @pl.when((scal[0] ^ k) == q)
            def _():
                outs[k][...] = bands


def pack_panel_body(pc, pcp, scal, own, other, small, twin, next_, *outs):
    cols = pc * GROUP
    total = own[...] + other[...]
    nodes = total.shape[0]
    for q in range(GROUP):
        panel = paired(
            total[:, q * pc : (q + 1) * pc], total[:, cols + q * pc : cols + (q + 1) * pc], pcp
        ).astype(BF16)
        for k in range(GROUP):

            @pl.when((scal[0] ^ k) == q)
            def _():
                outs[k][0:nodes, :] = panel

    tile = 2 * pcp
    for k in range(GROUP):
        row = nodes
        for part in (small, twin, next_):
            for at in range(0, part.shape[1], tile):
                outs[k][row : row + SMALL, :] = part[:, at : at + tile]
                row += SMALL


def rotate_body(parts, scal, vec, rot, *out):
    nodes, bands = vec.shape[1:]
    panel = rot.shape[2]
    mine = pl.ds(pl.multiple_of(scal[3] * bands, bands), bands)
    both = jnp.concatenate([vec[0], vec[1]], axis=0)
    with_re = jnp.dot(both, rot[0, mine, :], preferred_element_type=F32)
    with_im = jnp.dot(both, rot[1, mine, :], preferred_element_type=F32)
    out_re = with_re[0:nodes] - with_im[nodes:]
    out_im = with_im[0:nodes] + with_re[nodes:]
    cols = panel // parts
    for h in range(parts):
        value_re = out_re[:, h * cols : (h + 1) * cols]
        value_im = out_im[:, h * cols : (h + 1) * cols]
        if parts == 2:

            @pl.when(scal[3] == h)
            def _():
                out[0][:, 0:cols] = value_re
                out[0][:, cols : 2 * cols] = value_im

            @pl.when(scal[3] != h)
            def _():
                out[1][:, 0:cols] = value_re
                out[1][:, cols : 2 * cols] = value_im

        else:
            out[0][h, :, 0:cols] = value_re
            out[0][h, :, cols : 2 * cols] = value_im


def described(small, p, source, width):
    tile = small.shape[2]
    count = small.shape[1] // (3 * SMALL)
    start = source * count
    parts = [small[p, (start + at) * SMALL : (start + at + 1) * SMALL] for at in range(count)]
    return jnp.concatenate(parts, axis=1)[:, 0:width].astype(F32)


def spread_line(rows, row, nodes):
    line = rows[row : row + 1, 0:nodes] + rows[row : row + 1, nodes : 2 * nodes]
    line = line + rows[row : row + 1, 2 * nodes : 3 * nodes]
    shape = (nodes, nodes)
    diag = lax.broadcasted_iota(jnp.int32, shape, 0) == lax.broadcasted_iota(jnp.int32, shape, 1)
    return jnp.where(diag, line, 0.0), diag


def add_block(t, first, thirds, nodes, e_cap, ids, coefs_s, matrix, acc, base):
    width = matrix.shape[0]
    span = 3 * nodes
    rows = thirds * nodes

    def add(count):
        place = lax.broadcasted_iota(jnp.int32, (span, width), 0).astype(F32)
        marks = [ids[t, e : e + 1, :] for e in range(count)]
        hots = [jnp.where(place == mark, 1.0, 0.0).astype(BF16) for mark in marks]
        if thirds == 3:
            used = hots
        else:
            shift = (first * nodes).astype(F32)
            used = [jnp.where(place[:rows] == mark - shift, 1.0, 0.0).astype(BF16) for mark in marks]
        half = jnp.dot(jnp.concatenate(used, axis=0), matrix[...], preferred_element_type=F32)
        half = [half[e * rows : (e + 1) * rows] * coefs_s[t, e] for e in range(count)]
        tops = [value.astype(BF16) for value in half]
        lows = [(value - part.astype(F32)).astype(BF16) for value, part in zip(half, tops)]
        full = lax.dot_general(
            jnp.concatenate(tops + lows, axis=1),
            jnp.concatenate(hots + hots, axis=1),
            (((1,), (1,)), ((), ())),
            preferred_element_type=F32,
        )
        for j in range(thirds):
            third = first + j
            i = t + third - 3 - base
            at = pl.multiple_of((2 - third) * nodes, nodes)
            acc[i, :, pl.ds(at, span)] += full[j * nodes : (j + 1) * nodes]

    live = jnp.int32(0)
    for e in range(e_cap):
        live = live + (coefs_s[t, e] != 0.0).astype(jnp.int32)
    steps = [n for n in (1, 2, 3) if n < e_cap] + [e_cap]
    for at, count in enumerate(steps):
        least = steps[at - 1] if at else 0

        @pl.when((live > least) & (live <= count))
        def _():
            add(count)


def build_body(nodes, e_cap, scal, side_s, small, matrix, *refs):
    outs = refs[0:GROUP]
    ids, coefs, coefs_s, acc, sem = refs[GROUP:]
    side = side_s[0]
    odd = scal[1] & 1
    base = side * GROUP
    coefs[...] = jnp.zeros(coefs.shape, F32)
    acc[...] = jnp.zeros(acc.shape, F32)
    sources = ((0, 1), (1, 2 - 2 * odd), (2, 2 * odd))
    for source, dz in sources:
        for p in range(GROUP):
            rows = described(small, p, source, matrix.shape[0])
            t = dz * GROUP + p
            ids[t, 0:4, :] = rows[0:4] + 128.0 * rows[4:8]
            coefs[pl.ds(t, 1), :] = (rows[8:9] + rows[9:10] + rows[10:11])[:, 0:128]
    copy = pltpu.make_async_copy(coefs, coefs_s, sem)
    copy.start()
    for source, dz in sources:
        for p in range(GROUP):
            i = dz * GROUP + p - 2 - base

            @pl.when((i >= 0) & (i < GROUP))
            def _():
                rows = described(small, p, source, matrix.shape[0])
                line, diag = spread_line(rows, 11, nodes)
                acc[i, :, 2 * nodes : 3 * nodes] = line - jnp.where(diag, FILTER_CENTER, 0.0)

    copy.wait()
    args = (nodes, e_cap, ids, coefs_s, matrix, acc, base)
    low = side == 0

    def whole(step, carry):
        add_block(GROUP - 1 + side * GROUP + step, 0, 3, *args)
        return carry

    def two(step, carry):
        outer = step == 0
        t = jnp.where(low, jnp.where(outer, 2, 5), jnp.where(outer, 9, 6))
        add_block(t, jnp.where(low == outer, 1, 0), 2, *args)
        return carry

    def one(step, carry):
        outer = step == 0
        t = jnp.where(low, jnp.where(outer, 1, 6), jnp.where(outer, 10, 5))
        add_block(t, jnp.where(low == outer, 2, 0), 1, *args)
        return carry

    lax.fori_loop(0, 2, whole, 0)
    lax.fori_loop(0, 2, two, 0)
    lax.fori_loop(0, 2, one, 0)
    for i in range(GROUP):
        value = acc[i] * (1.0 / FILTER_HALF)
        top = value.astype(BF16)
        outs[i][:, 0 : 5 * nodes] = top
        outs[i][:, 5 * nodes :] = (value - top.astype(F32)).astype(BF16)


def join_body(scal, own, twin, next_, small, vec, cols):
    nodes = own.shape[1]
    rows_out = cols.shape[0]
    odd = scal[1] & 1
    for source, (array, dz) in enumerate(((own, 1), (twin, 2 - 2 * odd), (next_, 2 * odd))):
        for p in range(GROUP):
            t = dz * GROUP + p
            vec[pl.ds(pl.multiple_of(t * nodes, nodes), nodes), :] = array[p]
            i = t - 2

            @pl.when((i >= 0) & (i < rows_out))
            def _():
                rows = described(small, p, source, 3 * nodes)
                line, _ = spread_line(rows, 12, nodes)
                column = jnp.sum(line, axis=1, keepdims=True) * (1.0 / FILTER_HALF)
                cols[i] = jnp.broadcast_to(column, cols.shape[1:])


def filter_body(at, half, scal, side_s, vec, cols, *refs):
    k_one, k_two, refs = refs[:GROUP], refs[GROUP : 2 * GROUP], refs[2 * GROUP :]
    first, keep = refs[-2:]
    outs = refs[:-2]
    rows_out = 2 * GROUP
    nodes = cols.shape[1]
    sign = jnp.where(lax.broadcasted_iota(jnp.int32, (1, 2 * half), 1) < half, 1.0, -1.0)

    def rows_at(block, count):
        return pl.ds(pl.multiple_of(block * nodes, nodes), count * nodes)

    def applied(source, lanes, start, i, rows):
        block = source[rows_at(start, 5), lanes]
        twice = jnp.concatenate([block, block], axis=0)
        total = jnp.dot(rows[...], twice, preferred_element_type=F32)
        mid = source[rows_at(start + 2, 1), lanes].astype(F32)
        return total + (cols[i][:, 0:1] * sign) * pltpu.roll(mid, half, 1)

    inside_low = scal[1] > 0
    inside_high = scal[1] < scal[2] - 1
    sides = ((k_one, side_s[0]), (k_two, 1 - side_s[0]))
    for parts, side in sides:
        for local in range(GROUP):
            i = side * GROUP + local
            value = applied(vec, slice(at, at + 2 * half), i, i, parts[local])
            kept = ((i >= 2) | inside_low) & ((i < rows_out - 2) | inside_high)
            first[rows_at(i, 1), :] = jnp.where(kept, value, 0.0).astype(BF16)
    for low in (True, False):
        for step in range(GROUP // 2):
            local = GROUP // 2 + step if low else step
            i = step if low else GROUP // 2 + step
            anchor = vec[rows_at(GROUP + i, 1), at : at + 2 * half].astype(F32)
            for parts, side in sides:

                @pl.when((side == 0) == low)
                def _():
                    keep[...] = applied(first, slice(None), i, i + 2, parts[local])

            value = 2.0 * keep[...] - anchor
            if len(outs) == 1:
                outs[0][i] = value.astype(BF16)
                continue
            outs[GROUP][:, rows_at(i, 1)] = jnp.transpose(value).astype(BF16)
            value = value.astype(BF16)
            for k in range(GROUP):

                @pl.when((scal[0] ^ k) == i)
                def _():
                    outs[k][...] = value


def collect_body(w, wp, scal, g0, g1, g2, g3, out):
    mine = scal[0]
    for k, part in enumerate((g0, g1, g2, g3)):
        re = part[:, 0:w]
        im = part[:, wp : wp + w]
        for q in range(GROUP):

            @pl.when((mine ^ k) == q)
            def _():
                out[0, :, q * w : (q + 1) * w] = re
                out[1, :, q * w : (q + 1) * w] = im


def overlap_body(w, wp, pc, pcp, parts, scale, split, scal, left, *refs):
    panels = refs[0 : GROUP * parts]
    outs = refs[GROUP * parts : -3]
    rotated, right, result = refs[-3:]
    mine, band = scal[0], scal[3]
    nodes = panels[0].shape[1]
    tile = 2 * pcp
    chunks = parts * GROUP
    panel = pc * chunks
    for g in range(parts):
        for j in range(GROUP):
            half = (band + g) % parts
            at = pl.multiple_of((half * GROUP + (mine ^ j)) * tile, tile)
            for p in range(GROUP):
                right[p * nodes : (p + 1) * nodes, pl.ds(at, tile)] = panels[g * GROUP + j][p]
    for j in range(GROUP):
        value = panels[j][mine]
        for q in range(GROUP):

            @pl.when((mine ^ j) == q)
            def _():
                rotated[0, :, q * pc : (q + 1) * pc] = value[:, 0:pc]
                rotated[1, :, q * pc : (q + 1) * pc] = value[:, pcp : pcp + pc]

    product = jnp.dot(left[...], right[...], preferred_element_type=F32) * scale
    top, bottom = product[0:w], product[wp : wp + w]
    for s in range(chunks):
        a, b = s * tile, s * tile + pcp
        result[:, s * pc : (s + 1) * pc] = top[:, a : a + pc] - bottom[:, b : b + pc]
        result[:, panel + s * pc : panel + (s + 1) * pc] = top[:, b : b + pc] + bottom[:, a : a + pc]
    if split == 1:
        outs[0][...] = result[...]
    else:
        rows = w // split
        for j in range(split):
            at = pl.multiple_of((scal[1] ^ j) * rows, rows)
            outs[j][...] = result[pl.ds(at, rows), :].astype(BF16)


def sum_body(s0, s1, s2, s3, out):
    total = s0[...].astype(F32) + s1[...].astype(F32)
    total = total + (s2[...].astype(F32) + s3[...].astype(F32))
    out[...] = total.astype(BF16)


def copy_body(given, out):
    out[...] = given[...]


def spread_body(w, rows, plan, count, panel, scal, *refs):
    out, buffer, sems = refs[-3:]
    mine, group = scal[0], scal[1]
    copies = []
    for slot, (array, at, k, j) in enumerate(plan):
        value = refs[array][at].astype(F32)
        buffer[slot, :, 0, :] = value[:, 0:panel]
        buffer[slot, :, 1, :] = value[:, panel : 2 * panel]
        start = (mine ^ k) * w + ((group ^ j) * rows if rows < w else 0)
        copy = pltpu.make_async_copy(buffer.at[slot], out.at[pl.ds(start, rows)], sems.at[slot])
        copy.start()
        copies.append(copy)
    for copy in copies:
        copy.wait()


def on_device(
    orbitals, elem_count, connectivity, elem_coef, elem_matrix, potential, absorber, rotation
):
    nodes, _, bands = orbitals.shape
    blocks = lax.axis_size("elem")
    parts = lax.axis_size("band")
    e_cap, elem_nodes = connectivity.shape[1:]
    panel = rotation.shape[2]
    groups = blocks // GROUP
    w = bands // GROUP
    span = 3 * nodes
    width = up(max(elem_nodes, span), 128)
    wp = max(up(w, 64), width // 2)
    lanes = 2 * wp
    cols = panel // parts
    pc = cols // GROUP
    pcp = up(pc, 64)
    elem = lax.axis_index("elem")
    band = lax.axis_index("band")
    scal = jnp.stack([elem % GROUP, elem // GROUP, jnp.int32(groups), band]).astype(jnp.int32)

    def struct(*shape, dtype=BF16):
        return jax.ShapeDtypeStruct(shape, dtype)

    def in_group(k):
        return [(i, i ^ k) for i in range(blocks)]

    def swap(values):
        return [values[0]] + [lax.ppermute(values[k], "elem", in_group(k)) for k in range(1, GROUP)]

    twins = [(i, i ^ GROUP) for i in range(blocks) if i ^ GROUP < blocks]
    nexts = [(i, i + GROUP) for i in range(blocks - GROUP) if i // GROUP % 2]
    nexts = nexts + [(b, a) for a, b in nexts]

    def neighbours(value):
        return lax.ppermute(value, "elem", twins), lax.ppermute(value, "elem", nexts)

    turn = [(0, 1), (1, 0)]

    values = jnp.concatenate([jnp.pad(elem_coef[0], (0, 128 - e_cap)), potential, absorber])[None]
    small = call(
        describe_body,
        struct(SMALL, width),
        [SMEM, VMEM, VMEM],
        (elem_count, connectivity[0], values),
        scratch=[pltpu.VMEM((SMALL, width), F32)],
    )
    small_near = neighbours(small)
    orbitals, small = lax.optimization_barrier((orbitals, small))
    vec = jnp.moveaxis(orbitals, 1, 0)
    messages = call(
        functools.partial(pack_bands_body, w, wp),
        [struct(nodes, lanes)] * GROUP,
        [SMEM, VMEM],
        (scal, vec),
        moved=4 * nodes * bands * 2,
    )
    messages, rotation, small_near = lax.optimization_barrier((messages, rotation, small_near))
    messages = call(
        order_body, struct(GROUP, nodes, lanes), [SMEM] + [VMEM] * GROUP, (scal, *swap(messages))
    )

    rot = jnp.moveaxis(rotation, 1, 0)
    half = struct(nodes, 2 * cols, dtype=F32)
    sums = call(
        functools.partial(rotate_body, parts),
        [half, half] if parts == 2 else [struct(parts, nodes, 2 * cols, dtype=F32)],
        [SMEM, VMEM, VMEM],
        (scal, vec, rot),
        flops=WEIGHT,
        moved=WEIGHT // 256,
    )
    if parts == 2:
        terms = (sums[0], lax.ppermute(sums[1], "band", turn))
    else:
        whole = lax.psum_scatter(sums[0], "band", scatter_dimension=0, tiled=True)[0]
        terms = (whole, jnp.zeros_like(whole))

    all_lanes = lanes + 2 * pcp
    tall = 3 * SMALL * (up(width, 2 * pcp) // (2 * pcp))
    panels = call(
        functools.partial(pack_panel_body, pc, pcp),
        [struct(nodes + tall, 2 * pcp)] * GROUP,
        [SMEM] + [VMEM] * 5,
        (scal, *terms, small, *small_near),
        moved=8 * nodes * cols,
    )
    messages, small = call(
        combine_body,
        [struct(GROUP, nodes, all_lanes), struct(GROUP, tall, 2 * pcp)],
        [SMEM] + [VMEM] * (1 + GROUP),
        (scal, messages, *swap(panels)),
    )
    near = neighbours(messages)

    matrix = jnp.pad(elem_matrix, ((0, width - elem_nodes), (0, width - elem_nodes)))
    table = (up(3 * GROUP, 8), 128)

    def operator(side):
        return call(
            functools.partial(build_body, nodes, e_cap),
            [struct(nodes, 10 * nodes)] * GROUP,
            [SMEM, SMEM, VMEM, VMEM],
            (scal, side, small, matrix),
            scratch=[
                pltpu.VMEM((3 * GROUP, 8, width), F32),
                pltpu.VMEM(table, F32),
                pltpu.SMEM(table, F32),
                pltpu.VMEM((GROUP, nodes, 5 * nodes), F32),
                pltpu.SemaphoreType.DMA,
            ],
            flops=4 * 2 * 6 * width * width * span,
            moved=8 * GROUP * nodes * 5 * nodes,
        )

    if parts == 2:
        side = band[None].astype(jnp.int32)
        halves = [operator(side)]
        halves.append([lax.ppermute(part, "band", turn) for part in halves[0]])
    else:
        side = jnp.zeros((1,), jnp.int32)
        halves = [operator(side), operator(side + 1)]

    vec, absorb = call(
        join_body,
        [struct(3 * GROUP * nodes, all_lanes), struct(2 * GROUP, nodes, 128, dtype=F32)],
        [SMEM] + [VMEM] * 4,
        (scal, messages, *near, small),
    )

    def filtered_lanes(at, size, out_shape):
        return call(
            functools.partial(filter_body, at, size // 2),
            out_shape,
            [SMEM, SMEM] + [VMEM] * (2 + 2 * GROUP),
            (scal, side, vec, absorb, *halves[0], *halves[1]),
            scratch=[pltpu.VMEM((2 * GROUP * nodes, size), BF16), pltpu.VMEM((nodes, size), F32)],
            flops=2 * 2 * 12 * nodes * 5 * nodes * size,
            moved=8 * GROUP * nodes * 5 * nodes,
        )

    out_panel = filtered_lanes(lanes, 2 * pcp, struct(GROUP, nodes, 2 * pcp))
    *fields, left = filtered_lanes(
        0, lanes, [struct(nodes, lanes)] * GROUP + [struct(lanes, GROUP * nodes)]
    )

    gathered = swap([out_panel] * GROUP)
    gathered, left, fields = lax.optimization_barrier((gathered, left, list(fields)))
    if parts == 2:
        all_panels = gathered + [lax.ppermute(x, "band", turn) for x in gathered]
    else:
        every = lax.all_gather(jnp.stack(gathered), "band", axis=0)
        every = jnp.roll(every, -band, axis=0)
        all_panels = [every[h, j] for h in range(parts) for j in range(GROUP)]

    direct = groups == 4 and w % (groups * 16) == 0
    split = groups if direct else 1
    rows = w // split
    *terms, rotated = call(
        functools.partial(
            overlap_body, w, wp, pc, pcp, parts, 1.0 / (nodes * blocks) ** 0.5, split
        ),
        [struct(rows, 2 * panel, dtype=BF16 if direct else F32)] * split + [struct(2, nodes, cols)],
        [SMEM] + [VMEM] * (1 + GROUP * parts),
        (scal, left, *all_panels),
        scratch=[
            pltpu.VMEM((GROUP * nodes, 2 * pcp * GROUP * parts), BF16),
            pltpu.VMEM((w, 2 * panel), F32),
        ],
        flops=2 * GROUP * nodes * lanes * 2 * panel,
        moved=4 * GROUP * nodes * panel,
    )
    if direct:

        def across(values):
            return [values[0]] + [
                lax.ppermute(values[j], "elem", [(i, i ^ (GROUP * j)) for i in range(blocks)])
                for j in range(1, split)
            ]

        moved = across(terms)
        moved[1], fields = lax.optimization_barrier((moved[1], fields))
        received = swap(fields)
        moved[2:], received = lax.optimization_barrier((moved[2:], received))
        own = call(sum_body, struct(rows, 2 * panel), [VMEM] * split, moved)
        stack = [own, None, lax.ppermute(own, "elem", [(i, i ^ (2 * GROUP)) for i in range(blocks)])]
        stack.append(lax.ppermute(stack[2], "elem", twins))
    else:
        received = swap(fields)
        lines = [[GROUP * z + i for z in range(groups)] for i in range(GROUP)]
        stack = [lax.psum(terms[0], "elem", axis_index_groups=lines).astype(BF16)]
    filtered = call(
        functools.partial(collect_body, w, wp),
        struct(2, nodes, bands),
        [SMEM] + [VMEM] * GROUP,
        (scal, *received),
    )
    filtered, rotated = jnp.moveaxis(filtered, 0, 1), jnp.moveaxis(rotated, 0, 1)

    def write(arrays, plan, base=None):
        more = [] if base is None else [base]
        return call(
            functools.partial(spread_body, w, rows, plan, len(arrays), panel),
            struct(bands, 2, panel, dtype=F32),
            [SMEM] + [VMEM] * len(arrays) + [ANY] * len(more),
            (scal, *arrays, *more),
            scratch=[pltpu.VMEM((len(plan), rows, 2, panel), F32), pltpu.SemaphoreType.DMA((len(plan),))],
            out_specs=ANY,
            aliases=None if base is None else {1 + len(arrays): 0},
        )

    everywhere = range(GROUP)
    mine = stack[0][None]
    if direct:
        mine = call(copy_body, struct(1, rows, 2 * panel), [VMEM], (mine,), flops=WEIGHT, moved=WEIGHT // 256)
    near_pieces = swap([mine] * GROUP)
    intersection = write(near_pieces, [(k, 0, k, 0) for k in everywhere])
    if direct:
        far = jnp.stack(stack[2:])
        twin_pieces, far, filtered, rotated = lax.optimization_barrier(
            (jnp.concatenate(near_pieces), far, filtered, rotated)
        )
        far_pieces = swap([far] * GROUP)
        twin_pieces = lax.ppermute(twin_pieces, "elem", twins)
        plan = [(0, k, k, 1) for k in everywhere] + [(1, j - 2, 0, j) for j in range(2, split)]
        intersection = write([twin_pieces, far], plan, intersection)
        plan = [(k - 1, j - 2, k, j) for k in range(1, GROUP) for j in range(2, split)]
        intersection = write(far_pieces[1:], plan, intersection)
    return (filtered, rotated, intersection)


def solution(mesh):
    placed = (
        P("elem", None, "band"),
        P("elem"),
        P("elem", None, None),
        P("elem", None),
        P(),
        P("elem"),
        P("elem"),
        P(),
    )
    return jax.shard_map(
        on_device,
        mesh=mesh,
        in_specs=placed,
        out_specs=(P("elem", None, "band"), P("elem", None, "band"), P("band", None, None)),
        check_vma=False,
    )
```

```python
import functools

import jax
import jax.numpy as jnp
from jax import lax
from jax.experimental import pallas as pl
from jax.experimental.pallas import tpu as pltpu
from jax.sharding import PartitionSpec as P

FILTER_CENTER = 1.0
FILTER_HALF = 4.0
GROUP = 4
BF16 = jnp.bfloat16
F32 = jnp.float32
SMALL = 16
VMEM_LIMIT = 48 * 1024 * 1024
WEIGHT = 4 * 10**9
VMEM = pl.BlockSpec(memory_space=pltpu.VMEM)
SMEM = pl.BlockSpec(memory_space=pltpu.SMEM)
ANY = pl.BlockSpec(memory_space=pl.ANY)


def up(value, step):
    return -(-value // step) * step


def call(body, out_shape, specs, arrays, scratch=(), flops=0, moved=0, out_specs=None, aliases=None):
    if out_specs is None:
        out_specs = [VMEM] * len(out_shape) if isinstance(out_shape, list) else VMEM
    return pl.pallas_call(
        body,
        out_shape=out_shape,
        in_specs=specs,
        out_specs=out_specs,
        scratch_shapes=list(scratch),
        input_output_aliases=aliases or {},
        compiler_params=pltpu.CompilerParams(vmem_limit_bytes=VMEM_LIMIT),
        cost_estimate=pl.CostEstimate(flops=flops, bytes_accessed=moved, transcendentals=0),
    )(*arrays)


def pieces(value):
    top = value.astype(BF16).astype(F32)
    rest = value - top
    middle = rest.astype(BF16).astype(F32)
    return (top, middle, rest - middle)


def describe_body(count, conn, values, out, small):
    e_cap, elem_nodes = conn.shape
    nodes = (values.shape[1] - 128) // 2
    small[...] = jnp.zeros(small.shape, F32)
    ids = conn[...]
    high = ids >> 7
    small[0:e_cap, 0:elem_nodes] = (ids - (high << 7)).astype(F32)
    small[4 : 4 + e_cap, :] = jnp.full((e_cap, small.shape[1]), 64.0, F32)
    small[4 : 4 + e_cap, 0:elem_nodes] = high.astype(F32)
    lane = lax.broadcasted_iota(jnp.int32, (1, 128), 1)
    coef = jnp.where(lane < jnp.minimum(count[0], e_cap), values[:, 0:128], 0.0)
    for at, part in enumerate(pieces(coef)):
        small[8 + at : 9 + at, 0:128] = part
    for row in (0, 1):
        for at, part in enumerate(pieces(values[:, 128 + row * nodes : 128 + (row + 1) * nodes])):
            small[11 + row : 12 + row, at * nodes : (at + 1) * nodes] = part
    out[...] = small[...].astype(BF16)


def order_body(scal, a0, a1, a2, a3, out):
    for k, part in enumerate((a0, a1, a2, a3)):
        out[scal[0] ^ k] = part[...]


def combine_body(scal, bands, a0, a1, a2, a3, out, small):
    nodes, lanes = bands.shape[1:]
    tile = out.shape[2] - lanes
    out[:, :, 0:lanes] = bands[...]
    for k, part in enumerate((a0, a1, a2, a3)):
        out[scal[0] ^ k, :, lanes:] = part[0:nodes, 0:tile]
        small[scal[0] ^ k] = part[nodes:]


def paired(re, im, size):
    if size == re.shape[1]:
        return jnp.concatenate([re, im], axis=1)
    fill = jnp.zeros((re.shape[0], size - re.shape[1]), re.dtype)
    return jnp.concatenate([re, fill, im, fill], axis=1)


def pack_bands_body(w, wp, scal, vec, *outs):
    for q in range(GROUP):
        bands = paired(vec[0, :, q * w : (q + 1) * w], vec[1, :, q * w : (q + 1) * w], wp)
        for k in range(GROUP):

            @pl.when((scal[0] ^ k) == q)
            def _():
                outs[k][...] = bands


def pack_panel_body(pc, pcp, scal, own, other, small, twin, next_, *outs):
    cols = pc * GROUP
    total = own[...] + other[...]
    nodes = total.shape[0]
    for q in range(GROUP):
        panel = paired(
            total[:, q * pc : (q + 1) * pc], total[:, cols + q * pc : cols + (q + 1) * pc], pcp
        ).astype(BF16)
        for k in range(GROUP):

            @pl.when((scal[0] ^ k) == q)
            def _():
                outs[k][0:nodes, :] = panel

    tile = 2 * pcp
    for k in range(GROUP):
        row = nodes
        for part in (small, twin, next_):
            for at in range(0, part.shape[1], tile):
                outs[k][row : row + SMALL, :] = part[:, at : at + tile]
                row += SMALL


def rotate_body(parts, scal, vec, rot, *out):
    nodes, bands = vec.shape[1:]
    panel = rot.shape[2]
    mine = pl.ds(pl.multiple_of(scal[3] * bands, bands), bands)
    both = jnp.concatenate([vec[0], vec[1]], axis=0)
    with_re = jnp.dot(both, rot[0, mine, :], preferred_element_type=F32)
    with_im = jnp.dot(both, rot[1, mine, :], preferred_element_type=F32)
    out_re = with_re[0:nodes] - with_im[nodes:]
    out_im = with_im[0:nodes] + with_re[nodes:]
    cols = panel // parts
    for h in range(parts):
        value_re = out_re[:, h * cols : (h + 1) * cols]
        value_im = out_im[:, h * cols : (h + 1) * cols]
        if parts == 2:

            @pl.when(scal[3] == h)
            def _():
                out[0][:, 0:cols] = value_re
                out[0][:, cols : 2 * cols] = value_im

            @pl.when(scal[3] != h)
            def _():
                out[1][:, 0:cols] = value_re
                out[1][:, cols : 2 * cols] = value_im

        else:
            out[0][h, :, 0:cols] = value_re
            out[0][h, :, cols : 2 * cols] = value_im


def described(small, p, source, width):
    tile = small.shape[2]
    count = small.shape[1] // (3 * SMALL)
    start = source * count
    parts = [small[p, (start + at) * SMALL : (start + at + 1) * SMALL] for at in range(count)]
    return jnp.concatenate(parts, axis=1)[:, 0:width].astype(F32)


def spread_line(rows, row, nodes):
    line = rows[row : row + 1, 0:nodes] + rows[row : row + 1, nodes : 2 * nodes]
    line = line + rows[row : row + 1, 2 * nodes : 3 * nodes]
    shape = (nodes, nodes)
    diag = lax.broadcasted_iota(jnp.int32, shape, 0) == lax.broadcasted_iota(jnp.int32, shape, 1)
    return jnp.where(diag, line, 0.0), diag


def add_block(t, first, thirds, nodes, e_cap, ids, coefs_s, matrix, acc, base):
    width = matrix.shape[0]
    span = 3 * nodes
    rows = thirds * nodes

    def add(count):
        place = lax.broadcasted_iota(jnp.int32, (span, width), 0).astype(F32)
        marks = [ids[t, e : e + 1, :] for e in range(count)]
        hots = [jnp.where(place == mark, 1.0, 0.0).astype(BF16) for mark in marks]
        if thirds == 3:
            used = hots
        else:
            shift = (first * nodes).astype(F32)
            used = [jnp.where(place[:rows] == mark - shift, 1.0, 0.0).astype(BF16) for mark in marks]
        half = jnp.dot(jnp.concatenate(used, axis=0), matrix[...], preferred_element_type=F32)
        half = [half[e * rows : (e + 1) * rows] * coefs_s[t, e] for e in range(count)]
        tops = [value.astype(BF16) for value in half]
        lows = [(value - part.astype(F32)).astype(BF16) for value, part in zip(half, tops)]
        full = lax.dot_general(
            jnp.concatenate(tops + lows, axis=1),
            jnp.concatenate(hots + hots, axis=1),
            (((1,), (1,)), ((), ())),
            preferred_element_type=F32,
        )
        for j in range(thirds):
            third = first + j
            i = t + third - 3 - base
            at = pl.multiple_of((2 - third) * nodes, nodes)
            acc[i, :, pl.ds(at, span)] += full[j * nodes : (j + 1) * nodes]

    live = jnp.int32(0)
    for e in range(e_cap):
        live = live + (coefs_s[t, e] != 0.0).astype(jnp.int32)
    steps = [n for n in (1, 2, 3) if n < e_cap] + [e_cap]
    for at, count in enumerate(steps):
        least = steps[at - 1] if at else 0

        @pl.when((live > least) & (live <= count))
        def _():
            add(count)


def build_body(nodes, e_cap, scal, side_s, small, matrix, *refs):
    outs = refs[0:GROUP]
    ids, coefs, coefs_s, acc, sem = refs[GROUP:]
    side = side_s[0]
    odd = scal[1] & 1
    base = side * GROUP
    coefs[...] = jnp.zeros(coefs.shape, F32)
    acc[...] = jnp.zeros(acc.shape, F32)
    sources = ((0, 1), (1, 2 - 2 * odd), (2, 2 * odd))
    for source, dz in sources:
        for p in range(GROUP):
            rows = described(small, p, source, matrix.shape[0])
            t = dz * GROUP + p
            ids[t, 0:4, :] = rows[0:4] + 128.0 * rows[4:8]
            coefs[pl.ds(t, 1), :] = (rows[8:9] + rows[9:10] + rows[10:11])[:, 0:128]
    copy = pltpu.make_async_copy(coefs, coefs_s, sem)
    copy.start()
    for source, dz in sources:
        for p in range(GROUP):
            i = dz * GROUP + p - 2 - base

            @pl.when((i >= 0) & (i < GROUP))
            def _():
                rows = described(small, p, source, matrix.shape[0])
                line, diag = spread_line(rows, 11, nodes)
                acc[i, :, 2 * nodes : 3 * nodes] = line - jnp.where(diag, FILTER_CENTER, 0.0)

    copy.wait()
    args = (nodes, e_cap, ids, coefs_s, matrix, acc, base)
    low = side == 0

    def whole(step, carry):
        add_block(GROUP - 1 + side * GROUP + step, 0, 3, *args)
        return carry

    def two(step, carry):
        outer = step == 0
        t = jnp.where(low, jnp.where(outer, 2, 5), jnp.where(outer, 9, 6))
        add_block(t, jnp.where(low == outer, 1, 0), 2, *args)
        return carry

    def one(step, carry):
        outer = step == 0
        t = jnp.where(low, jnp.where(outer, 1, 6), jnp.where(outer, 10, 5))
        add_block(t, jnp.where(low == outer, 2, 0), 1, *args)
        return carry

    lax.fori_loop(0, 2, whole, 0)
    lax.fori_loop(0, 2, two, 0)
    lax.fori_loop(0, 2, one, 0)
    for i in range(GROUP):
        value = acc[i] * (1.0 / FILTER_HALF)
        top = value.astype(BF16)
        outs[i][:, 0 : 5 * nodes] = top
        outs[i][:, 5 * nodes :] = (value - top.astype(F32)).astype(BF16)


def join_body(scal, own, twin, next_, small, vec, cols):
    nodes = own.shape[1]
    rows_out = cols.shape[0]
    odd = scal[1] & 1
    for source, (array, dz) in enumerate(((own, 1), (twin, 2 - 2 * odd), (next_, 2 * odd))):
        for p in range(GROUP):
            t = dz * GROUP + p
            vec[pl.ds(pl.multiple_of(t * nodes, nodes), nodes), :] = array[p]
            i = t - 2

            @pl.when((i >= 0) & (i < rows_out))
            def _():
                rows = described(small, p, source, 3 * nodes)
                line, _ = spread_line(rows, 12, nodes)
                column = jnp.sum(line, axis=1, keepdims=True) * (1.0 / FILTER_HALF)
                cols[i] = jnp.broadcast_to(column, cols.shape[1:])


def filter_body(at, half, scal, side_s, vec, cols, *refs):
    k_one, k_two, refs = refs[:GROUP], refs[GROUP : 2 * GROUP], refs[2 * GROUP :]
    first, keep = refs[-2:]
    outs = refs[:-2]
    rows_out = 2 * GROUP
    nodes = cols.shape[1]
    sign = jnp.where(lax.broadcasted_iota(jnp.int32, (1, 2 * half), 1) < half, 1.0, -1.0)

    def rows_at(block, count):
        return pl.ds(pl.multiple_of(block * nodes, nodes), count * nodes)

    def applied(source, lanes, start, i, rows):
        block = source[rows_at(start, 5), lanes]
        twice = jnp.concatenate([block, block], axis=0)
        total = jnp.dot(rows[...], twice, preferred_element_type=F32)
        mid = source[rows_at(start + 2, 1), lanes].astype(F32)
        return total + (cols[i][:, 0:1] * sign) * pltpu.roll(mid, half, 1)

    inside_low = scal[1] > 0
    inside_high = scal[1] < scal[2] - 1
    sides = ((k_one, side_s[0]), (k_two, 1 - side_s[0]))
    for parts, side in sides:
        for local in range(GROUP):
            i = side * GROUP + local
            value = applied(vec, slice(at, at + 2 * half), i, i, parts[local])
            kept = ((i >= 2) | inside_low) & ((i < rows_out - 2) | inside_high)
            first[rows_at(i, 1), :] = jnp.where(kept, value, 0.0).astype(BF16)
    for low in (True, False):
        for step in range(GROUP // 2):
            local = GROUP // 2 + step if low else step
            i = step if low else GROUP // 2 + step
            anchor = vec[rows_at(GROUP + i, 1), at : at + 2 * half].astype(F32)
            for parts, side in sides:

                @pl.when((side == 0) == low)
                def _():
                    keep[...] = applied(first, slice(None), i, i + 2, parts[local])

            value = 2.0 * keep[...] - anchor
            if len(outs) == 1:
                outs[0][i] = value.astype(BF16)
                continue
            outs[GROUP][:, rows_at(i, 1)] = jnp.transpose(value).astype(BF16)
            value = value.astype(BF16)
            for k in range(GROUP):

                @pl.when((scal[0] ^ k) == i)
                def _():
                    outs[k][...] = value


def collect_body(w, wp, scal, g0, g1, g2, g3, out):
    mine = scal[0]
    for k, part in enumerate((g0, g1, g2, g3)):
        re = part[:, 0:w]
        im = part[:, wp : wp + w]
        for q in range(GROUP):

            @pl.when((mine ^ k) == q)
            def _():
                out[0, :, q * w : (q + 1) * w] = re
                out[1, :, q * w : (q + 1) * w] = im


def overlap_body(w, wp, pc, pcp, parts, scale, split, scal, left, *refs):
    panels = refs[0 : GROUP * parts]
    outs = refs[GROUP * parts : -3]
    rotated, right, result = refs[-3:]
    mine, band = scal[0], scal[3]
    nodes = panels[0].shape[1]
    tile = 2 * pcp
    chunks = parts * GROUP
    panel = pc * chunks
    for g in range(parts):
        for j in range(GROUP):
            half = (band + g) % parts
            at = pl.multiple_of((half * GROUP + (mine ^ j)) * tile, tile)
            for p in range(GROUP):
                right[p * nodes : (p + 1) * nodes, pl.ds(at, tile)] = panels[g * GROUP + j][p]
    for j in range(GROUP):
        value = panels[j][mine]
        for q in range(GROUP):

            @pl.when((mine ^ j) == q)
            def _():
                rotated[0, :, q * pc : (q + 1) * pc] = value[:, 0:pc]
                rotated[1, :, q * pc : (q + 1) * pc] = value[:, pcp : pcp + pc]

    product = jnp.dot(left[...], right[...], preferred_element_type=F32) * scale
    top, bottom = product[0:w], product[wp : wp + w]
    for s in range(chunks):
        a, b = s * tile, s * tile + pcp
        result[:, s * pc : (s + 1) * pc] = top[:, a : a + pc] - bottom[:, b : b + pc]
        result[:, panel + s * pc : panel + (s + 1) * pc] = top[:, b : b + pc] + bottom[:, a : a + pc]
    if split == 1:
        outs[0][...] = result[...]
    else:
        rows = w // split
        for j in range(split):
            at = pl.multiple_of((scal[1] ^ j) * rows, rows)
            outs[j][...] = result[pl.ds(at, rows), :].astype(BF16)


def sum_body(s0, s1, s2, s3, out):
    total = s0[...].astype(F32) + s1[...].astype(F32)
    total = total + (s2[...].astype(F32) + s3[...].astype(F32))
    out[...] = total.astype(BF16)


def copy_body(given, out):
    out[...] = given[...]


def spread_body(w, rows, plan, count, panel, scal, *refs):
    out, buffer, sems = refs[-3:]
    mine, group = scal[0], scal[1]
    copies = []
    for slot, (array, at, k, j) in enumerate(plan):
        value = refs[array][at].astype(F32)
        buffer[slot, :, 0, :] = value[:, 0:panel]
        buffer[slot, :, 1, :] = value[:, panel : 2 * panel]
        start = (mine ^ k) * w + ((group ^ j) * rows if rows < w else 0)
        copy = pltpu.make_async_copy(buffer.at[slot], out.at[pl.ds(start, rows)], sems.at[slot])
        copy.start()
        copies.append(copy)
    for copy in copies:
        copy.wait()


def on_device(
    orbitals, elem_count, connectivity, elem_coef, elem_matrix, potential, absorber, rotation
):
    nodes, _, bands = orbitals.shape
    blocks = lax.axis_size("elem")
    parts = lax.axis_size("band")
    e_cap, elem_nodes = connectivity.shape[1:]
    panel = rotation.shape[2]
    groups = blocks // GROUP
    w = bands // GROUP
    span = 3 * nodes
    width = up(max(elem_nodes, span), 128)
    wp = max(up(w, 64), width // 2)
    lanes = 2 * wp
    cols = panel // parts
    pc = cols // GROUP
    pcp = up(pc, 64)
    elem = lax.axis_index("elem")
    band = lax.axis_index("band")
    scal = jnp.stack([elem % GROUP, elem // GROUP, jnp.int32(groups), band]).astype(jnp.int32)

    def struct(*shape, dtype=BF16):
        return jax.ShapeDtypeStruct(shape, dtype)

    def in_group(k):
        return [(i, i ^ k) for i in range(blocks)]

    def swap(values):
        return [values[0]] + [lax.ppermute(values[k], "elem", in_group(k)) for k in range(1, GROUP)]

    twins = [(i, i ^ GROUP) for i in range(blocks) if i ^ GROUP < blocks]
    nexts = [(i, i + GROUP) for i in range(blocks - GROUP) if i // GROUP % 2]
    nexts = nexts + [(b, a) for a, b in nexts]

    def neighbours(value):
        return lax.ppermute(value, "elem", twins), lax.ppermute(value, "elem", nexts)

    turn = [(0, 1), (1, 0)]

    values = jnp.concatenate([jnp.pad(elem_coef[0], (0, 128 - e_cap)), potential, absorber])[None]
    small = call(
        describe_body,
        struct(SMALL, width),
        [SMEM, VMEM, VMEM],
        (elem_count, connectivity[0], values),
        scratch=[pltpu.VMEM((SMALL, width), F32)],
    )
    small_near = neighbours(small)
    orbitals, small = lax.optimization_barrier((orbitals, small))
    vec = jnp.moveaxis(orbitals, 1, 0)
    messages = call(
        functools.partial(pack_bands_body, w, wp),
        [struct(nodes, lanes)] * GROUP,
        [SMEM, VMEM],
        (scal, vec),
        moved=4 * nodes * bands * 2,
    )
    messages, rotation, small_near = lax.optimization_barrier((messages, rotation, small_near))
    messages = call(
        order_body, struct(GROUP, nodes, lanes), [SMEM] + [VMEM] * GROUP, (scal, *swap(messages))
    )

    rot = jnp.moveaxis(rotation, 1, 0)
    half = struct(nodes, 2 * cols, dtype=F32)
    sums = call(
        functools.partial(rotate_body, parts),
        [half, half] if parts == 2 else [struct(parts, nodes, 2 * cols, dtype=F32)],
        [SMEM, VMEM, VMEM],
        (scal, vec, rot),
        flops=WEIGHT,
        moved=WEIGHT // 256,
    )
    if parts == 2:
        terms = (sums[0], lax.ppermute(sums[1], "band", turn))
    else:
        whole = lax.psum_scatter(sums[0], "band", scatter_dimension=0, tiled=True)[0]
        terms = (whole, jnp.zeros_like(whole))

    all_lanes = lanes + 2 * pcp
    tall = 3 * SMALL * (up(width, 2 * pcp) // (2 * pcp))
    panels = call(
        functools.partial(pack_panel_body, pc, pcp),
        [struct(nodes + tall, 2 * pcp)] * GROUP,
        [SMEM] + [VMEM] * 5,
        (scal, *terms, small, *small_near),
        moved=8 * nodes * cols,
    )
    messages, small = call(
        combine_body,
        [struct(GROUP, nodes, all_lanes), struct(GROUP, tall, 2 * pcp)],
        [SMEM] + [VMEM] * (1 + GROUP),
        (scal, messages, *swap(panels)),
    )
    near = neighbours(messages)

    matrix = jnp.pad(elem_matrix, ((0, width - elem_nodes), (0, width - elem_nodes)))
    table = (up(3 * GROUP, 8), 128)

    def operator(side):
        return call(
            functools.partial(build_body, nodes, e_cap),
            [struct(nodes, 10 * nodes)] * GROUP,
            [SMEM, SMEM, VMEM, VMEM],
            (scal, side, small, matrix),
            scratch=[
                pltpu.VMEM((3 * GROUP, 8, width), F32),
                pltpu.VMEM(table, F32),
                pltpu.SMEM(table, F32),
                pltpu.VMEM((GROUP, nodes, 5 * nodes), F32),
                pltpu.SemaphoreType.DMA,
            ],
            flops=4 * 2 * 6 * width * width * span,
            moved=8 * GROUP * nodes * 5 * nodes,
        )

    if parts == 2:
        side = band[None].astype(jnp.int32)
        halves = [operator(side)]
        halves.append([lax.ppermute(part, "band", turn) for part in halves[0]])
    else:
        side = jnp.zeros((1,), jnp.int32)
        halves = [operator(side), operator(side + 1)]

    vec, absorb = call(
        join_body,
        [struct(3 * GROUP * nodes, all_lanes), struct(2 * GROUP, nodes, 128, dtype=F32)],
        [SMEM] + [VMEM] * 4,
        (scal, messages, *near, small),
    )

    def filtered_lanes(at, size, out_shape):
        return call(
            functools.partial(filter_body, at, size // 2),
            out_shape,
            [SMEM, SMEM] + [VMEM] * (2 + 2 * GROUP),
            (scal, side, vec, absorb, *halves[0], *halves[1]),
            scratch=[pltpu.VMEM((2 * GROUP * nodes, size), BF16), pltpu.VMEM((nodes, size), F32)],
            flops=2 * 2 * 12 * nodes * 5 * nodes * size,
            moved=8 * GROUP * nodes * 5 * nodes,
        )

    out_panel = filtered_lanes(lanes, 2 * pcp, struct(GROUP, nodes, 2 * pcp))
    *fields, left = filtered_lanes(
        0, lanes, [struct(nodes, lanes)] * GROUP + [struct(lanes, GROUP * nodes)]
    )

    gathered = swap([out_panel] * GROUP)
    gathered, left, fields = lax.optimization_barrier((gathered, left, list(fields)))
    if parts == 2:
        all_panels = gathered + [lax.ppermute(x, "band", turn) for x in gathered]
    else:
        every = lax.all_gather(jnp.stack(gathered), "band", axis=0)
        every = jnp.roll(every, -band, axis=0)
        all_panels = [every[h, j] for h in range(parts) for j in range(GROUP)]

    direct = groups == 4 and w % (groups * 16) == 0
    split = groups if direct else 1
    rows = w // split
    *terms, rotated = call(
        functools.partial(
            overlap_body, w, wp, pc, pcp, parts, 1.0 / (nodes * blocks) ** 0.5, split
        ),
        [struct(rows, 2 * panel, dtype=BF16 if direct else F32)] * split + [struct(2, nodes, cols)],
        [SMEM] + [VMEM] * (1 + GROUP * parts),
        (scal, left, *all_panels),
        scratch=[
            pltpu.VMEM((GROUP * nodes, 2 * pcp * GROUP * parts), BF16),
            pltpu.VMEM((w, 2 * panel), F32),
        ],
        flops=2 * GROUP * nodes * lanes * 2 * panel,
        moved=4 * GROUP * nodes * panel,
    )
    if direct:

        def across(values):
            return [values[0]] + [
                lax.ppermute(values[j], "elem", [(i, i ^ (GROUP * j)) for i in range(blocks)])
                for j in range(1, split)
            ]

        moved = across(terms)
        moved[1], fields = lax.optimization_barrier((moved[1], fields))
        received = swap(fields)
        moved[2:], received = lax.optimization_barrier((moved[2:], received))
        own = call(sum_body, struct(rows, 2 * panel), [VMEM] * split, moved)
        stack = [own, None, lax.ppermute(own, "elem", [(i, i ^ (2 * GROUP)) for i in range(blocks)])]
        stack.append(lax.ppermute(stack[2], "elem", twins))
    else:
        received = swap(fields)
        lines = [[GROUP * z + i for z in range(groups)] for i in range(GROUP)]
        stack = [lax.psum(terms[0], "elem", axis_index_groups=lines).astype(BF16)]
    filtered = call(
        functools.partial(collect_body, w, wp),
        struct(2, nodes, bands),
        [SMEM] + [VMEM] * GROUP,
        (scal, *received),
    )
    filtered, rotated = jnp.moveaxis(filtered, 0, 1), jnp.moveaxis(rotated, 0, 1)

    def write(arrays, plan, base=None):
        more = [] if base is None else [base]
        return call(
            functools.partial(spread_body, w, rows, plan, len(arrays), panel),
            struct(bands, 2, panel, dtype=F32),
            [SMEM] + [VMEM] * len(arrays) + [ANY] * len(more),
            (scal, *arrays, *more),
            scratch=[pltpu.VMEM((len(plan), rows, 2, panel), F32), pltpu.SemaphoreType.DMA((len(plan),))],
            out_specs=ANY,
            aliases=None if base is None else {1 + len(arrays): 0},
        )

    everywhere = range(GROUP)
    mine = stack[0][None]
    if direct:
        mine = call(copy_body, struct(1, rows, 2 * panel), [VMEM], (mine,), flops=WEIGHT, moved=WEIGHT // 256)
    near_pieces = swap([mine] * GROUP)
    intersection = write(near_pieces, [(k, 0, k, 0) for k in everywhere])
    if direct:
        far = jnp.stack(stack[2:])
        twin_pieces = jnp.concatenate(near_pieces)
        _, far, filtered, rotated = lax.optimization_barrier((twin_pieces, far, filtered, rotated))
        far_pieces = swap([far] * GROUP)
        twin_pieces = lax.ppermute(twin_pieces, "elem", twins)
        plan = [(0, k, k, 1) for k in everywhere] + [(1, j - 2, 0, j) for j in range(2, split)]
        intersection = write([twin_pieces, far], plan, intersection)
        plan = [(k - 1, j - 2, k, j) for k in range(1, GROUP) for j in range(2, split)]
        intersection = write(far_pieces[1:], plan, intersection)
    return (filtered, rotated, intersection)


def solution(mesh):
    placed = (
        P("elem", None, "band"),
        P("elem"),
        P("elem", None, None),
        P("elem", None),
        P(),
        P("elem"),
        P("elem"),
        P(),
    )
    return jax.shard_map(
        on_device,
        mesh=mesh,
        in_specs=placed,
        out_specs=(P("elem", None, "band"), P("elem", None, "band"), P("band", None, None)),
        check_vma=False,
    )
```

```python
import functools

import jax
import jax.numpy as jnp
from jax import lax
from jax.experimental import pallas as pl
from jax.experimental.pallas import tpu as pltpu
from jax.sharding import PartitionSpec as P

FILTER_CENTER = 1.0
FILTER_HALF = 4.0
GROUP = 4
BF16 = jnp.bfloat16
F32 = jnp.float32
SMALL = 16
VMEM_LIMIT = 48 * 1024 * 1024
WEIGHT = 4 * 10**9
VMEM = pl.BlockSpec(memory_space=pltpu.VMEM)
SMEM = pl.BlockSpec(memory_space=pltpu.SMEM)
ANY = pl.BlockSpec(memory_space=pl.ANY)


def up(value, step):
    return -(-value // step) * step


def call(body, out_shape, specs, arrays, scratch=(), flops=0, moved=0, out_specs=None, aliases=None):
    if out_specs is None:
        out_specs = [VMEM] * len(out_shape) if isinstance(out_shape, list) else VMEM
    return pl.pallas_call(
        body,
        out_shape=out_shape,
        in_specs=specs,
        out_specs=out_specs,
        scratch_shapes=list(scratch),
        input_output_aliases=aliases or {},
        compiler_params=pltpu.CompilerParams(vmem_limit_bytes=VMEM_LIMIT),
        cost_estimate=pl.CostEstimate(flops=flops, bytes_accessed=moved, transcendentals=0),
    )(*arrays)


def pieces(value):
    top = value.astype(BF16).astype(F32)
    rest = value - top
    middle = rest.astype(BF16).astype(F32)
    return (top, middle, rest - middle)


def describe_body(count, conn, values, out, small):
    e_cap, elem_nodes = conn.shape
    nodes = (values.shape[1] - 128) // 2
    small[...] = jnp.zeros(small.shape, F32)
    ids = conn[...]
    high = ids >> 7
    small[0:e_cap, 0:elem_nodes] = (ids - (high << 7)).astype(F32)
    small[4 : 4 + e_cap, :] = jnp.full((e_cap, small.shape[1]), 64.0, F32)
    small[4 : 4 + e_cap, 0:elem_nodes] = high.astype(F32)
    lane = lax.broadcasted_iota(jnp.int32, (1, 128), 1)
    coef = jnp.where(lane < jnp.minimum(count[0], e_cap), values[:, 0:128], 0.0)
    for at, part in enumerate(pieces(coef)):
        small[8 + at : 9 + at, 0:128] = part
    for row in (0, 1):
        for at, part in enumerate(pieces(values[:, 128 + row * nodes : 128 + (row + 1) * nodes])):
            small[11 + row : 12 + row, at * nodes : (at + 1) * nodes] = part
    out[...] = small[...].astype(BF16)


def order_body(scal, a0, a1, a2, a3, out):
    for k, part in enumerate((a0, a1, a2, a3)):
        out[scal[0] ^ k] = part[...]


def combine_body(scal, bands, a0, a1, a2, a3, out, small):
    nodes, lanes = bands.shape[1:]
    tile = out.shape[2] - lanes
    out[:, :, 0:lanes] = bands[...]
    for k, part in enumerate((a0, a1, a2, a3)):
        out[scal[0] ^ k, :, lanes:] = part[0:nodes, 0:tile]
        small[scal[0] ^ k] = part[nodes:]


def paired(re, im, size):
    if size == re.shape[1]:
        return jnp.concatenate([re, im], axis=1)
    fill = jnp.zeros((re.shape[0], size - re.shape[1]), re.dtype)
    return jnp.concatenate([re, fill, im, fill], axis=1)


def pack_bands_body(w, wp, scal, vec, *outs):
    for q in range(GROUP):
        bands = paired(vec[0, :, q * w : (q + 1) * w], vec[1, :, q * w : (q + 1) * w], wp)
        for k in range(GROUP):

            @pl.when((scal[0] ^ k) == q)
            def _():
                outs[k][...] = bands


def pack_panel_body(pc, pcp, scal, own, other, small, twin, next_, *outs):
    cols = pc * GROUP
    total = own[...] + other[...]
    nodes = total.shape[0]
    for q in range(GROUP):
        panel = paired(
            total[:, q * pc : (q + 1) * pc], total[:, cols + q * pc : cols + (q + 1) * pc], pcp
        ).astype(BF16)
        for k in range(GROUP):

            @pl.when((scal[0] ^ k) == q)
            def _():
                outs[k][0:nodes, :] = panel

    tile = 2 * pcp
    for k in range(GROUP):
        row = nodes
        for part in (small, twin, next_):
            for at in range(0, part.shape[1], tile):
                outs[k][row : row + SMALL, :] = part[:, at : at + tile]
                row += SMALL


def rotate_body(parts, scal, vec, rot, *out):
    nodes, bands = vec.shape[1:]
    panel = rot.shape[2]
    mine = pl.ds(pl.multiple_of(scal[3] * bands, bands), bands)
    both = jnp.concatenate([vec[0], vec[1]], axis=0)
    with_re = jnp.dot(both, rot[0, mine, :], preferred_element_type=F32)
    with_im = jnp.dot(both, rot[1, mine, :], preferred_element_type=F32)
    out_re = with_re[0:nodes] - with_im[nodes:]
    out_im = with_im[0:nodes] + with_re[nodes:]
    cols = panel // parts
    for h in range(parts):
        value_re = out_re[:, h * cols : (h + 1) * cols]
        value_im = out_im[:, h * cols : (h + 1) * cols]
        if parts == 2:

            @pl.when(scal[3] == h)
            def _():
                out[0][:, 0:cols] = value_re
                out[0][:, cols : 2 * cols] = value_im

            @pl.when(scal[3] != h)
            def _():
                out[1][:, 0:cols] = value_re
                out[1][:, cols : 2 * cols] = value_im

        else:
            out[0][h, :, 0:cols] = value_re
            out[0][h, :, cols : 2 * cols] = value_im


def described(small, p, source, width):
    tile = small.shape[2]
    count = small.shape[1] // (3 * SMALL)
    start = source * count
    parts = [small[p, (start + at) * SMALL : (start + at + 1) * SMALL] for at in range(count)]
    return jnp.concatenate(parts, axis=1)[:, 0:width].astype(F32)


def spread_line(rows, row, nodes):
    line = rows[row : row + 1, 0:nodes] + rows[row : row + 1, nodes : 2 * nodes]
    line = line + rows[row : row + 1, 2 * nodes : 3 * nodes]
    shape = (nodes, nodes)
    diag = lax.broadcasted_iota(jnp.int32, shape, 0) == lax.broadcasted_iota(jnp.int32, shape, 1)
    return jnp.where(diag, line, 0.0), diag


def add_block(t, first, thirds, nodes, e_cap, ids, coefs_s, matrix, acc, base):
    width = matrix.shape[0]
    span = 3 * nodes
    rows = thirds * nodes

    def add(count):
        place = lax.broadcasted_iota(jnp.int32, (span, width), 0).astype(F32)
        marks = [ids[t, e : e + 1, :] for e in range(count)]
        hots = [jnp.where(place == mark, 1.0, 0.0).astype(BF16) for mark in marks]
        if thirds == 3:
            used = hots
        else:
            shift = (first * nodes).astype(F32)
            used = [jnp.where(place[:rows] == mark - shift, 1.0, 0.0).astype(BF16) for mark in marks]
        half = jnp.dot(jnp.concatenate(used, axis=0), matrix[...], preferred_element_type=F32)
        half = [half[e * rows : (e + 1) * rows] * coefs_s[t, e] for e in range(count)]
        tops = [value.astype(BF16) for value in half]
        lows = [(value - part.astype(F32)).astype(BF16) for value, part in zip(half, tops)]
        full = lax.dot_general(
            jnp.concatenate(tops + lows, axis=1),
            jnp.concatenate(hots + hots, axis=1),
            (((1,), (1,)), ((), ())),
            preferred_element_type=F32,
        )
        for j in range(thirds):
            third = first + j
            i = t + third - 3 - base
            at = pl.multiple_of((2 - third) * nodes, nodes)
            acc[i, :, pl.ds(at, span)] += full[j * nodes : (j + 1) * nodes]

    live = jnp.int32(0)
    for e in range(e_cap):
        live = live + (coefs_s[t, e] != 0.0).astype(jnp.int32)
    steps = [n for n in (1, 2, 3) if n < e_cap] + [e_cap]
    for at, count in enumerate(steps):
        least = steps[at - 1] if at else 0

        @pl.when((live > least) & (live <= count))
        def _():
            add(count)


def build_body(nodes, e_cap, scal, side_s, small, matrix, *refs):
    outs = refs[0:GROUP]
    ids, coefs, coefs_s, acc, sem = refs[GROUP:]
    side = side_s[0]
    odd = scal[1] & 1
    base = side * GROUP
    coefs[...] = jnp.zeros(coefs.shape, F32)
    acc[...] = jnp.zeros(acc.shape, F32)
    sources = ((0, 1), (1, 2 - 2 * odd), (2, 2 * odd))
    for source, dz in sources:
        for p in range(GROUP):
            rows = described(small, p, source, matrix.shape[0])
            t = dz * GROUP + p
            ids[t, 0:4, :] = rows[0:4] + 128.0 * rows[4:8]
            coefs[pl.ds(t, 1), :] = (rows[8:9] + rows[9:10] + rows[10:11])[:, 0:128]
    copy = pltpu.make_async_copy(coefs, coefs_s, sem)
    copy.start()
    for source, dz in sources:
        for p in range(GROUP):
            i = dz * GROUP + p - 2 - base

            @pl.when((i >= 0) & (i < GROUP))
            def _():
                rows = described(small, p, source, matrix.shape[0])
                line, diag = spread_line(rows, 11, nodes)
                acc[i, :, 2 * nodes : 3 * nodes] = line - jnp.where(diag, FILTER_CENTER, 0.0)

    copy.wait()
    args = (nodes, e_cap, ids, coefs_s, matrix, acc, base)
    low = side == 0

    def whole(step, carry):
        add_block(GROUP - 1 + side * GROUP + step, 0, 3, *args)
        return carry

    def two(step, carry):
        outer = step == 0
        t = jnp.where(low, jnp.where(outer, 2, 5), jnp.where(outer, 9, 6))
        add_block(t, jnp.where(low == outer, 1, 0), 2, *args)
        return carry

    def one(step, carry):
        outer = step == 0
        t = jnp.where(low, jnp.where(outer, 1, 6), jnp.where(outer, 10, 5))
        add_block(t, jnp.where(low == outer, 2, 0), 1, *args)
        return carry

    lax.fori_loop(0, 2, whole, 0)
    lax.fori_loop(0, 2, two, 0)
    lax.fori_loop(0, 2, one, 0)
    for i in range(GROUP):
        value = acc[i] * (1.0 / FILTER_HALF)
        top = value.astype(BF16)
        outs[i][:, 0 : 5 * nodes] = top
        outs[i][:, 5 * nodes :] = (value - top.astype(F32)).astype(BF16)


def join_body(scal, own, twin, next_, small, vec, cols):
    nodes = own.shape[1]
    rows_out = cols.shape[0]
    odd = scal[1] & 1
    for source, (array, dz) in enumerate(((own, 1), (twin, 2 - 2 * odd), (next_, 2 * odd))):
        for p in range(GROUP):
            t = dz * GROUP + p
            vec[pl.ds(pl.multiple_of(t * nodes, nodes), nodes), :] = array[p]
            i = t - 2

            @pl.when((i >= 0) & (i < rows_out))
            def _():
                rows = described(small, p, source, 3 * nodes)
                line, _ = spread_line(rows, 12, nodes)
                column = jnp.sum(line, axis=1, keepdims=True) * (1.0 / FILTER_HALF)
                cols[i] = jnp.broadcast_to(column, cols.shape[1:])


def filter_body(at, half, scal, side_s, vec, cols, *refs):
    k_one, k_two, refs = refs[:GROUP], refs[GROUP : 2 * GROUP], refs[2 * GROUP :]
    first, keep = refs[-2:]
    outs = refs[:-2]
    rows_out = 2 * GROUP
    nodes = cols.shape[1]
    sign = jnp.where(lax.broadcasted_iota(jnp.int32, (1, 2 * half), 1) < half, 1.0, -1.0)

    def rows_at(block, count):
        return pl.ds(pl.multiple_of(block * nodes, nodes), count * nodes)

    def applied(source, lanes, start, i, rows):
        block = source[rows_at(start, 5), lanes]
        twice = jnp.concatenate([block, block], axis=0)
        total = jnp.dot(rows[...], twice, preferred_element_type=F32)
        mid = source[rows_at(start + 2, 1), lanes].astype(F32)
        return total + (cols[i][:, 0:1] * sign) * pltpu.roll(mid, half, 1)

    inside_low = scal[1] > 0
    inside_high = scal[1] < scal[2] - 1
    sides = ((k_one, side_s[0]), (k_two, 1 - side_s[0]))
    for parts, side in sides:
        for local in range(GROUP):
            i = side * GROUP + local
            value = applied(vec, slice(at, at + 2 * half), i, i, parts[local])
            kept = ((i >= 2) | inside_low) & ((i < rows_out - 2) | inside_high)
            first[rows_at(i, 1), :] = jnp.where(kept, value, 0.0).astype(BF16)
    for low in (True, False):
        for step in range(GROUP // 2):
            local = GROUP // 2 + step if low else step
            i = step if low else GROUP // 2 + step
            anchor = vec[rows_at(GROUP + i, 1), at : at + 2 * half].astype(F32)
            for parts, side in sides:

                @pl.when((side == 0) == low)
                def _():
                    keep[...] = applied(first, slice(None), i, i + 2, parts[local])

            value = 2.0 * keep[...] - anchor
            if len(outs) == 1:
                outs[0][i] = value.astype(BF16)
                continue
            outs[GROUP][:, rows_at(i, 1)] = jnp.transpose(value).astype(BF16)
            value = value.astype(BF16)
            for k in range(GROUP):

                @pl.when((scal[0] ^ k) == i)
                def _():
                    outs[k][...] = value


def collect_body(w, wp, scal, g0, g1, g2, g3, out):
    mine = scal[0]
    for k, part in enumerate((g0, g1, g2, g3)):
        re = part[:, 0:w]
        im = part[:, wp : wp + w]
        for q in range(GROUP):

            @pl.when((mine ^ k) == q)
            def _():
                out[0, :, q * w : (q + 1) * w] = re
                out[1, :, q * w : (q + 1) * w] = im


def overlap_body(w, wp, pc, pcp, parts, scale, split, scal, left, *refs):
    panels = refs[0 : GROUP * parts]
    outs = refs[GROUP * parts : -3]
    rotated, right, result = refs[-3:]
    mine, band = scal[0], scal[3]
    nodes = panels[0].shape[1]
    tile = 2 * pcp
    chunks = parts * GROUP
    panel = pc * chunks
    for g in range(parts):
        for j in range(GROUP):
            half = (band + g) % parts
            at = pl.multiple_of((half * GROUP + (mine ^ j)) * tile, tile)
            for p in range(GROUP):
                right[p * nodes : (p + 1) * nodes, pl.ds(at, tile)] = panels[g * GROUP + j][p]
    for j in range(GROUP):
        value = panels[j][mine]
        for q in range(GROUP):

            @pl.when((mine ^ j) == q)
            def _():
                rotated[0, :, q * pc : (q + 1) * pc] = value[:, 0:pc]
                rotated[1, :, q * pc : (q + 1) * pc] = value[:, pcp : pcp + pc]

    product = jnp.dot(left[...], right[...], preferred_element_type=F32) * scale
    top, bottom = product[0:w], product[wp : wp + w]
    for s in range(chunks):
        a, b = s * tile, s * tile + pcp
        result[:, s * pc : (s + 1) * pc] = top[:, a : a + pc] - bottom[:, b : b + pc]
        result[:, panel + s * pc : panel + (s + 1) * pc] = top[:, b : b + pc] + bottom[:, a : a + pc]
    if split == 1:
        outs[0][...] = result[...]
    else:
        rows = w // split
        for j in range(split):
            at = pl.multiple_of((scal[1] ^ j) * rows, rows)
            outs[j][...] = result[pl.ds(at, rows), :].astype(BF16)


def sum_body(s0, s1, s2, s3, out):
    total = s0[...].astype(F32) + s1[...].astype(F32)
    total = total + (s2[...].astype(F32) + s3[...].astype(F32))
    out[...] = total.astype(BF16)


def copy_body(given, out):
    out[...] = given[...]


def spread_body(w, rows, plan, count, panel, scal, *refs):
    out, buffer, sems = refs[-3:]
    mine, group = scal[0], scal[1]
    copies = []
    for slot, (array, at, k, j) in enumerate(plan):
        value = refs[array][at].astype(F32)
        buffer[slot, :, 0, :] = value[:, 0:panel]
        buffer[slot, :, 1, :] = value[:, panel : 2 * panel]
        start = (mine ^ k) * w + ((group ^ j) * rows if rows < w else 0)
        copy = pltpu.make_async_copy(buffer.at[slot], out.at[pl.ds(start, rows)], sems.at[slot])
        copy.start()
        copies.append(copy)
    for copy in copies:
        copy.wait()


def on_device(
    orbitals, elem_count, connectivity, elem_coef, elem_matrix, potential, absorber, rotation
):
    nodes, _, bands = orbitals.shape
    blocks = lax.axis_size("elem")
    parts = lax.axis_size("band")
    e_cap, elem_nodes = connectivity.shape[1:]
    panel = rotation.shape[2]
    groups = blocks // GROUP
    w = bands // GROUP
    span = 3 * nodes
    width = up(max(elem_nodes, span), 128)
    wp = max(up(w, 64), width // 2)
    lanes = 2 * wp
    cols = panel // parts
    pc = cols // GROUP
    pcp = up(pc, 64)
    elem = lax.axis_index("elem")
    band = lax.axis_index("band")
    scal = jnp.stack([elem % GROUP, elem // GROUP, jnp.int32(groups), band]).astype(jnp.int32)

    def struct(*shape, dtype=BF16):
        return jax.ShapeDtypeStruct(shape, dtype)

    def in_group(k):
        return [(i, i ^ k) for i in range(blocks)]

    def swap(values):
        return [values[0]] + [lax.ppermute(values[k], "elem", in_group(k)) for k in range(1, GROUP)]

    twins = [(i, i ^ GROUP) for i in range(blocks) if i ^ GROUP < blocks]
    nexts = [(i, i + GROUP) for i in range(blocks - GROUP) if i // GROUP % 2]
    nexts = nexts + [(b, a) for a, b in nexts]

    def neighbours(value):
        return lax.ppermute(value, "elem", twins), lax.ppermute(value, "elem", nexts)

    turn = [(0, 1), (1, 0)]

    values = jnp.concatenate([jnp.pad(elem_coef[0], (0, 128 - e_cap)), potential, absorber])[None]
    small = call(
        describe_body,
        struct(SMALL, width),
        [SMEM, VMEM, VMEM],
        (elem_count, connectivity[0], values),
        scratch=[pltpu.VMEM((SMALL, width), F32)],
    )
    small_near = neighbours(small)
    orbitals, small = lax.optimization_barrier((orbitals, small))
    vec = jnp.moveaxis(orbitals, 1, 0)
    messages = call(
        functools.partial(pack_bands_body, w, wp),
        [struct(nodes, lanes)] * GROUP,
        [SMEM, VMEM],
        (scal, vec),
        moved=4 * nodes * bands * 2,
    )
    messages, rotation, small_near = lax.optimization_barrier((messages, rotation, small_near))
    messages = call(
        order_body, struct(GROUP, nodes, lanes), [SMEM] + [VMEM] * GROUP, (scal, *swap(messages))
    )

    rot = jnp.moveaxis(rotation, 1, 0)
    half = struct(nodes, 2 * cols, dtype=F32)
    sums = call(
        functools.partial(rotate_body, parts),
        [half, half] if parts == 2 else [struct(parts, nodes, 2 * cols, dtype=F32)],
        [SMEM, VMEM, VMEM],
        (scal, vec, rot),
        flops=WEIGHT,
        moved=WEIGHT // 256,
    )
    if parts == 2:
        terms = (sums[0], lax.ppermute(sums[1], "band", turn))
    else:
        whole = lax.psum_scatter(sums[0], "band", scatter_dimension=0, tiled=True)[0]
        terms = (whole, jnp.zeros_like(whole))

    all_lanes = lanes + 2 * pcp
    tall = 3 * SMALL * (up(width, 2 * pcp) // (2 * pcp))
    panels = call(
        functools.partial(pack_panel_body, pc, pcp),
        [struct(nodes + tall, 2 * pcp)] * GROUP,
        [SMEM] + [VMEM] * 5,
        (scal, *terms, small, *small_near),
        moved=8 * nodes * cols,
    )
    messages, small = call(
        combine_body,
        [struct(GROUP, nodes, all_lanes), struct(GROUP, tall, 2 * pcp)],
        [SMEM] + [VMEM] * (1 + GROUP),
        (scal, messages, *swap(panels)),
    )
    near = neighbours(messages)

    matrix = jnp.pad(elem_matrix, ((0, width - elem_nodes), (0, width - elem_nodes)))
    table = (up(3 * GROUP, 8), 128)

    def operator(side):
        return call(
            functools.partial(build_body, nodes, e_cap),
            [struct(nodes, 10 * nodes)] * GROUP,
            [SMEM, SMEM, VMEM, VMEM],
            (scal, side, small, matrix),
            scratch=[
                pltpu.VMEM((3 * GROUP, 8, width), F32),
                pltpu.VMEM(table, F32),
                pltpu.SMEM(table, F32),
                pltpu.VMEM((GROUP, nodes, 5 * nodes), F32),
                pltpu.SemaphoreType.DMA,
            ],
            flops=4 * 2 * 6 * width * width * span,
            moved=8 * GROUP * nodes * 5 * nodes,
        )

    if parts == 2:
        side = band[None].astype(jnp.int32)
        halves = [operator(side)]
        halves.append([lax.ppermute(part, "band", turn) for part in halves[0]])
    else:
        side = jnp.zeros((1,), jnp.int32)
        halves = [operator(side), operator(side + 1)]

    vec, absorb = call(
        join_body,
        [struct(3 * GROUP * nodes, all_lanes), struct(2 * GROUP, nodes, 128, dtype=F32)],
        [SMEM] + [VMEM] * 4,
        (scal, messages, *near, small),
    )

    def filtered_lanes(at, size, out_shape):
        return call(
            functools.partial(filter_body, at, size // 2),
            out_shape,
            [SMEM, SMEM] + [VMEM] * (2 + 2 * GROUP),
            (scal, side, vec, absorb, *halves[0], *halves[1]),
            scratch=[pltpu.VMEM((2 * GROUP * nodes, size), BF16), pltpu.VMEM((nodes, size), F32)],
            flops=2 * 2 * 12 * nodes * 5 * nodes * size,
            moved=8 * GROUP * nodes * 5 * nodes,
        )

    out_panel = filtered_lanes(lanes, 2 * pcp, struct(GROUP, nodes, 2 * pcp))
    *fields, left = filtered_lanes(
        0, lanes, [struct(nodes, lanes)] * GROUP + [struct(lanes, GROUP * nodes)]
    )

    gathered = swap([out_panel] * GROUP)
    gathered, left, fields = lax.optimization_barrier((gathered, left, list(fields)))
    if parts == 2:
        all_panels = gathered + [lax.ppermute(x, "band", turn) for x in gathered]
    else:
        every = lax.all_gather(jnp.stack(gathered), "band", axis=0)
        every = jnp.roll(every, -band, axis=0)
        all_panels = [every[h, j] for h in range(parts) for j in range(GROUP)]

    direct = groups == 4 and w % (groups * 16) == 0
    split = groups if direct else 1
    rows = w // split
    *terms, rotated = call(
        functools.partial(
            overlap_body, w, wp, pc, pcp, parts, 1.0 / (nodes * blocks) ** 0.5, split
        ),
        [struct(rows, 2 * panel, dtype=BF16 if direct else F32)] * split + [struct(2, nodes, cols)],
        [SMEM] + [VMEM] * (1 + GROUP * parts),
        (scal, left, *all_panels),
        scratch=[
            pltpu.VMEM((GROUP * nodes, 2 * pcp * GROUP * parts), BF16),
            pltpu.VMEM((w, 2 * panel), F32),
        ],
        flops=2 * GROUP * nodes * lanes * 2 * panel,
        moved=4 * GROUP * nodes * panel,
    )
    if direct:

        def across(values):
            return [values[0]] + [
                lax.ppermute(values[j], "elem", [(i, i ^ (GROUP * j)) for i in range(blocks)])
                for j in range(1, split)
            ]

        moved = across(terms)
        moved[1], fields = lax.optimization_barrier((moved[1], fields))
        received = swap(fields)
        moved[2:], received = lax.optimization_barrier((moved[2:], received))
        own = call(sum_body, struct(rows, 2 * panel), [VMEM] * split, moved)
        stack = [own, None, lax.ppermute(own, "elem", [(i, i ^ (2 * GROUP)) for i in range(blocks)])]
        stack.append(lax.ppermute(stack[2], "elem", twins))
    else:
        received = swap(fields)
        lines = [[GROUP * z + i for z in range(groups)] for i in range(GROUP)]
        stack = [lax.psum(terms[0], "elem", axis_index_groups=lines).astype(BF16)]
    filtered = call(
        functools.partial(collect_body, w, wp),
        struct(2, nodes, bands),
        [SMEM] + [VMEM] * GROUP,
        (scal, *received),
    )
    filtered, rotated = jnp.moveaxis(filtered, 0, 1), jnp.moveaxis(rotated, 0, 1)

    def write(arrays, plan, base=None):
        more = [] if base is None else [base]
        return call(
            functools.partial(spread_body, w, rows, plan, len(arrays), panel),
            struct(bands, 2, panel, dtype=F32),
            [SMEM] + [VMEM] * len(arrays) + [ANY] * len(more),
            (scal, *arrays, *more),
            scratch=[pltpu.VMEM((len(plan), rows, 2, panel), F32), pltpu.SemaphoreType.DMA((len(plan),))],
            out_specs=ANY,
            aliases=None if base is None else {1 + len(arrays): 0},
        )

    everywhere = range(GROUP)
    mine = stack[0][None]
    if direct:
        mine = call(copy_body, struct(1, rows, 2 * panel), [VMEM], (mine,), flops=WEIGHT, moved=WEIGHT // 256)
    near_pieces = swap([mine] * GROUP)
    plan = [(k, 0, k, 0) for k in everywhere]
    if not direct:
        intersection = write(near_pieces, plan)
    else:
        far = jnp.stack(stack[2:])
        twin_pieces = jnp.concatenate(near_pieces)
        _, far, filtered, rotated = lax.optimization_barrier((twin_pieces, far, filtered, rotated))
        far_pieces = swap([far] * GROUP)
        twin_pieces = lax.ppermute(twin_pieces, "elem", twins)
        plan += [(GROUP, k, k, 1) for k in everywhere] + [(GROUP + 1, j - 2, 0, j) for j in range(2, split)]
        intersection = write([*near_pieces, twin_pieces, far], plan)
        plan = [(k - 1, j - 2, k, j) for k in range(1, GROUP) for j in range(2, split)]
        intersection = write(far_pieces[1:], plan, intersection)
    return (filtered, rotated, intersection)


def solution(mesh):
    placed = (
        P("elem", None, "band"),
        P("elem"),
        P("elem", None, None),
        P("elem", None),
        P(),
        P("elem"),
        P("elem"),
        P(),
    )
    return jax.shard_map(
        on_device,
        mesh=mesh,
        in_specs=placed,
        out_specs=(P("elem", None, "band"), P("elem", None, "band"), P("band", None, None)),
        check_vma=False,
    )
```

```python
import functools

import jax
import jax.numpy as jnp
from jax import lax
from jax.experimental import pallas as pl
from jax.experimental.pallas import tpu as pltpu
from jax.sharding import PartitionSpec as P

FILTER_CENTER = 1.0
FILTER_HALF = 4.0
GROUP = 4
BF16 = jnp.bfloat16
F32 = jnp.float32
SMALL = 16
VMEM_LIMIT = 48 * 1024 * 1024
WEIGHT = 4 * 10**9
VMEM = pl.BlockSpec(memory_space=pltpu.VMEM)
SMEM = pl.BlockSpec(memory_space=pltpu.SMEM)
ANY = pl.BlockSpec(memory_space=pl.ANY)


def up(value, step):
    return -(-value // step) * step


def call(body, out_shape, specs, arrays, scratch=(), flops=0, moved=0, out_specs=None, aliases=None):
    if out_specs is None:
        out_specs = [VMEM] * len(out_shape) if isinstance(out_shape, list) else VMEM
    return pl.pallas_call(
        body,
        out_shape=out_shape,
        in_specs=specs,
        out_specs=out_specs,
        scratch_shapes=list(scratch),
        input_output_aliases=aliases or {},
        compiler_params=pltpu.CompilerParams(vmem_limit_bytes=VMEM_LIMIT),
        cost_estimate=pl.CostEstimate(flops=flops, bytes_accessed=moved, transcendentals=0),
    )(*arrays)


def pieces(value):
    top = value.astype(BF16).astype(F32)
    rest = value - top
    middle = rest.astype(BF16).astype(F32)
    return (top, middle, rest - middle)


def describe_body(count, conn, values, out, small):
    e_cap, elem_nodes = conn.shape
    nodes = (values.shape[1] - 128) // 2
    small[...] = jnp.zeros(small.shape, F32)
    ids = conn[...]
    high = ids >> 7
    small[0:e_cap, 0:elem_nodes] = (ids - (high << 7)).astype(F32)
    small[4 : 4 + e_cap, :] = jnp.full((e_cap, small.shape[1]), 64.0, F32)
    small[4 : 4 + e_cap, 0:elem_nodes] = high.astype(F32)
    lane = lax.broadcasted_iota(jnp.int32, (1, 128), 1)
    coef = jnp.where(lane < jnp.minimum(count[0], e_cap), values[:, 0:128], 0.0)
    for at, part in enumerate(pieces(coef)):
        small[8 + at : 9 + at, 0:128] = part
    for row in (0, 1):
        for at, part in enumerate(pieces(values[:, 128 + row * nodes : 128 + (row + 1) * nodes])):
            small[11 + row : 12 + row, at * nodes : (at + 1) * nodes] = part
    out[...] = small[...].astype(BF16)


def order_body(scal, a0, a1, a2, a3, out):
    for k, part in enumerate((a0, a1, a2, a3)):
        out[scal[0] ^ k] = part[...]


def combine_body(scal, bands, a0, a1, a2, a3, out, small):
    nodes, lanes = bands.shape[1:]
    tile = out.shape[2] - lanes
    out[:, :, 0:lanes] = bands[...]
    for k, part in enumerate((a0, a1, a2, a3)):
        out[scal[0] ^ k, :, lanes:] = part[0:nodes, 0:tile]
        small[scal[0] ^ k] = part[nodes:]


def paired(re, im, size):
    if size == re.shape[1]:
        return jnp.concatenate([re, im], axis=1)
    fill = jnp.zeros((re.shape[0], size - re.shape[1]), re.dtype)
    return jnp.concatenate([re, fill, im, fill], axis=1)


def pack_bands_body(w, wp, scal, vec, *outs):
    for q in range(GROUP):
        bands = paired(vec[0, :, q * w : (q + 1) * w], vec[1, :, q * w : (q + 1) * w], wp)
        for k in range(GROUP):

            @pl.when((scal[0] ^ k) == q)
            def _():
                outs[k][...] = bands


def pack_panel_body(pc, pcp, scal, own, other, small, twin, next_, *outs):
    cols = pc * GROUP
    total = own[...] + other[...]
    nodes = total.shape[0]
    for q in range(GROUP):
        panel = paired(
            total[:, q * pc : (q + 1) * pc], total[:, cols + q * pc : cols + (q + 1) * pc], pcp
        ).astype(BF16)
        for k in range(GROUP):

            @pl.when((scal[0] ^ k) == q)
            def _():
                outs[k][0:nodes, :] = panel

    tile = 2 * pcp
    for k in range(GROUP):
        row = nodes
        for part in (small, twin, next_):
            for at in range(0, part.shape[1], tile):
                outs[k][row : row + SMALL, :] = part[:, at : at + tile]
                row += SMALL


def rotate_body(parts, scal, vec, rot, *out):
    nodes, bands = vec.shape[1:]
    panel = rot.shape[2]
    mine = pl.ds(pl.multiple_of(scal[3] * bands, bands), bands)
    both = jnp.concatenate([vec[0], vec[1]], axis=0)
    with_re = jnp.dot(both, rot[0, mine, :], preferred_element_type=F32)
    with_im = jnp.dot(both, rot[1, mine, :], preferred_element_type=F32)
    out_re = with_re[0:nodes] - with_im[nodes:]
    out_im = with_im[0:nodes] + with_re[nodes:]
    cols = panel // parts
    for h in range(parts):
        value_re = out_re[:, h * cols : (h + 1) * cols]
        value_im = out_im[:, h * cols : (h + 1) * cols]
        if parts == 2:

            @pl.when(scal[3] == h)
            def _():
                out[0][:, 0:cols] = value_re
                out[0][:, cols : 2 * cols] = value_im

            @pl.when(scal[3] != h)
            def _():
                out[1][:, 0:cols] = value_re
                out[1][:, cols : 2 * cols] = value_im

        else:
            out[0][h, :, 0:cols] = value_re
            out[0][h, :, cols : 2 * cols] = value_im


def described(small, p, source, width):
    tile = small.shape[2]
    count = small.shape[1] // (3 * SMALL)
    start = source * count
    parts = [small[p, (start + at) * SMALL : (start + at + 1) * SMALL] for at in range(count)]
    return jnp.concatenate(parts, axis=1)[:, 0:width].astype(F32)


def spread_line(rows, row, nodes):
    line = rows[row : row + 1, 0:nodes] + rows[row : row + 1, nodes : 2 * nodes]
    line = line + rows[row : row + 1, 2 * nodes : 3 * nodes]
    shape = (nodes, nodes)
    diag = lax.broadcasted_iota(jnp.int32, shape, 0) == lax.broadcasted_iota(jnp.int32, shape, 1)
    return jnp.where(diag, line, 0.0), diag


def add_block(t, first, thirds, nodes, e_cap, ids, coefs_s, matrix, acc, base):
    width = matrix.shape[0]
    span = 3 * nodes
    rows = thirds * nodes

    def add(count):
        place = lax.broadcasted_iota(jnp.int32, (span, width), 0).astype(F32)
        marks = [ids[t, e : e + 1, :] for e in range(count)]
        hots = [jnp.where(place == mark, 1.0, 0.0).astype(BF16) for mark in marks]
        if thirds == 3:
            used = hots
        else:
            shift = (first * nodes).astype(F32)
            used = [jnp.where(place[:rows] == mark - shift, 1.0, 0.0).astype(BF16) for mark in marks]
        half = jnp.dot(jnp.concatenate(used, axis=0), matrix[...], preferred_element_type=F32)
        half = [half[e * rows : (e + 1) * rows] * coefs_s[t, e] for e in range(count)]
        tops = [value.astype(BF16) for value in half]
        lows = [(value - part.astype(F32)).astype(BF16) for value, part in zip(half, tops)]
        full = lax.dot_general(
            jnp.concatenate(tops + lows, axis=1),
            jnp.concatenate(hots + hots, axis=1),
            (((1,), (1,)), ((), ())),
            preferred_element_type=F32,
        )
        for j in range(thirds):
            third = first + j
            i = t + third - 3 - base
            at = pl.multiple_of((2 - third) * nodes, nodes)
            acc[i, :, pl.ds(at, span)] += full[j * nodes : (j + 1) * nodes]

    live = jnp.int32(0)
    for e in range(e_cap):
        live = live + (coefs_s[t, e] != 0.0).astype(jnp.int32)
    steps = [n for n in ((1, 2, 3) if thirds > 1 else (2,)) if n < e_cap] + [e_cap]
    for at, count in enumerate(steps):
        least = steps[at - 1] if at else 0

        @pl.when((live > least) & (live <= count))
        def _():
            add(count)


def build_body(nodes, e_cap, scal, side_s, small, matrix, *refs):
    outs = refs[0:GROUP]
    ids, coefs, coefs_s, acc, sem = refs[GROUP:]
    side = side_s[0]
    odd = scal[1] & 1
    base = side * GROUP
    coefs[...] = jnp.zeros(coefs.shape, F32)
    acc[...] = jnp.zeros(acc.shape, F32)
    sources = ((0, 1), (1, 2 - 2 * odd), (2, 2 * odd))
    for source, dz in sources:
        for p in range(GROUP):
            rows = described(small, p, source, matrix.shape[0])
            t = dz * GROUP + p
            ids[t, 0:4, :] = rows[0:4] + 128.0 * rows[4:8]
            coefs[pl.ds(t, 1), :] = (rows[8:9] + rows[9:10] + rows[10:11])[:, 0:128]
    copy = pltpu.make_async_copy(coefs, coefs_s, sem)
    copy.start()
    for source, dz in sources:
        for p in range(GROUP):
            i = dz * GROUP + p - 2 - base

            @pl.when((i >= 0) & (i < GROUP))
            def _():
                rows = described(small, p, source, matrix.shape[0])
                line, diag = spread_line(rows, 11, nodes)
                acc[i, :, 2 * nodes : 3 * nodes] = line - jnp.where(diag, FILTER_CENTER, 0.0)

    copy.wait()
    args = (nodes, e_cap, ids, coefs_s, matrix, acc, base)
    low = side == 0

    def whole(step, carry):
        add_block(GROUP - 1 + side * GROUP + step, 0, 3, *args)
        return carry

    def two(step, carry):
        outer = step == 0
        t = jnp.where(low, jnp.where(outer, 2, 5), jnp.where(outer, 9, 6))
        add_block(t, jnp.where(low == outer, 1, 0), 2, *args)
        return carry

    def one(step, carry):
        outer = step == 0
        t = jnp.where(low, jnp.where(outer, 1, 6), jnp.where(outer, 10, 5))
        add_block(t, jnp.where(low == outer, 2, 0), 1, *args)
        return carry

    lax.fori_loop(0, 2, whole, 0)
    lax.fori_loop(0, 2, two, 0)
    lax.fori_loop(0, 2, one, 0)
    for i in range(GROUP):
        value = acc[i] * (1.0 / FILTER_HALF)
        top = value.astype(BF16)
        outs[i][:, 0 : 5 * nodes] = top
        outs[i][:, 5 * nodes :] = (value - top.astype(F32)).astype(BF16)


def join_body(scal, own, twin, next_, small, vec, cols):
    nodes = own.shape[1]
    rows_out = cols.shape[0]
    odd = scal[1] & 1
    for source, (array, dz) in enumerate(((own, 1), (twin, 2 - 2 * odd), (next_, 2 * odd))):
        for p in range(GROUP):
            t = dz * GROUP + p
            vec[pl.ds(pl.multiple_of(t * nodes, nodes), nodes), :] = array[p]
            i = t - 2

            @pl.when((i >= 0) & (i < rows_out))
            def _():
                rows = described(small, p, source, 3 * nodes)
                line, _ = spread_line(rows, 12, nodes)
                column = jnp.sum(line, axis=1, keepdims=True) * (1.0 / FILTER_HALF)
                cols[i] = jnp.broadcast_to(column, cols.shape[1:])


def filter_body(at, half, scal, side_s, vec, cols, *refs):
    k_one, k_two, refs = refs[:GROUP], refs[GROUP : 2 * GROUP], refs[2 * GROUP :]
    first, keep = refs[-2:]
    outs = refs[:-2]
    rows_out = 2 * GROUP
    nodes = cols.shape[1]
    sign = jnp.where(lax.broadcasted_iota(jnp.int32, (1, 2 * half), 1) < half, 1.0, -1.0)

    def rows_at(block, count):
        return pl.ds(pl.multiple_of(block * nodes, nodes), count * nodes)

    def applied(source, lanes, start, i, rows):
        block = source[rows_at(start, 5), lanes]
        twice = jnp.concatenate([block, block], axis=0)
        total = jnp.dot(rows[...], twice, preferred_element_type=F32)
        mid = source[rows_at(start + 2, 1), lanes].astype(F32)
        return total + (cols[i][:, 0:1] * sign) * pltpu.roll(mid, half, 1)

    inside_low = scal[1] > 0
    inside_high = scal[1] < scal[2] - 1
    sides = ((k_one, side_s[0]), (k_two, 1 - side_s[0]))
    for parts, side in sides:
        for local in range(GROUP):
            i = side * GROUP + local
            value = applied(vec, slice(at, at + 2 * half), i, i, parts[local])
            kept = ((i >= 2) | inside_low) & ((i < rows_out - 2) | inside_high)
            first[rows_at(i, 1), :] = jnp.where(kept, value, 0.0).astype(BF16)
    for low in (True, False):
        for step in range(GROUP // 2):
            local = GROUP // 2 + step if low else step
            i = step if low else GROUP // 2 + step
            anchor = vec[rows_at(GROUP + i, 1), at : at + 2 * half].astype(F32)
            for parts, side in sides:

                @pl.when((side == 0) == low)
                def _():
                    keep[...] = applied(first, slice(None), i, i + 2, parts[local])

            value = 2.0 * keep[...] - anchor
            if len(outs) == 1:
                outs[0][i] = value.astype(BF16)
                continue
            outs[GROUP][:, rows_at(i, 1)] = jnp.transpose(value).astype(BF16)
            value = value.astype(BF16)
            for k in range(GROUP):

                @pl.when((scal[0] ^ k) == i)
                def _():
                    outs[k][...] = value


def collect_body(w, wp, scal, g0, g1, g2, g3, out):
    mine = scal[0]
    for k, part in enumerate((g0, g1, g2, g3)):
        re = part[:, 0:w]
        im = part[:, wp : wp + w]
        for q in range(GROUP):

            @pl.when((mine ^ k) == q)
            def _():
                out[0, :, q * w : (q + 1) * w] = re
                out[1, :, q * w : (q + 1) * w] = im


def overlap_body(w, wp, pc, pcp, parts, scale, split, scal, left, *refs):
    panels = refs[0 : GROUP * parts]
    outs = refs[GROUP * parts : -3]
    rotated, right, result = refs[-3:]
    mine, band = scal[0], scal[3]
    nodes = panels[0].shape[1]
    tile = 2 * pcp
    chunks = parts * GROUP
    panel = pc * chunks
    for g in range(parts):
        for j in range(GROUP):
            half = (band + g) % parts
            at = pl.multiple_of((half * GROUP + (mine ^ j)) * tile, tile)
            for p in range(GROUP):
                right[p * nodes : (p + 1) * nodes, pl.ds(at, tile)] = panels[g * GROUP + j][p]
    for j in range(GROUP):
        value = panels[j][mine]
        for q in range(GROUP):

            @pl.when((mine ^ j) == q)
            def _():
                rotated[0, :, q * pc : (q + 1) * pc] = value[:, 0:pc]
                rotated[1, :, q * pc : (q + 1) * pc] = value[:, pcp : pcp + pc]

    product = jnp.dot(left[...], right[...], preferred_element_type=F32) * scale
    top, bottom = product[0:w], product[wp : wp + w]
    for s in range(chunks):
        a, b = s * tile, s * tile + pcp
        result[:, s * pc : (s + 1) * pc] = top[:, a : a + pc] - bottom[:, b : b + pc]
        result[:, panel + s * pc : panel + (s + 1) * pc] = top[:, b : b + pc] + bottom[:, a : a + pc]
    if split == 1:
        outs[0][...] = result[...]
    else:
        rows = w // split
        for j in range(split):
            at = pl.multiple_of((scal[1] ^ j) * rows, rows)
            outs[j][...] = result[pl.ds(at, rows), :].astype(BF16)


def sum_body(s0, s1, s2, s3, out):
    total = s0[...].astype(F32) + s1[...].astype(F32)
    total = total + (s2[...].astype(F32) + s3[...].astype(F32))
    out[...] = total.astype(BF16)


def copy_body(given, out):
    out[...] = given[...]


def spread_body(w, rows, plan, count, panel, scal, *refs):
    out, buffer, sems = refs[-3:]
    mine, group = scal[0], scal[1]
    copies = []
    for slot, (array, at, k, j) in enumerate(plan):
        value = refs[array][at].astype(F32)
        buffer[slot, :, 0, :] = value[:, 0:panel]
        buffer[slot, :, 1, :] = value[:, panel : 2 * panel]
        start = (mine ^ k) * w + ((group ^ j) * rows if rows < w else 0)
        copy = pltpu.make_async_copy(buffer.at[slot], out.at[pl.ds(start, rows)], sems.at[slot])
        copy.start()
        copies.append(copy)
    for copy in copies:
        copy.wait()


def on_device(
    orbitals, elem_count, connectivity, elem_coef, elem_matrix, potential, absorber, rotation
):
    nodes, _, bands = orbitals.shape
    blocks = lax.axis_size("elem")
    parts = lax.axis_size("band")
    e_cap, elem_nodes = connectivity.shape[1:]
    panel = rotation.shape[2]
    groups = blocks // GROUP
    w = bands // GROUP
    span = 3 * nodes
    width = up(max(elem_nodes, span), 128)
    wp = max(up(w, 64), width // 2)
    lanes = 2 * wp
    cols = panel // parts
    pc = cols // GROUP
    pcp = up(pc, 64)
    elem = lax.axis_index("elem")
    band = lax.axis_index("band")
    scal = jnp.stack([elem % GROUP, elem // GROUP, jnp.int32(groups), band]).astype(jnp.int32)

    def struct(*shape, dtype=BF16):
        return jax.ShapeDtypeStruct(shape, dtype)

    def in_group(k):
        return [(i, i ^ k) for i in range(blocks)]

    def swap(values):
        return [values[0]] + [lax.ppermute(values[k], "elem", in_group(k)) for k in range(1, GROUP)]

    twins = [(i, i ^ GROUP) for i in range(blocks) if i ^ GROUP < blocks]
    nexts = [(i, i + GROUP) for i in range(blocks - GROUP) if i // GROUP % 2]
    nexts = nexts + [(b, a) for a, b in nexts]

    def neighbours(value):
        return lax.ppermute(value, "elem", twins), lax.ppermute(value, "elem", nexts)

    turn = [(0, 1), (1, 0)]

    values = jnp.concatenate([jnp.pad(elem_coef[0], (0, 128 - e_cap)), potential, absorber])[None]
    small = call(
        describe_body,
        struct(SMALL, width),
        [SMEM, VMEM, VMEM],
        (elem_count, connectivity[0], values),
        scratch=[pltpu.VMEM((SMALL, width), F32)],
    )
    small_near = neighbours(small)
    orbitals, small = lax.optimization_barrier((orbitals, small))
    vec = jnp.moveaxis(orbitals, 1, 0)
    messages = call(
        functools.partial(pack_bands_body, w, wp),
        [struct(nodes, lanes)] * GROUP,
        [SMEM, VMEM],
        (scal, vec),
        moved=4 * nodes * bands * 2,
    )
    messages, rotation, small_near = lax.optimization_barrier((messages, rotation, small_near))
    messages = call(
        order_body, struct(GROUP, nodes, lanes), [SMEM] + [VMEM] * GROUP, (scal, *swap(messages))
    )

    rot = jnp.moveaxis(rotation, 1, 0)
    half = struct(nodes, 2 * cols, dtype=F32)
    sums = call(
        functools.partial(rotate_body, parts),
        [half, half] if parts == 2 else [struct(parts, nodes, 2 * cols, dtype=F32)],
        [SMEM, VMEM, VMEM],
        (scal, vec, rot),
        flops=WEIGHT,
        moved=WEIGHT // 256,
    )
    if parts == 2:
        terms = (sums[0], lax.ppermute(sums[1], "band", turn))
    else:
        whole = lax.psum_scatter(sums[0], "band", scatter_dimension=0, tiled=True)[0]
        terms = (whole, jnp.zeros_like(whole))

    all_lanes = lanes + 2 * pcp
    tall = 3 * SMALL * (up(width, 2 * pcp) // (2 * pcp))
    panels = call(
        functools.partial(pack_panel_body, pc, pcp),
        [struct(nodes + tall, 2 * pcp)] * GROUP,
        [SMEM] + [VMEM] * 5,
        (scal, *terms, small, *small_near),
        moved=8 * nodes * cols,
    )
    messages, small = call(
        combine_body,
        [struct(GROUP, nodes, all_lanes), struct(GROUP, tall, 2 * pcp)],
        [SMEM] + [VMEM] * (1 + GROUP),
        (scal, messages, *swap(panels)),
    )
    near = neighbours(messages)

    matrix = jnp.pad(elem_matrix, ((0, width - elem_nodes), (0, width - elem_nodes)))
    table = (up(3 * GROUP, 8), 128)

    def operator(side):
        return call(
            functools.partial(build_body, nodes, e_cap),
            [struct(nodes, 10 * nodes)] * GROUP,
            [SMEM, SMEM, VMEM, VMEM],
            (scal, side, small, matrix),
            scratch=[
                pltpu.VMEM((3 * GROUP, 8, width), F32),
                pltpu.VMEM(table, F32),
                pltpu.SMEM(table, F32),
                pltpu.VMEM((GROUP, nodes, 5 * nodes), F32),
                pltpu.SemaphoreType.DMA,
            ],
            flops=4 * 2 * 6 * width * width * span,
            moved=8 * GROUP * nodes * 5 * nodes,
        )

    if parts == 2:
        side = band[None].astype(jnp.int32)
        halves = [operator(side)]
        halves.append([lax.ppermute(part, "band", turn) for part in halves[0]])
    else:
        side = jnp.zeros((1,), jnp.int32)
        halves = [operator(side), operator(side + 1)]

    vec, absorb = call(
        join_body,
        [struct(3 * GROUP * nodes, all_lanes), struct(2 * GROUP, nodes, 128, dtype=F32)],
        [SMEM] + [VMEM] * 4,
        (scal, messages, *near, small),
    )

    def filtered_lanes(at, size, out_shape):
        return call(
            functools.partial(filter_body, at, size // 2),
            out_shape,
            [SMEM, SMEM] + [VMEM] * (2 + 2 * GROUP),
            (scal, side, vec, absorb, *halves[0], *halves[1]),
            scratch=[pltpu.VMEM((2 * GROUP * nodes, size), BF16), pltpu.VMEM((nodes, size), F32)],
            flops=2 * 2 * 12 * nodes * 5 * nodes * size,
            moved=8 * GROUP * nodes * 5 * nodes,
        )

    out_panel = filtered_lanes(lanes, 2 * pcp, struct(GROUP, nodes, 2 * pcp))
    *fields, left = filtered_lanes(
        0, lanes, [struct(nodes, lanes)] * GROUP + [struct(lanes, GROUP * nodes)]
    )

    gathered = swap([out_panel] * GROUP)
    gathered, left, fields = lax.optimization_barrier((gathered, left, list(fields)))
    if parts == 2:
        all_panels = gathered + [lax.ppermute(x, "band", turn) for x in gathered]
    else:
        every = lax.all_gather(jnp.stack(gathered), "band", axis=0)
        every = jnp.roll(every, -band, axis=0)
        all_panels = [every[h, j] for h in range(parts) for j in range(GROUP)]

    direct = groups == 4 and w % (groups * 16) == 0
    split = groups if direct else 1
    rows = w // split
    *terms, rotated = call(
        functools.partial(
            overlap_body, w, wp, pc, pcp, parts, 1.0 / (nodes * blocks) ** 0.5, split
        ),
        [struct(rows, 2 * panel, dtype=BF16 if direct else F32)] * split + [struct(2, nodes, cols)],
        [SMEM] + [VMEM] * (1 + GROUP * parts),
        (scal, left, *all_panels),
        scratch=[
            pltpu.VMEM((GROUP * nodes, 2 * pcp * GROUP * parts), BF16),
            pltpu.VMEM((w, 2 * panel), F32),
        ],
        flops=2 * GROUP * nodes * lanes * 2 * panel,
        moved=4 * GROUP * nodes * panel,
    )
    if direct:

        def across(values):
            return [values[0]] + [
                lax.ppermute(values[j], "elem", [(i, i ^ (GROUP * j)) for i in range(blocks)])
                for j in range(1, split)
            ]

        moved = across(terms)
        moved[1], fields = lax.optimization_barrier((moved[1], fields))
        received = swap(fields)
        moved[2:], received = lax.optimization_barrier((moved[2:], received))
        own = call(sum_body, struct(rows, 2 * panel), [VMEM] * split, moved)
        stack = [own, None, lax.ppermute(own, "elem", [(i, i ^ (2 * GROUP)) for i in range(blocks)])]
        stack.append(lax.ppermute(stack[2], "elem", twins))
    else:
        received = swap(fields)
        lines = [[GROUP * z + i for z in range(groups)] for i in range(GROUP)]
        stack = [lax.psum(terms[0], "elem", axis_index_groups=lines).astype(BF16)]
    filtered = call(
        functools.partial(collect_body, w, wp),
        struct(2, nodes, bands),
        [SMEM] + [VMEM] * GROUP,
        (scal, *received),
    )
    filtered, rotated = jnp.moveaxis(filtered, 0, 1), jnp.moveaxis(rotated, 0, 1)

    def write(arrays, plan, base=None):
        more = [] if base is None else [base]
        return call(
            functools.partial(spread_body, w, rows, plan, len(arrays), panel),
            struct(bands, 2, panel, dtype=F32),
            [SMEM] + [VMEM] * len(arrays) + [ANY] * len(more),
            (scal, *arrays, *more),
            scratch=[pltpu.VMEM((len(plan), rows, 2, panel), F32), pltpu.SemaphoreType.DMA((len(plan),))],
            out_specs=ANY,
            aliases=None if base is None else {1 + len(arrays): 0},
        )

    everywhere = range(GROUP)
    mine = stack[0][None]
    if direct:
        mine = call(copy_body, struct(1, rows, 2 * panel), [VMEM], (mine,), flops=WEIGHT, moved=WEIGHT // 256)
    near_pieces = swap([mine] * GROUP)
    plan = [(k, 0, k, 0) for k in everywhere]
    if not direct:
        intersection = write(near_pieces, plan)
    else:
        far = jnp.stack(stack[2:])
        twin_pieces = jnp.concatenate(near_pieces)
        _, far, filtered, rotated = lax.optimization_barrier((twin_pieces, far, filtered, rotated))
        far_pieces = swap([far] * GROUP)
        twin_pieces = lax.ppermute(twin_pieces, "elem", twins)
        plan += [(GROUP, k, k, 1) for k in everywhere] + [(GROUP + 1, j - 2, 0, j) for j in range(2, split)]
        intersection = write([*near_pieces, twin_pieces, far], plan)
        plan = [(k - 1, j - 2, k, j) for k in range(1, GROUP) for j in range(2, split)]
        intersection = write(far_pieces[1:], plan, intersection)
    return (filtered, rotated, intersection)


def solution(mesh):
    placed = (
        P("elem", None, "band"),
        P("elem"),
        P("elem", None, None),
        P("elem", None),
        P(),
        P("elem"),
        P("elem"),
        P(),
    )
    return jax.shard_map(
        on_device,
        mesh=mesh,
        in_specs=placed,
        out_specs=(P("elem", None, "band"), P("elem", None, "band"), P("band", None, None)),
        check_vma=False,
    )
```
